128 devices in a mesh: dp: 64 (over z_hi, y, x, core), tensor: 2 (over z_lo).
Axes of the slice: x: 4, y: 4, z: 4 (z_hi: 2, z_lo: 2; z = z_hi * 2 + z_lo), core: 2. Of those that a mesh axis runs over, the one named last changes fastest.
Arguments:
- tokens: bfloat16 [32768, 1024], P('dp'), may hold values from -16 to 16
- gain_one: float32 [1024], replicated, may hold values from 0.5 to 1.5
- shift_one: float32 [1024], replicated, may hold values from -1.25 to 1.25
- qkv_weight: bfloat16 [1024, 3, 1024], P(None, None, 'tensor'), may hold values from -0.1875 to 0.1875
- qv_bias: bfloat16 [2, 1024], P(None, 'tensor'), may hold values from -1.75 to 1.75
- out_weight: bfloat16 [1024, 1024], P('tensor'), may hold values from -0.375 to 0.375
- out_bias: bfloat16 [1024], replicated, may hold values from -1.75 to 1.75
- gain_two: float32 [1024], replicated, may hold values from 0.5 to 1.5
- shift_two: float32 [1024], replicated, may hold values from -1.25 to 1.25
- up_weight: bfloat16 [1024, 4096], P(None, 'tensor'), may hold values from -0.1875 to 0.1875
- up_bias: bfloat16 [4096], P('tensor'), may hold values from -1.75 to 1.75
- down_weight: bfloat16 [4096, 1024], P('tensor'), may hold values from -0.09375 to 0.09375
- down_bias: bfloat16 [1024], replicated, may hold values from -1.75 to 1.75
- cotangent: bfloat16 [32768, 1024], P('dp'), may hold values from -16 to 16
Outputs:
- block_out: bfloat16 [32768, 1024], P('dp')
- token_grad: float32 [32768, 1024], P('dp')
- grad_gain_one: float32 [1024], P('dp')
- grad_shift_one: float32 [1024], P('dp')
- grad_qkv_weight: float32 [1024, 3, 1024], P('dp', None, 'tensor')
- grad_qv_bias: float32 [2, 1024], P(None, 'tensor')
- grad_out_weight: float32 [1024, 1024], P('tensor', 'dp')
- grad_out_bias: float32 [1024], P('dp')
- grad_gain_two: float32 [1024], P('dp')
- grad_shift_two: float32 [1024], P('dp')
- grad_up_weight: float32 [1024, 4096], P('dp', 'tensor')
- grad_up_bias: float32 [4096], P('tensor')
- grad_down_weight: float32 [4096, 1024], P('tensor', 'dp')
- grad_down_bias: float32 [1024], P('dp')
The draws below stay inside these ranges and needn't reach their ends.
All inputs are finite; a program needn't handle non-finite values.
Results may differ from the reference program's by a relative error of at most 0.01.
Values sent between devices are 32-bit elements; how exact they have to be, the bound alone decides.
A program may use at most 256 MiB of HBM per device.

```python
import math
import jax
import jax.numpy as jnp
from jax import lax

D = 1024
H = 16
DH = 64
FF = 4096
SEQ_LEN = 512
TOKENS = 32768
N_DP = 64


def raised(entries, rng, source, target, blocks, factor):
    def block_of(dim):
        return (jnp.arange(entries.shape[dim]) // (entries.shape[dim] // blocks)).reshape((-1,) + (1,) * (entries.ndim - 1 - dim))

    near = jax.random.permutation(rng, blocks)[block_of(target)]
    far = (block_of(target) + blocks // 2) % blocks
    return jnp.where((block_of(source) == near) | (block_of(source) == far), factor * entries, entries)


def block_levels(key, shape, cuts, least, high):
    level, own = 1.0, jax.random.fold_in(key, 6)
    for position, shards_of in cuts:
        steps = jnp.exp(jax.random.uniform(jax.random.fold_in(own, position), (shards_of,), jnp.float32, least / len(cuts), high / len(cuts)))
        level = level * jnp.repeat(steps, shape[position] // shards_of).reshape([-1 if axis == position else 1 for axis in range(len(shape))])
    return level


def normal_values(rng, shape, width, reach, cuts=(), kind=jnp.bfloat16):
    values = jax.random.normal(rng, shape, jnp.float32) * width
    if len(cuts) > 0:
        values = block_levels(rng, shape, cuts, -0.22, 0.18) * values
    return jnp.clip(values, min=-reach, max=reach).astype(kind)


def gaussian_with(rng, shape, width, most, shards, heavy, held_as=jnp.bfloat16):
    result = width * jax.random.normal(rng, shape, jnp.float32)
    if shards:
        result = result * block_levels(rng, shape, shards, -0.22, 0.18)
    return jnp.clip(raised(result, jax.random.fold_in(rng, 3), *heavy), -most, most).astype(held_as)


def setup_inputs(seed: int = 0) -> dict:
    key_list = jax.random.split(jax.random.key(seed), 15)
    tokens = gaussian_with(key_list[0], (TOKENS, D), 1.0, 16.0, ((0, 64),), (0, 1, 64, 4.0))
    gain_one = jnp.clip(1.0 + 0.1 * jax.random.normal(key_list[1], (D,), jnp.float32), 0.5, 1.5)
    shift_one = normal_values(key_list[2], (D,), 0.2, 1.25, (), jnp.float32)
    qkv_weight = normal_values(key_list[3], (D, 3, D), D ** -0.5, 0.1875, ((2, 2),))
    qv_bias = normal_values(key_list[4], (2, D), 0.3, 1.75, ((1, 2),))
    out_weight = normal_values(key_list[5], (D, D), (D // 4) ** -0.5, 0.375, ((0, 2),))
    out_bias = normal_values(key_list[6], (D,), 0.3, 1.75)
    gain_two = jnp.clip(1.0 + 0.1 * jax.random.normal(key_list[7], (D,), jnp.float32), 0.5, 1.5)
    shift_two = normal_values(key_list[8], (D,), 0.2, 1.25, (), jnp.float32)
    up_weight = normal_values(key_list[9], (D, FF), D ** -0.5, 0.1875, ((1, 2),))
    up_bias = normal_values(key_list[10], (FF,), 0.3, 1.75, ((0, 2),))
    down_weight = normal_values(key_list[11], (FF, D), FF ** -0.5, 0.09375, ((0, 2),))
    down_bias = normal_values(key_list[12], (D,), 0.3, 1.75)
    cotangent = gaussian_with(key_list[13], (TOKENS, D), 1.0, 16.0, ((0, 64),), (0, 1, 64, 4.0))
    return dict(tokens=tokens, gain_one=gain_one, shift_one=shift_one, qkv_weight=qkv_weight, qv_bias=qv_bias, out_weight=out_weight, out_bias=out_bias, gain_two=gain_two, shift_two=shift_two, up_weight=up_weight, up_bias=up_bias, down_weight=down_weight, down_bias=down_bias, cotangent=cotangent)


@jax.custom_vjp
def low(v):
    return lax.optimization_barrier(v.astype(jnp.bfloat16)).astype(jnp.float32)

@jax.custom_vjp
def low_back(v):
    return v

def low_keep(v):
    return (low(v), None)

def low_pass(kept, grad):
    return (grad,)

def back_keep(v):
    return (v, None)

def back_low(kept, grad):
    return (low(grad),)
low.defvjp(low_keep, low_pass)
low_back.defvjp(back_keep, back_low)
epsilon = 1e-05
highest = lax.Precision.HIGHEST

def layer_norm(values, gain, shift):
    centre = lax.optimization_barrier(jnp.mean(values, axis=-1, keepdims=True))
    centered = values - centre
    spread = lax.optimization_barrier(jnp.mean(centered * centered, axis=-1, keepdims=True))
    return centered * lax.rsqrt(spread + epsilon) * gain + shift

def gelu_tanh(values):
    inner_arg = 0.7978845608028654 * (values + 0.044715 * values * values * values)
    return 0.5 * values * (1.0 + jnp.tanh(inner_arg))

def block_forward(inputs, gain_one, shift_one, qkv_weight, qv_bias, out_weight, out_bias, gain_two, shift_two, up_weight, up_bias, down_weight, down_bias):
    length = inputs.shape[0]
    score_scale = 1.0 / math.sqrt(DH)
    normed_one = low(layer_norm(inputs, gain_one, shift_one))
    projected = jnp.einsum('td,dcf->tcf', normed_one, qkv_weight, precision=highest)
    queries = low(low_back(projected[:, 0] + qv_bias[0])).reshape(length, H, DH)
    key_rows = low(low_back(projected[:, 1])).reshape(length, H, DH)
    values = low(low_back(projected[:, 2] + qv_bias[1])).reshape(length, H, DH)
    slopes = jnp.exp2(-8.0 * (jnp.arange(H, dtype=jnp.int32) + 1).astype(jnp.float32) / H)
    positions = jnp.arange(length, dtype=jnp.int32)
    distance = (positions[:, None] - positions[None, :]).astype(jnp.float32)
    scores = jnp.einsum('qhd,khd->hqk', queries, key_rows, precision=highest) * score_scale
    scores = low_back(scores - slopes[:, None, None] * distance)
    scores = jnp.where(distance >= 0.0, scores, -1000000000.0)
    attention = low(jax.nn.softmax(scores, axis=-1))
    attended = jnp.einsum('hqk,khd->qhd', attention, values, precision=highest).reshape(length, D)
    attended = low_back(low(attended))
    branch = low_back(jnp.dot(attended, out_weight, precision=highest) + out_bias)
    middle = inputs + branch
    normed_two = low(layer_norm(middle, gain_two, shift_two))
    hidden = low_back(jnp.dot(normed_two, up_weight, precision=highest) + up_bias)
    active = low(gelu_tanh(hidden))
    feed_out = low_back(jnp.dot(active, down_weight, precision=highest) + down_bias)
    return middle + feed_out

def reference(tokens, gain_one, shift_one, qkv_weight, qv_bias, out_weight, out_bias, gain_two, shift_two, up_weight, up_bias, down_weight, down_bias, cotangent):
    weights_all = tuple((item.astype(jnp.float32) for item in (gain_one, shift_one, qkv_weight, qv_bias, out_weight, out_bias, gain_two, shift_two, up_weight, up_bias, down_weight, down_bias)))
    group_size = math.gcd(N_DP, max(1, 4096 // SEQ_LEN))
    token_rows = tokens.astype(jnp.float32).reshape(N_DP // group_size, group_size, SEQ_LEN, D)
    cot_rows = cotangent.astype(jnp.float32).reshape(N_DP // group_size, group_size, SEQ_LEN, D)

    def one_group(totals, group_pair):
        seq_block, cot_block = group_pair

        def forward(block_in, weight_in):
            return jax.vmap(lambda single: block_forward(single, *weight_in))(block_in)
        outputs, pullback = jax.vjp(forward, seq_block, weights_all)
        grad_block, grad_weights = pullback(cot_block)
        totals = jax.tree.map(lambda left, right: left + right, totals, grad_weights)
        return (totals, (outputs, grad_block))
    zero_grads = jax.tree.map(jnp.zeros_like, weights_all)
    totals, (outputs, grad_rows) = lax.scan(one_group, zero_grads, (token_rows, cot_rows))
    block_out = outputs.reshape(TOKENS, D).astype(jnp.bfloat16)
    token_grad = grad_rows.reshape(TOKENS, D)
    return (block_out, token_grad, totals[0], totals[1], totals[2], totals[3], totals[4], totals[5], totals[6], totals[7], totals[8], totals[9], totals[10], totals[11])
```

```python
import functools
import math

import jax
import jax.numpy as jnp
from jax import lax
from jax.experimental import pallas as pl
from jax.experimental.pallas import tpu as pltpu
from jax.sharding import PartitionSpec as P

DH = 64
BOTH = ("dp", "tensor")
epsilon = 1e-05
bf16 = jnp.bfloat16
f32 = jnp.float32


def place_of(dp, t):
    return (dp // 2) % 4, (dp // 8) % 4, (dp // 32) * 2 + t, dp % 2


def index_of(x, y, z, core):
    return ((((z // 2) * 4 + y % 4) * 4 + x % 4) * 2 + core) * 2 + z % 2


def permuted(move):
    pairs = []
    for dp in range(64):
        for t in range(2):
            x, y, z, core = place_of(dp, t)
            pairs.append((dp * 2 + t, index_of(*move(x, y, z, core))))
    return pairs


def along_z(step):
    return permuted(lambda x, y, z, core: (x, y, (z + step) % 4, core))


def along_ring(step):
    return permuted(
        lambda x, y, z, core: (x + step, y, z, core) if core == 0 else (x, y + step, z, core)
    )


def to_core():
    return permuted(lambda x, y, z, core: (x, y, z, 1 - core))


def send(array, perm):
    return lax.ppermute(array, BOTH, perm)


def gather_other(piece):
    half = piece.shape[0] // 2
    low = send(piece[:half], along_z(1))
    high = send(piece[half:], along_z(-1))
    mine = lax.optimization_barrier(jnp.concatenate([low, high], axis=0))
    before = send(mine, along_ring(1))
    after = send(mine, along_ring(-1))
    mid = mine.shape[1] // 2
    far_low = send(before[:, :mid], along_ring(1))
    far_high = send(after[:, mid:], along_ring(-1))
    far = lax.optimization_barrier(jnp.concatenate([far_low, far_high], axis=1))
    own = [mine, before, after, far]
    return [lax.optimization_barrier(p) for p in own + [send(p, to_core()) for p in own]]


def layer_norm_parts(values):
    centre = jnp.mean(values, axis=-1, keepdims=True)
    centered = values - centre
    spread = jnp.mean(centered * centered, axis=-1, keepdims=True)
    r = lax.rsqrt(spread + epsilon)
    return centered * r, r


def layer_norm_back(grad, n, r, gain):
    e = grad * gain
    mean_e = jnp.mean(e, axis=-1, keepdims=True)
    mean_en = jnp.mean(e * n, axis=-1, keepdims=True)
    return (
        r * (e - mean_e - n * mean_en),
        jnp.sum(grad * n, axis=0),
        jnp.sum(grad, axis=0),
    )


GC, GA = 0.7978845608028654, 0.044715


def gelu_both(v):
    t = jnp.tanh(GC * (v + GA * v * v * v))
    value = 0.5 * v * (1.0 + t)
    slope = 0.5 * (1.0 + t) + 0.5 * v * (1.0 - t * t) * GC * (1.0 + 3.0 * GA * v * v)
    return value, slope


NT = (((1,), (1,)), ((), ()))
TN = (((0,), (0,)), ((), ()))
NN = (((1,), (0,)), ((), ()))


def dot(a, b, dims=NN):
    return lax.dot_general(a, b, dims, preferred_element_type=f32)


def half_lanes(block, side):
    lane = lax.broadcasted_iota(jnp.int32, block.shape, 1)
    return jnp.where((lane >= 64) == (side == 1), block, jnp.zeros_like(block))


def pair_scores(q, k, side, slope):
    s = dot(half_lanes(q, side), k, NT) * 0.125
    row = lax.broadcasted_iota(jnp.int32, s.shape, 0)
    col = lax.broadcasted_iota(jnp.int32, s.shape, 1)
    distance = (row - col).astype(f32)
    return jnp.where(row >= col, s - slope * distance, -1000000000.0)


def attend_kernel(slopes, q_ref, k_ref, v_ref, o_ref, lse_ref):
    pair = pl.program_id(0)
    q, k, v = q_ref[...], k_ref[...], v_ref[...]
    outs, lses = [], []
    for side in range(2):
        s = pair_scores(q, k, side, slopes[2 * pair + side])
        top = jnp.max(s, axis=-1, keepdims=True)
        e = jnp.exp(s - top)
        total = jnp.sum(e, axis=-1, keepdims=True)
        a = (e * (1.0 / total)).astype(bf16)
        outs.append(dot(a, v))
        lses.append(top + jnp.log(total))
    lane = lax.broadcasted_iota(jnp.int32, outs[0].shape, 1)
    o_ref[...] = jnp.where(lane < 64, outs[0], outs[1]).astype(bf16)
    lse_ref[...] = jnp.where(lane < 64, lses[0], lses[1])


def attend_back_kernel(slopes, q_ref, k_ref, v_ref, lse_ref, g_ref, dq_ref, dk_ref, dv_ref):
    pair = pl.program_id(0)
    q, k, v, g = q_ref[...], k_ref[...], v_ref[...], g_ref[...]
    lse = lse_ref[...]
    dqs, dks, dvs = [], [], []
    for side in range(2):
        s = pair_scores(q, k, side, slopes[2 * pair + side])
        a = jnp.exp(s - lse[:, 64 * side : 64 * side + 1])
        w = dot(half_lanes(g, side), v, NT)
        inner = jnp.sum(a * w, axis=-1, keepdims=True)
        ds = (a * (w - inner)).astype(bf16)
        dvs.append(dot(a.astype(bf16), g, TN))
        dqs.append(dot(ds, k) * 0.125)
        dks.append(dot(ds, q, TN) * 0.125)
    lane = lax.broadcasted_iota(jnp.int32, dqs[0].shape, 1)
    for ref, parts in ((dq_ref, dqs), (dk_ref, dks), (dv_ref, dvs)):
        ref[...] = jnp.where(lane < 64, parts[0], parts[1]).astype(bf16)


def attend(slopes, q, k, v):
    length, width = q.shape
    pairs = width // 128
    block = pl.BlockSpec((length, 128), lambda i, *_: (0, i))
    return pl.pallas_call(
        attend_kernel,
        grid_spec=pltpu.PrefetchScalarGridSpec(
            num_scalar_prefetch=1, grid=(pairs,), in_specs=[block] * 3, out_specs=[block] * 2
        ),
        out_shape=[
            jax.ShapeDtypeStruct((length, width), bf16),
            jax.ShapeDtypeStruct((length, width), f32),
        ],
        cost_estimate=pl.CostEstimate(
            flops=pairs * 8 * length * length * 128,
            bytes_accessed=length * width * 12,
            transcendentals=pairs * 2 * length * length,
        ),
        compiler_params=pltpu.CompilerParams(vmem_limit_bytes=32 * 2**20),
    )(slopes, q, k, v)


def attend_back(slopes, q, k, v, lse, g):
    length, width = q.shape
    pairs = width // 128
    block = pl.BlockSpec((length, 128), lambda i, *_: (0, i))
    return pl.pallas_call(
        attend_back_kernel,
        grid_spec=pltpu.PrefetchScalarGridSpec(
            num_scalar_prefetch=1, grid=(pairs,), in_specs=[block] * 5, out_specs=[block] * 3
        ),
        out_shape=[jax.ShapeDtypeStruct((length, width), bf16)] * 3,
        cost_estimate=pl.CostEstimate(
            flops=pairs * 20 * length * length * 128,
            bytes_accessed=length * width * 18,
            transcendentals=pairs * 2 * length * length,
        ),
        compiler_params=pltpu.CompilerParams(vmem_limit_bytes=32 * 2**20),
    )(slopes, q, k, v, lse, g)


W = 256
OFFSETS = (0, 2, 4, 6, 8, 10, 12)
MESH = pl.DeviceIdType.MESH


def scatter_kernel(
    counts, lt_ref, *refs
):
    n = len(counts)
    rs, small_ref, out_ref, every_ref = refs[:n], refs[n], refs[n + 1], refs[n + 2]
    (s, other, crecv, p1, m1, p2, m2, t, q1, r1, q2, r2, u, zrecv, every, ssem, rsem, gs, gr) = refs[
        n + 3 :
    ]
    blocks = sum(counts) + 1
    dp = lax.axis_index("dp")
    core = dp % 2
    x, y, zh = (dp // 2) % 4, (dp // 8) % 4, dp // 32
    a = jnp.where(core == 0, x, y)
    b = jnp.where(core == 0, y, x)

    def device(na, nb):
        nx = jnp.where(core == 0, na, nb)
        ny = jnp.where(core == 0, nb, na)
        return ((zh * 4 + ny) * 4 + nx) * 2 + core

    ap, am, a2 = (a + 1) % 4, (a + 3) % 4, (a + 2) % 4
    bp, bm, b2 = (b + 1) % 4, (b + 3) % 4, (b + 2) % 4
    to_ap, to_am = device(ap, b), device(am, b)
    to_bp, to_bm = device(a, bp), device(a, bm)
    to_a2, to_b2 = device(a2, b), device(a, b2)
    partner = dp + 1 - 2 * core
    across = dp + 32 - 64 * zh

    barrier = pltpu.get_barrier_semaphore()
    for d in (partner, to_ap, to_am, to_bp, to_bm, to_a2, to_b2, across):
        pl.semaphore_signal(barrier, inc=1, device_id={"dp": d}, device_id_type=MESH)
    pl.semaphore_wait(barrier, 8)

    def copy(kind, i, src, dst, d):
        return pltpu.make_async_remote_copy(
            src_ref=src,
            dst_ref=dst,
            send_sem=ssem.at[kind, i],
            recv_sem=rsem.at[kind, i],
            device_id={"dp": d},
            device_id_type=MESH,
        )

    def copies(stage, i):
        if stage == 0:
            return [copy(0, i, other.at[i % 4], crecv.at[i], partner)]
        if stage == 1:
            return [
                copy(1, i, s.at[i, a2, pl.ds(0, 64)], p1.at[i], to_ap),
                copy(2, i, s.at[i, a2, pl.ds(64, 64)], m1.at[i], to_am),
            ]
        if stage == 2:
            return [
                copy(3, i, s.at[i, ap], p2.at[i], to_ap),
                copy(4, i, s.at[i, am], m2.at[i], to_am),
            ]
        if stage == 3:
            return [
                copy(5, i, t.at[i, b2, pl.ds(0, 16)], q1.at[i], to_bp),
                copy(6, i, t.at[i, b2, pl.ds(16, 16)], r1.at[i], to_bm),
            ]
        if stage == 4:
            return [
                copy(7, i, t.at[i, bp], q2.at[i], to_bp),
                copy(8, i, t.at[i, bm], r2.at[i], to_bm),
            ]
        return [copy(9, i, u.at[i, 1 - zh], zrecv.at[i], across)]

    def start(stage, i):
        for c in copies(stage, i):
            c.start()

    def wait(stage, i):
        for c in copies(stage, i):
            c.wait()

    def make(i):
        first = 0
        for number, count in enumerate(counts):
            @pl.when((i >= first) & (i < first + count))
            def _(number=number, first=first):
                right = rs[number][:, pl.ds(pl.multiple_of((i - first) * W, W), W)]
                for chunk in range(4):
                    rows = pl.ds(chunk * 128, 128)
                    s[i, chunk] = dot(lt_ref[number, core, rows, :], right)
                    other[i % 4, chunk] = dot(lt_ref[number, 1 - core, rows, :], right)

            first += count

        @pl.when(i == blocks - 1)
        def _():
            for chunk in range(4):
                rows = pl.ds(chunk * 128, 128)
                s[i, chunk] = small_ref[core, rows, :]
                other[i % 4, chunk] = small_ref[1 - core, rows, :]

        start(0, i)

    def join_cores(i):
        wait(0, i)
        for chunk in range(4):
            s[i, chunk] = s[i, chunk] + crecv[i, chunk]
        start(1, i)

    def first_ring(i):
        wait(1, i)
        s[i, ap, :64] = s[i, ap, :64] + p1[i]
        s[i, am, 64:] = s[i, am, 64:] + m1[i]
        start(2, i)

    def first_done(i):
        wait(2, i)
        for chunk in range(4):
            rows = pl.ds(chunk * 32, 32)
            t[i, chunk] = s[i, a, rows] + p2[i, rows] + m2[i, rows]
        start(3, i)

    def second_ring(i):
        wait(3, i)
        t[i, bp, :16] = t[i, bp, :16] + q1[i]
        t[i, bm, 16:] = t[i, bm, 16:] + r1[i]
        start(4, i)

    def second_done(i):
        wait(4, i)
        for chunk in range(2):
            rows = pl.ds(chunk * 16, 16)
            u[i, chunk] = t[i, b, rows] + q2[i, rows] + r2[i, rows]
        start(5, i)

    def finish(i):
        wait(5, i)
        out_ref[i] = u[i, zh] + zrecv[i]

    stages = (make, join_cores, first_ring, first_done, second_ring, second_done, finish)

    def spread(number):
        mine = every.at[core]
        if number == 0:
            moves = [(0, mine.at[a, b, zh], across)]
        elif number == 1:
            moves = [(k + 1, mine.at[a, b], d) for k, d in enumerate((to_bp, to_bm, to_b2))]
        elif number == 2:
            moves = [(k + 4, mine.at[a], d) for k, d in enumerate((to_ap, to_am, to_a2))]
        else:
            moves = [(7, mine, partner)]
        return [
            pltpu.make_async_remote_copy(
                src_ref=place,
                dst_ref=place,
                send_sem=gs.at[k],
                recv_sem=gr.at[k],
                device_id={"dp": d},
                device_id_type=MESH,
            )
            for k, place, d in moves
        ]

    def spread_step(number):
        if number == 0:
            every[core, a, b, zh] = out_ref[blocks - 1, :, :128]
        else:
            for c in spread(number - 1):
                c.wait()
        if number < 4:
            for c in spread(number):
                c.start()
        else:
            every_ref[...] = every[...]

    def step(j, carry):
        for stage, offset in zip(stages, OFFSETS):
            i = j - offset

            @pl.when((i >= 0) & (i < blocks))
            def _(stage=stage, i=i):
                stage(i)

        return carry

    lax.fori_loop(0, blocks + OFFSETS[-1], step, 0)
    for number in range(5):
        spread_step(number)


def scatter(lefts, rights, small):
    counts = tuple(r.shape[1] // W for r in rights)
    nb = sum(counts) + 1
    vmem = pl.BlockSpec(memory_space=pltpu.VMEM)
    return pl.pallas_call(
        functools.partial(scatter_kernel, counts),
        out_shape=[
            jax.ShapeDtypeStruct((nb, 16, W), f32),
            jax.ShapeDtypeStruct((2, 4, 4, 2, 16, 128), f32),
        ],
        in_specs=[vmem] * (2 + len(rights)),
        out_specs=[vmem, vmem],
        scratch_shapes=[
            pltpu.VMEM((nb, 4, 128, W), f32),
            pltpu.VMEM((4, 4, 128, W), f32),
            pltpu.VMEM((nb, 4, 128, W), f32),
            pltpu.VMEM((nb, 64, W), f32),
            pltpu.VMEM((nb, 64, W), f32),
            pltpu.VMEM((nb, 128, W), f32),
            pltpu.VMEM((nb, 128, W), f32),
            pltpu.VMEM((nb, 4, 32, W), f32),
            pltpu.VMEM((nb, 16, W), f32),
            pltpu.VMEM((nb, 16, W), f32),
            pltpu.VMEM((nb, 32, W), f32),
            pltpu.VMEM((nb, 32, W), f32),
            pltpu.VMEM((nb, 2, 16, W), f32),
            pltpu.VMEM((nb, 16, W), f32),
            pltpu.VMEM((2, 4, 4, 2, 16, 128), f32),
            pltpu.SemaphoreType.DMA((10, nb)),
            pltpu.SemaphoreType.DMA((10, nb)),
            pltpu.SemaphoreType.DMA((8,)),
            pltpu.SemaphoreType.DMA((8,)),
        ],
        compiler_params=pltpu.CompilerParams(
            collective_id=0, has_side_effects=True, vmem_limit_bytes=62 * 2**20
        ),
    )(lefts, *rights, small)


def in_order(rows):
    wide = rows.reshape(2, 4, 4, 2, 16, -1)
    even = wide[:, :, :, 0].transpose(2, 1, 0, 3, 4).reshape(512, -1)
    odd = wide[:, :, :, 1].transpose(1, 2, 0, 3, 4).reshape(512, -1)
    return jnp.stack([even, odd])


def on_device(
    tokens,
    gain_one,
    shift_one,
    qkv_weight,
    qv_bias,
    out_weight,
    out_bias,
    gain_two,
    shift_two,
    up_weight,
    up_bias,
    down_weight,
    down_bias,
    cotangent,
):
    length = tokens.shape[0]
    dp, tensor = lax.axis_index("dp"), lax.axis_index("tensor")
    core, x, y = dp % 2, (dp // 2) % 4, (dp // 8) % 4
    ring = jnp.where(core == 0, x, y)
    ring_other = jnp.where(core == 0, y, x)
    piece_id = 4 * core + ring
    offsets = (0, 3, 1, 2)
    other_ids = [4 * core + (ring + o) % 4 for o in offsets]
    other_ids += [4 * (1 - core) + (ring_other + o) % 4 for o in offsets]

    qkv_t = qkv_weight.transpose(1, 2, 0)
    head_piece = jnp.concatenate(
        [
            lax.dynamic_slice_in_dim(qkv_t, piece_id * DH, DH, 1),
            lax.dynamic_slice_in_dim(out_weight, piece_id * DH, DH, 0)[None],
        ],
        axis=0,
    ).astype(f32)
    biases = jnp.concatenate([qv_bias.reshape(-1), up_bias]).astype(f32)
    other_biases = send(biases, along_z(1))
    heads = gather_other(head_piece)
    unit_piece = jnp.stack(
        [
            lax.dynamic_slice_in_dim(up_weight, piece_id * 256, 256, 1).T,
            lax.dynamic_slice_in_dim(down_weight, piece_id * 256, 256, 0),
        ]
    ).astype(f32)
    units = gather_other(unit_piece)

    nothing = jnp.minimum(jnp.abs(gain_one[0]), 0.0)

    def rounded(received):
        return (received + nothing).astype(bf16)

    inputs = tokens.astype(f32)
    n_one, r_one = layer_norm_parts(inputs)
    normed_one = (n_one * gain_one + shift_one).astype(bf16)

    own_bias = qv_bias.astype(f32)
    q_own = (dot(normed_one, qkv_weight[:, 0]) + own_bias[0]).astype(bf16)
    k_own = dot(normed_one, qkv_weight[:, 1]).astype(bf16)
    v_own = (dot(normed_one, qkv_weight[:, 2]) + own_bias[1]).astype(bf16)
    own_heads = tensor * 8 + jnp.arange(8, dtype=jnp.int32)
    slopes_own = jnp.exp2(-8.0 * (own_heads + 1).astype(f32) / 16)
    att_own, lse_own = attend(slopes_own, q_own, k_own, v_own)

    wq, wk, wv, wo = (jnp.concatenate([rounded(h[i]) for h in heads], axis=0) for i in range(4))
    other_qv = other_biases[:1024].reshape(2, 8, DH)
    other_qv = jnp.concatenate(
        [lax.dynamic_slice_in_dim(other_qv, i, 1, 1) for i in other_ids], axis=1
    ).reshape(2, 512)
    q_oth = (dot(normed_one, wq, NT) + other_qv[0]).astype(bf16)
    k_oth = dot(normed_one, wk, NT).astype(bf16)
    v_oth = (dot(normed_one, wv, NT) + other_qv[1]).astype(bf16)
    oth_heads = (1 - tensor) * 8 + jnp.stack(other_ids).astype(jnp.int32)
    slopes_oth = jnp.exp2(-8.0 * (oth_heads + 1).astype(f32) / 16)
    att_oth, lse_oth = attend(slopes_oth, q_oth, k_oth, v_oth)

    branch = dot(att_own, out_weight) + dot(att_oth, wo) + out_bias.astype(f32)
    middle = inputs + branch
    n_two, r_two = layer_norm_parts(middle)
    normed_two = (n_two * gain_two + shift_two).astype(bf16)

    hidden_own = dot(normed_two, up_weight) + up_bias.astype(f32)
    up_oth = jnp.concatenate([rounded(u[0]) for u in units], axis=0)
    down_oth = jnp.concatenate([rounded(u[1]) for u in units], axis=0)
    bias_oth = other_biases[1024:].reshape(8, 256)
    bias_oth = jnp.concatenate(
        [lax.dynamic_slice_in_dim(bias_oth, i, 1, 0) for i in other_ids], axis=0
    ).reshape(2048)
    hidden_oth = dot(normed_two, up_oth, NT) + bias_oth
    active_own, slope_own = gelu_both(hidden_own)
    active_oth, slope_oth = gelu_both(hidden_oth)
    active_own, active_oth = active_own.astype(bf16), active_oth.astype(bf16)
    feed_out = dot(active_own, down_weight) + dot(active_oth, down_oth) + down_bias.astype(f32)
    block_out = (middle + feed_out).astype(bf16)

    cot_wide = cotangent.astype(f32)
    grad_down_bias = jnp.sum(cot_wide, axis=0)
    gh_own = (dot(cotangent, down_weight, NT) * slope_own).astype(bf16)
    gh_oth = (dot(cotangent, down_oth, NT) * slope_oth).astype(bf16)
    grad_up_bias = jnp.sum(gh_own.astype(f32), axis=0)
    grad_normed_two = dot(gh_own, up_weight, NT) + dot(gh_oth, up_oth)
    back_two, grad_gain_two, grad_shift_two = layer_norm_back(
        grad_normed_two, n_two, r_two, gain_two
    )
    grad_middle = cot_wide + back_two
    grad_branch = grad_middle.astype(bf16)
    grad_out_bias = jnp.sum(grad_branch.astype(f32), axis=0)
    ga_own = dot(grad_branch, out_weight, NT).astype(bf16)
    ga_oth = dot(grad_branch, wo, NT).astype(bf16)
    dq_own, dk_own, dv_own = attend_back(slopes_own, q_own, k_own, v_own, lse_own, ga_own)
    dq_oth, dk_oth, dv_oth = attend_back(slopes_oth, q_oth, k_oth, v_oth, lse_oth, ga_oth)
    grad_qv_bias = jnp.stack(
        [jnp.sum(dq_own.astype(f32), axis=0), jnp.sum(dv_own.astype(f32), axis=0)]
    )

    grad_normed_one = (
        dot(dq_own, qkv_weight[:, 0], NT)
        + dot(dk_own, qkv_weight[:, 1], NT)
        + dot(dv_own, qkv_weight[:, 2], NT)
        + dot(dq_oth, wq)
        + dot(dk_oth, wk)
        + dot(dv_oth, wv)
    )
    back_one, grad_gain_one, grad_shift_one = layer_norm_back(
        grad_normed_one, n_one, r_one, gain_one
    )
    token_grad = grad_middle + back_one

    vectors = jnp.stack(
        [
            grad_gain_one,
            grad_shift_one,
            grad_out_bias,
            grad_gain_two,
            grad_shift_two,
            grad_down_bias,
            grad_up_bias[:1024],
            grad_up_bias[1024:],
            grad_qv_bias.reshape(-1),
        ],
        axis=1,
    )
    small = in_order(jnp.pad(vectors, ((0, 0), (0, W - 9))))
    lefts = jnp.stack([in_order(m.T) for m in (cotangent, normed_two, grad_branch, normed_one)])
    stack = jnp.concatenate([dq_own, dk_own, dv_own], axis=1)
    shares, everyone = scatter(lefts, (active_own, gh_own, att_own, stack), small)

    def columns(first, count):
        return shares[first : first + count].transpose(1, 0, 2).reshape(16, count * W)

    share_down = columns(0, 8).T
    share_up = columns(8, 8)
    share_out = columns(16, 2).T
    share_qkv = columns(18, 6).reshape(16, 3, 512)
    vector = shares[24]
    even = everyone[0, ..., 6:9].transpose(2, 1, 0, 3, 4)
    odd = everyone[1, ..., 6:9].transpose(2, 0, 1, 3, 4)
    summed = jnp.stack([even, odd], axis=3).reshape(1024, 3)
    return (
        block_out,
        token_grad,
        vector[:, 0],
        vector[:, 1],
        share_qkv,
        summed[:, 2].reshape(2, 512),
        share_out,
        vector[:, 2],
        vector[:, 3],
        vector[:, 4],
        share_up,
        jnp.concatenate([summed[:, 0], summed[:, 1]]),
        share_down,
        vector[:, 5],
    )


def solution(mesh):
    placed = (
        P("dp", None),
        P(),
        P(),
        P(None, None, "tensor"),
        P(None, "tensor"),
        P("tensor", None),
        P(),
        P(),
        P(),
        P(None, "tensor"),
        P("tensor"),
        P("tensor", None),
        P(),
        P("dp", None),
    )
    return jax.shard_map(
        on_device,
        mesh=mesh,
        in_specs=placed,
        out_specs=(
            P("dp", None),
            P("dp", None),
            P("dp"),
            P("dp"),
            P("dp", None, "tensor"),
            P(None, "tensor"),
            P("tensor", "dp"),
            P("dp"),
            P("dp"),
            P("dp"),
            P("dp", "tensor"),
            P("tensor"),
            P("tensor", "dp"),
            P("dp"),
        ),
        check_vma=False,
    )
```

```python
import functools
import math

import jax
import jax.numpy as jnp
from jax import lax
from jax.experimental import pallas as pl
from jax.experimental.pallas import tpu as pltpu
from jax.sharding import PartitionSpec as P

DH = 64
epsilon = 1e-05
bf16 = jnp.bfloat16
f32 = jnp.float32


def layer_norm_parts(values):
    centre = jnp.mean(values, axis=-1, keepdims=True)
    centered = values - centre
    spread = jnp.mean(centered * centered, axis=-1, keepdims=True)
    r = lax.rsqrt(spread + epsilon)
    return centered * r, r


def layer_norm_back(grad, n, r, gain):
    e = grad * gain
    mean_e = jnp.mean(e, axis=-1, keepdims=True)
    mean_en = jnp.mean(e * n, axis=-1, keepdims=True)
    return (
        r * (e - mean_e - n * mean_en),
        jnp.sum(grad * n, axis=0),
        jnp.sum(grad, axis=0),
    )


GC, GA = 0.7978845608028654, 0.044715


def gelu_both(v):
    t = jnp.tanh(GC * (v + GA * v * v * v))
    value = 0.5 * v * (1.0 + t)
    slope = 0.5 * (1.0 + t) + 0.5 * v * (1.0 - t * t) * GC * (1.0 + 3.0 * GA * v * v)
    return value, slope


NT = (((1,), (1,)), ((), ()))
TN = (((0,), (0,)), ((), ()))
NN = (((1,), (0,)), ((), ()))


def dot(a, b, dims=NN):
    return lax.dot_general(a, b, dims, preferred_element_type=f32)


def half_lanes(block, side):
    lane = lax.broadcasted_iota(jnp.int32, block.shape, 1)
    return jnp.where((lane >= 64) == (side == 1), block, jnp.zeros_like(block))


def pair_scores(q, k, side, slope):
    s = dot(half_lanes(q, side), k, NT) * 0.125
    row = lax.broadcasted_iota(jnp.int32, s.shape, 0)
    col = lax.broadcasted_iota(jnp.int32, s.shape, 1)
    distance = (row - col).astype(f32)
    return jnp.where(row >= col, s - slope * distance, -1000000000.0)


def attend_pair(q, k, v, slopes):
    outs, lses = [], []
    for side in range(2):
        s = pair_scores(q, k, side, slopes[side])
        top = jnp.max(s, axis=-1, keepdims=True)
        e = jnp.exp(s - top)
        total = jnp.sum(e, axis=-1, keepdims=True)
        a = (e * (1.0 / total)).astype(bf16)
        outs.append(dot(a, v))
        lses.append(top + jnp.log(total))
    lane = lax.broadcasted_iota(jnp.int32, outs[0].shape, 1)
    return jnp.where(lane < 64, outs[0], outs[1]).astype(bf16), lses


def attend_back_pair(q, k, v, lse, g, slopes):
    dqs, dks, dvs = [], [], []
    for side in range(2):
        s = pair_scores(q, k, side, slopes[side])
        a = jnp.exp(s - lse[side])
        w = dot(half_lanes(g, side), v, NT)
        inner = jnp.sum(a * w, axis=-1, keepdims=True)
        ds = (a * (w - inner)).astype(bf16)
        dvs.append(dot(a.astype(bf16), g, TN))
        dqs.append(dot(ds, k) * 0.125)
        dks.append(dot(ds, q, TN) * 0.125)
    lane = lax.broadcasted_iota(jnp.int32, dqs[0].shape, 1)
    return [jnp.where(lane < 64, p[0], p[1]).astype(bf16) for p in (dqs, dks, dvs)]


def unit_block(n2, cot, up, up_dims, bias, down):
    value, slope = gelu_both(dot(n2, up, up_dims) + bias)
    active = value.astype(bf16)
    gh = (dot(cot, down, NT) * slope).astype(bf16)
    back_dims = NT if up_dims is NN else NN
    return active, gh, dot(active, down), dot(gh, up, back_dims)


MESH = pl.DeviceIdType.MESH


def forward_kernel(
    slopes,
    tokens,
    rows_ref,
    wqkv,
    own_bias,
    bias_piece,
    wout,
    piece,
    up_any,
    up_bias,
    down_any,
    cot_any,
    gain_two,
    down_bias,
    n1_ref,
    q_ref,
    k_ref,
    v_ref,
    att_ref,
    lse_ref,
    woth_ref,
    units_any,
    n2_ref,
    act_ref,
    gh_ref,
    gb_ref,
    out_ref,
    grad_ref,
    branch_ref,
    vec_ref,
    got,
    got_bias,
    bias_out,
    up,
    down,
    cot,
    feed_ref,
    gn_ref,
    hsend,
    hrecv,
    usend,
    urecv,
    bsend,
    brecv,
    lsem,
    fsem,
):
    dp, tensor = lax.axis_index("dp"), lax.axis_index("tensor")
    core, x, y, zh = dp % 2, (dp // 2) % 4, (dp // 8) % 4, dp // 32
    z = zh * 2 + tensor
    ring = jnp.where(core == 0, x, y)

    def device(nx, ny, nz, nc):
        return ((((nz // 2) * 4 + ny) * 4 + nx) * 2 + nc, nz % 2)

    def on_ring(r):
        return device(jnp.where(core == 0, r, x), jnp.where(core == 0, y, r), z, core)

    z_plus, z_minus = device(x, y, (z + 1) % 4, core), device(x, y, (z + 3) % 4, core)
    r_plus, r_minus = on_ring((ring + 1) % 4), on_ring((ring + 3) % 4)
    partner = device(x, y, z, 1 - core)
    barrier = pltpu.get_barrier_semaphore()
    for d in (z_plus, z_minus, r_plus, r_minus, partner):
        pl.semaphore_signal(barrier, inc=1, device_id=d, device_id_type=MESH)
    pl.semaphore_wait(barrier, 5)

    local = [
        pltpu.make_async_copy(a, b, lsem.at[k])
        for k, (a, b) in enumerate(((up_any, up), (down_any, down), (cot_any, cot)))
    ]
    for c in local:
        c.start()

    def place(u, slot, sub):
        at = pl.ds(sub * 64, 64)
        return got.at[slot, at] if u == 0 else units_any.at[u - 1, slot, at]

    def move(u, src, slot, sub, way, target):
        send = hsend.at[slot, sub, way] if u == 0 else usend.at[u - 1, slot, sub, way]
        recv = hrecv.at[slot, sub] if u == 0 else urecv.at[u - 1, slot, sub]
        return pltpu.make_async_remote_copy(
            src_ref=src,
            dst_ref=place(u, slot, sub),
            send_sem=send,
            recv_sem=recv,
            device_id=target,
            device_id_type=MESH,
        )

    started = [[], [], []]

    def begin(u, src, slot, sub, target):
        c = move(u, src, slot, sub, 0, target)
        c.start()
        started[u].append(c)

    def arrived(u, slot, sub):
        move(u, place(u, slot, sub), slot, sub, 0, partner).wait_recv()

    bias_move = pltpu.make_async_remote_copy(
        src_ref=bias_piece, dst_ref=got_bias, send_sem=bsend, recv_sem=brecv, device_id=z_plus, device_id_type=MESH
    )
    for u in range(3):
        for sub in (0, 2, 1, 3):
            begin(u, piece.at[u, pl.ds(sub * 64, 64)], 0, sub, z_plus if sub < 2 else z_minus)
        if u == 0:
            bias_move.start()
    for sub in (0, 2, 1, 3):
        begin(2, piece.at[3, pl.ds(sub * 64, 64)], 3, sub, z_plus if sub < 2 else z_minus)

    def own_came(u, subs):
        for sub in subs:
            arrived(u, 0, sub)
            begin(u, place(u, 0, sub), 1, sub, r_plus)
            begin(u, place(u, 0, sub), 2, sub, r_minus)
        for sub in subs:
            begin(u, place(u, 0, sub), 4, sub, partner)

    def next_came(u, low, high):
        arrived(u, 1, low)
        if low < 2 and u < 2:
            begin(u, place(u, 1, low), 3, low, r_plus)
        begin(u, place(u, 1, low), 5, low, partner)
        arrived(u, 2, high)
        if high >= 2 and u < 2:
            begin(u, place(u, 2, high), 3, high, r_minus)
        begin(u, place(u, 2, high), 6, high, partner)

    def far_came(u, subs):
        for sub in subs:
            arrived(u, 3, sub)
            begin(u, place(u, 3, sub), 7, sub, partner)

    def swapped(u, slots):
        for slot in slots:
            for sub in range(4):
                arrived(u, slot, sub)

    pump = [lambda u=u, f=f: f(u) for u in range(3) for f in (
        lambda u: own_came(u, (0, 2)),
        lambda u: own_came(u, (1, 3)),
        lambda u: next_came(u, 0, 2),
        lambda u: next_came(u, 2, 0),
        lambda u: next_came(u, 1, 3),
        lambda u: next_came(u, 3, 1),
        lambda u: far_came(u, (0, 2)),
        lambda u: far_came(u, (1, 3)),
        lambda u: swapped(u, range(4, 8) if u < 2 else (4, 5, 6)),
    )]

    def norm_one(r, carry):
        at = pl.ds(r * 128, 128)
        n, _ = layer_norm_parts(tokens[at, :].astype(f32))
        n1_ref[at, :] = (n * rows_ref[0:1, :] + rows_ref[1:2, :]).astype(bf16)
        return carry

    lax.fori_loop(0, 4, norm_one, 0)
    n1 = n1_ref[...]
    q_ref[0] = (dot(n1, wqkv[0]) + own_bias[0:1, :]).astype(bf16)
    k_ref[0] = dot(n1, wqkv[1]).astype(bf16)
    v_ref[0] = (dot(n1, wqkv[2]) + own_bias[1:2, :]).astype(bf16)

    lse_ref[...] = jnp.zeros_like(lse_ref)

    def put_lse(head, pair):
        lane = lax.broadcasted_iota(jnp.int32, lse_ref.shape, 1)
        for side in range(2):
            lse_ref[...] = jnp.where(lane == head + side, pair[side], lse_ref[...])

    def own_pair(p, carry):
        lanes = pl.ds(pl.multiple_of(p * 128, 128), 128)
        out, lse = attend_pair(
            q_ref[0, :, lanes], k_ref[0, :, lanes], v_ref[0, :, lanes], (slopes[2 * p], slopes[2 * p + 1])
        )
        att_ref[0, :, lanes] = out
        put_lse(2 * p, lse)
        return carry

    lax.fori_loop(0, 1, own_pair, 0)
    pump[0]()
    lax.fori_loop(1, 4, own_pair, 0)
    pump[1]()
    pump[2]()
    feed_ref[...] = dot(att_ref[0], wout[...])
    for k in range(3, 6):
        pump[k]()
    bias_move.wait()
    ring_other = jnp.where(core == 0, y, x)
    for k, o in enumerate((0, 3, 1, 2)):
        for slot, pid in ((k, 4 * core + (ring + o) % 4), (k + 4, 4 * (1 - core) + (ring_other + o) % 4)):
            bias_out[slot : slot + 1, :] = got_bias[pl.ds(pid, 1), :]
            bias_out[8 + slot : 9 + slot, :] = got_bias[pl.ds(8 + pid, 1), :]

    def other_pair(p, carry):
        lanes = pl.ds(pl.multiple_of(p * 128, 128), 128)
        for m in range(4):
            for side in range(2):
                at = pl.ds(pl.multiple_of(p * 128 + side * 64, 64), 64)
                woth_ref[m, at, :] = got[2 * p + side, m * 64 : m * 64 + 64, :].astype(bf16)
        low, high = bias_out[pl.ds(2 * p, 1), :], bias_out[pl.ds(2 * p + 1, 1), :]
        parts = []
        for m in range(3):
            parts.append(dot(n1_ref[...], woth_ref[m, lanes, :], NT))
        lane = lax.broadcasted_iota(jnp.int32, (1, 128), 1)
        q = (parts[0] + jnp.where(lane < 64, low[:, :128], high[:, :128])).astype(bf16)
        k = parts[1].astype(bf16)
        v = (parts[2] + jnp.where(lane < 64, low[:, 128:], high[:, 128:])).astype(bf16)
        q_ref[1, :, lanes] = q
        k_ref[1, :, lanes] = k
        v_ref[1, :, lanes] = v
        out, lse = attend_pair(q, k, v, (slopes[8 + 2 * p], slopes[9 + 2 * p]))
        att_ref[1, :, lanes] = out
        put_lse(8 + 2 * p, lse)
        return carry

    lax.fori_loop(0, 1, other_pair, 0)
    for k in (9, 6, 7, 8, 10):
        pump[k]()
    lax.fori_loop(1, 4, other_pair, 0)
    pump[11]()
    feed_ref[...] += dot(att_ref[1], woth_ref[3])
    pump[12]()

    def norm_two(r, carry):
        at = pl.ds(r * 128, 128)
        middle = tokens[at, :].astype(f32) + (feed_ref[at, :] + rows_ref[4:5, :])
        grad_ref[at, :] = middle
        n, _ = layer_norm_parts(middle)
        n2_ref[at, :] = (n * rows_ref[2:3, :] + rows_ref[3:4, :]).astype(bf16)
        return carry

    lax.fori_loop(0, 4, norm_two, 0)
    pump[13]()
    pump[14]()
    for c in local:
        c.wait()
    feed_ref[...] = jnp.zeros_like(feed_ref)
    gn_ref[...] = jnp.zeros_like(gn_ref)

    def unit_step(i, carry):
        lanes = pl.ds(pl.multiple_of(i * 512, 512), 512)
        active, gh, feed, gn = unit_block(
            n2_ref[...], cot[...], up[:, lanes], NN, up_bias[:, lanes], down[lanes, :]
        )
        act_ref[:, lanes] = active
        gh_ref[:, lanes] = gh
        gb_ref[:, lanes] = jnp.sum(gh.astype(f32), axis=0, keepdims=True)
        feed_ref[...] += feed
        gn_ref[...] += gn
        return carry

    def fetch(number, slot):
        return [
            pltpu.make_async_copy(units_any.at[k, slot], got.at[2 * number + k], fsem.at[number, k])
            for k in range(2)
        ]

    def other_step(number, slot):
        for c in fetch(number, slot):
            c.wait()
        _, _, feed, gn = unit_block(
            n2_ref[...],
            cot[...],
            got[2 * number].astype(bf16),
            NT,
            bias_out[8 + slot : 9 + slot, :],
            got[2 * number + 1].astype(bf16),
        )
        feed_ref[...] += feed
        gn_ref[...] += gn

    def bring(number, slot):
        for c in fetch(number, slot):
            c.start()

    lax.fori_loop(0, 1, unit_step, 0)
    for k in (18, 15, 16):
        pump[k]()
    lax.fori_loop(1, 2, unit_step, 0)
    for k in (19, 17):
        pump[k]()
    lax.fori_loop(2, 3, unit_step, 0)
    pump[20]()
    pump[21]()
    lax.fori_loop(3, 4, unit_step, 0)
    for c in started[0]:
        c.wait_send()
    bring(0, 0)
    swapped(2, (4,))
    bring(1, 4)
    other_step(0, 0)
    pump[22]()
    pump[24]()
    pump[25]()
    bring(0, 3)
    other_step(1, 4)
    swapped(2, (7,))
    bring(1, 7)
    other_step(0, 3)
    pump[23]()
    bring(0, 1)
    other_step(1, 7)
    bring(1, 2)
    other_step(0, 1)
    swapped(2, (5, 6))
    bring(0, 5)
    other_step(1, 2)
    bring(1, 6)
    other_step(0, 5)
    other_step(1, 6)
    vec_ref[...] = jnp.zeros_like(vec_ref)

    def rows_of(r, carry):
        at = pl.ds(pl.multiple_of(r * 64, 64), 64)
        middle = grad_ref[at, :]
        cotangent = cot[at, :].astype(f32)
        out_ref[at, :] = (middle + (feed_ref[at, :] + down_bias[...])).astype(bf16)
        n, root = layer_norm_parts(middle)
        back, ggain, gshift = layer_norm_back(gn_ref[at, :], n, root, gain_two[...])
        whole = cotangent + back
        rounded = whole.astype(bf16)
        grad_ref[at, :] = whole
        branch_ref[at, :] = rounded
        vec_ref[0:1, :] += ggain[None]
        vec_ref[1:2, :] += gshift[None]
        vec_ref[2:3, :] += jnp.sum(rounded.astype(f32), axis=0, keepdims=True)
        vec_ref[3:4, :] += jnp.sum(cotangent, axis=0, keepdims=True)
        return carry

    lax.fori_loop(0, 8, rows_of, 0)
    for c in started[1] + started[2]:
        c.wait_send()


def forward(slopes, tokens, rows, wqkv, own_bias, bias_piece, wout, piece, up, up_bias, down, cot, gain, db):
    length, width = tokens.shape
    local, units = wout.shape[0], up.shape[1]
    vmem = pl.BlockSpec(memory_space=pltpu.VMEM)
    hbm = pl.BlockSpec(memory_space=pl.ANY)

    def out(shape, kind):
        return jax.ShapeDtypeStruct(shape, kind)

    return pl.pallas_call(
        forward_kernel,
        in_specs=[pl.BlockSpec(memory_space=pltpu.SMEM)] + [vmem] * 7 + [hbm, vmem, hbm, hbm, vmem, vmem],
        out_specs=[vmem] * 7 + [hbm] + [vmem] * 8,
        out_shape=[
            out((length, width), bf16),
            out((2, length, local), bf16),
            out((2, length, local), bf16),
            out((2, length, local), bf16),
            out((2, length, local), bf16),
            out((length, 128), f32),
            out((4, local, width), bf16),
            out((2, 8, 256, width), f32),
            out((length, width), bf16),
            out((length, units), bf16),
            out((length, units), bf16),
            out((1, units), f32),
            out((length, width), bf16),
            out((length, width), f32),
            out((length, width), bf16),
            out((8, width), f32),
        ],
        scratch_shapes=[
            pltpu.VMEM((8, 256, width), f32),
            pltpu.VMEM((16, 256), f32),
            pltpu.VMEM((16, 256), f32),
            pltpu.VMEM((width, units), bf16),
            pltpu.VMEM((units, width), bf16),
            pltpu.VMEM((length, width), bf16),
            pltpu.VMEM((length, width), f32),
            pltpu.VMEM((length, width), f32),
            pltpu.SemaphoreType.DMA((8, 4, 1)),
            pltpu.SemaphoreType.DMA((8, 4)),
            pltpu.SemaphoreType.DMA((2, 8, 4, 1)),
            pltpu.SemaphoreType.DMA((2, 8, 4)),
            pltpu.SemaphoreType.DMA,
            pltpu.SemaphoreType.DMA,
            pltpu.SemaphoreType.DMA((3,)),
            pltpu.SemaphoreType.DMA((2, 2)),
        ],
        compiler_params=pltpu.CompilerParams(
            collective_id=1, has_side_effects=True, vmem_limit_bytes=62 * 2**20
        ),
    )(slopes, tokens, rows, wqkv, own_bias, bias_piece, wout, piece, up, up_bias, down, cot, gain, db)


W = 512
OFFSETS = (0, 1, 2, 3, 4, 5, 6)
SLOTS = 4


def ring_scratch(nb):
    return [
        pltpu.VMEM((2, 512, 512), bf16),
        pltpu.VMEM((SLOTS, 4, 128, W), f32),
        pltpu.VMEM((2, 4, 128, W), f32),
        pltpu.VMEM((SLOTS, 4, 128, W), f32),
        pltpu.VMEM((nb, 64, W), f32),
        pltpu.VMEM((nb, 64, W), f32),
        pltpu.VMEM((nb, 128, W), f32),
        pltpu.VMEM((nb, 128, W), f32),
        pltpu.VMEM((SLOTS, 4, 32, W), f32),
        pltpu.VMEM((nb, 16, W), f32),
        pltpu.VMEM((nb, 16, W), f32),
        pltpu.VMEM((nb, 32, W), f32),
        pltpu.VMEM((nb, 32, W), f32),
        pltpu.VMEM((SLOTS, 2, 16, W), f32),
        pltpu.VMEM((nb, 16, W), f32),
        pltpu.SemaphoreType.DMA((10, nb)),
        pltpu.SemaphoreType.DMA((10, nb)),
        pltpu.SemaphoreType.REGULAR,
    ]


class Ring:
    def __init__(self, blocks, narrow, scratch):
        self.blocks, self.narrow = blocks, narrow
        (
            self.lt, self.s, self.other, self.crecv, self.p1, self.m1, self.p2, self.m2, self.t,
            self.q1, self.r1, self.q2, self.r2, self.u, self.zrecv, self.ssem, self.rsem, self.credit,
        ) = scratch
        dp = lax.axis_index("dp")
        core = dp % 2
        x, y, zh = (dp // 2) % 4, (dp // 8) % 4, dp // 32
        self.core, self.zh = core, zh
        a = jnp.where(core == 0, x, y)
        b = jnp.where(core == 0, y, x)
        self.a, self.b = a, b

        def device(na, nb):
            nx = jnp.where(core == 0, na, nb)
            ny = jnp.where(core == 0, nb, na)
            return ((zh * 4 + ny) * 4 + nx) * 2 + core

        self.ap, self.am, self.a2 = (a + 1) % 4, (a + 3) % 4, (a + 2) % 4
        self.bp, self.bm, self.b2 = (b + 1) % 4, (b + 3) % 4, (b + 2) % 4
        self.to_ap, self.to_am = device(self.ap, b), device(self.am, b)
        self.to_bp, self.to_bm = device(a, self.bp), device(a, self.bm)
        self.to_a2, self.to_b2 = device(self.a2, b), device(a, self.b2)
        self.partner = dp + 1 - 2 * core
        self.across = dp + 32 - 64 * zh
        barrier = pltpu.get_barrier_semaphore()
        everyone = (
            self.partner, self.to_ap, self.to_am, self.to_bp, self.to_bm, self.to_a2, self.to_b2, self.across,
        )
        for d in everyone:
            pl.semaphore_signal(barrier, inc=1, device_id={"dp": d}, device_id_type=MESH)
        pl.semaphore_wait(barrier, 8)

    def copies(self, stage, i, wide):
        def copy(kind, src, dst, d):
            if not wide:
                lanes = (slice(None),) * (len(src.shape) - 1) + (pl.ds(0, 128),)
                src, dst = src.at[lanes], dst.at[lanes]
            return pltpu.make_async_remote_copy(
                src_ref=src,
                dst_ref=dst,
                send_sem=self.ssem.at[kind, i],
                recv_sem=self.rsem.at[kind, i],
                device_id={"dp": d},
                device_id_type=MESH,
            )

        k = i % SLOTS
        if stage == 0:
            return [copy(0, self.other.at[i % 2], self.crecv.at[k], self.partner)]
        if stage == 1:
            return [
                copy(1, self.s.at[k, self.a2, pl.ds(0, 64)], self.p1.at[i], self.to_ap),
                copy(2, self.s.at[k, self.a2, pl.ds(64, 64)], self.m1.at[i], self.to_am),
            ]
        if stage == 2:
            return [
                copy(3, self.s.at[k, self.ap], self.p2.at[i], self.to_ap),
                copy(4, self.s.at[k, self.am], self.m2.at[i], self.to_am),
            ]
        if stage == 3:
            return [
                copy(5, self.t.at[k, self.b2, pl.ds(0, 16)], self.q1.at[i], self.to_bp),
                copy(6, self.t.at[k, self.b2, pl.ds(16, 16)], self.r1.at[i], self.to_bm),
            ]
        if stage == 4:
            return [
                copy(7, self.t.at[k, self.bp], self.q2.at[i], self.to_bp),
                copy(8, self.t.at[k, self.bm], self.r2.at[i], self.to_bm),
            ]
        return [copy(9, self.u.at[k, 1 - self.zh], self.zrecv.at[i], self.across)]

    def each(self, stage, i, act):
        few = functools.reduce(jnp.logical_or, [i == n for n in self.narrow])
        for wide in (True, False):
            @pl.when(few != wide)
            def _(wide=wide):
                for c in self.copies(stage, i, wide):
                    act(c)

    def start(self, stage, i):
        self.each(stage, i, lambda c: c.start())

    def wait(self, stage, i):
        self.each(stage, i, lambda c: c.wait())

    @staticmethod
    def slabs(part):
        for k in range(8):
            yx, c = k // 2, k % 2
            half, row = part // 4, part % 4
            first, second = (yx, row) if c == 0 else (row, yx)
            yield c, first, (second * 2 + half) * 16, k * 16

    def turn(self, left):
        for part in range(8):
            flipped = left[:, part * 128 : (part + 1) * 128].T
            for c, first, at, row in self.slabs(part):
                self.lt[c, first * 128 + at : first * 128 + at + 16, :] = flipped[row : row + 16, :]

    def make_product(self, i, right):
        own = dot(self.lt[self.core], right)
        away = dot(self.lt[1 - self.core], right)
        for chunk in range(4):
            self.s[i % SLOTS, chunk] = own[chunk * 128 : (chunk + 1) * 128]
            self.other[i % 2, chunk] = away[chunk * 128 : (chunk + 1) * 128]

    def make_small(self, i, small):
        k = i % SLOTS
        for part in range(8):
            flipped = small[:, part * 128 : (part + 1) * 128].T
            for c, first, at, row in self.slabs(part):
                @pl.when(self.core == c)
                def _(first=first, at=at, row=row, flipped=flipped):
                    self.s[k, first, at : at + 16, :128] = flipped[row : row + 16, :]

                @pl.when(self.core != c)
                def _(first=first, at=at, row=row, flipped=flipped):
                    self.other[i % 2, first, at : at + 16, :128] = flipped[row : row + 16, :]

    def sent(self, i):
        @pl.when(i >= SLOTS)
        def _():
            pl.semaphore_wait(self.credit, 1)

        self.start(0, i)

    def join_cores(self, i):
        self.wait(0, i)
        k = i % SLOTS
        for chunk in range(4):
            self.s[k, chunk] = self.s[k, chunk] + self.crecv[k, chunk]

        @pl.when(i + SLOTS < self.blocks)
        def _():
            pl.semaphore_signal(
                self.credit, inc=1, device_id={"dp": self.partner}, device_id_type=MESH
            )

        self.start(1, i)

    def first_ring(self, i):
        self.wait(1, i)
        s, k = self.s, i % SLOTS
        s[k, self.ap, :64] = s[k, self.ap, :64] + self.p1[i]
        s[k, self.am, 64:] = s[k, self.am, 64:] + self.m1[i]
        self.start(2, i)

    def first_done(self, i):
        self.wait(2, i)
        k = i % SLOTS
        for chunk in range(4):
            rows = pl.ds(chunk * 32, 32)
            self.t[k, chunk] = self.s[k, self.a, rows] + self.p2[i, rows] + self.m2[i, rows]
        self.start(3, i)

    def second_ring(self, i):
        self.wait(3, i)
        t, k = self.t, i % SLOTS
        t[k, self.bp, :16] = t[k, self.bp, :16] + self.q1[i]
        t[k, self.bm, 16:] = t[k, self.bm, 16:] + self.r1[i]
        self.start(4, i)

    def second_done(self, i):
        self.wait(4, i)
        k = i % SLOTS
        for chunk in range(2):
            rows = pl.ds(chunk * 16, 16)
            self.u[k, chunk] = self.t[k, self.b, rows] + self.q2[i, rows] + self.r2[i, rows]
        self.start(5, i)

    def share(self, i):
        self.wait(5, i)
        return self.u[i % SLOTS, self.zh] + self.zrecv[i]

    def run(self, make, finish, extra):
        def made(i):
            make(i)
            self.sent(i)

        stages = (
            made, self.join_cores, self.first_ring, self.first_done, self.second_ring, self.second_done,
            lambda i: finish(i, self.share(i)),
        )

        def step(j, carry):
            for stage, offset in zip(stages, OFFSETS):
                i = j - offset

                @pl.when((i >= 0) & (i < self.blocks))
                def _(stage=stage, i=i):
                    stage(i)

            extra(j)
            return carry

        lax.fori_loop(0, self.blocks + OFFSETS[-1], step, 0)


def cols_of(i, first):
    return pl.ds(pl.multiple_of((i - first) * W, W), W)


def at_step(cond):
    def wrap(f):
        pl.when(cond)(f)

    return wrap


def back_kernel(
    slopes, n2_ref, cot_ref, branch_ref, n1_ref, lse_ref, vec_two, up_sums, gain_ref,
    act_any, gh_any, att_any, q_any, k_any, v_any, wout_any, woth_any, wqkv_any, tokens_any, grad_any,
    down_out, up_out, out_out, qkv_out, vec_out, vec_late, sum_out, token_ref,
    rbuf, q_v, k_v, v_v, wout, woth, wqkv, tokens, grad, ga, dq, dk, dv, small, every,
    rsems, lsem, gs, gr, *ring_refs,
):
    early = ((q_any, q_v), (k_any, k_v), (v_any, v_v), (wout_any, wout), (woth_any, woth))
    late = ((wqkv_any, wqkv), (tokens_any, tokens), (grad_any, grad))
    local = [
        pltpu.make_async_copy(src, dst, lsem.at[k]) for k, (src, dst) in enumerate(early + late)
    ]

    def right(kind, i):
        src = (act_any, gh_any)[kind]
        return pltpu.make_async_copy(src.at[:, cols_of(i, 4 * kind)], rbuf.at[i % 2], rsems.at[i % 2])

    right(0, 0).start()
    for c in local:
        c.start()
    att_copy = pltpu.make_async_copy(att_any.at[0], ga.at[0], rsems.at[2])
    ring = Ring(14, (8, 13), ring_refs)
    core, a, b, zh = ring.core, ring.a, ring.b, ring.zh
    parts = (dq, dk, dv)

    def make(i):
        for first, left in ((0, cot_ref), (4, n2_ref), (9, branch_ref), (10, n1_ref)):
            @pl.when(i == first)
            def _(left=left):
                ring.turn(left)

        for kind in range(2):
            @pl.when((i + 1 >= 4 * kind) & (i + 1 < 4 * kind + 4))
            def _(kind=kind):
                right(kind, i + 1).start()

        for kind in range(2):
            @pl.when((i >= 4 * kind) & (i < 4 * kind + 4))
            def _(kind=kind):
                right(kind, i).wait()
                ring.make_product(i, rbuf[i % 2])

        @pl.when(i == 8)
        def _():
            small[...] = jnp.zeros_like(small)
            small[0:8, :] = vec_two[...]
            small[10:12, :] = up_sums[...]
            small[12:13, :512] = jnp.sum(dq[0].astype(f32), axis=0, keepdims=True)
            small[12:13, 512:] = jnp.sum(dv[0].astype(f32), axis=0, keepdims=True)

        @pl.when((i == 8) | (i == 13))
        def _():
            ring.make_small(i, small)

        @pl.when(i == 9)
        def _():
            att_copy.wait()
            ring.make_product(i, ga[0])

        for k in range(3):
            @pl.when(i == 10 + k)
            def _(k=k):
                ring.make_product(i, parts[k][0])

    def finish(i, share):
        for first, target in ((0, down_out), (4, up_out)):
            @pl.when((i >= first) & (i < first + 4))
            def _(first=first, target=target):
                target[:, cols_of(i, first)] = share

        @pl.when(i == 8)
        def _():
            vec_out[...] = share[:, :128]

        @pl.when(i == 9)
        def _():
            out_out[...] = share

        @pl.when((i >= 10) & (i < 13))
        def _():
            qkv_out[:, cols_of(i, 10)] = share

        @pl.when(i == 13)
        def _():
            vec_late[...] = share[:, :128]

    def spread(number):
        mine = every.at[core]
        if number == 0:
            moves = [(0, mine.at[a, b, zh], ring.across)]
        elif number == 1:
            targets = (ring.to_bp, ring.to_bm, ring.to_b2)
            moves = [(k + 1, mine.at[a, b], d) for k, d in enumerate(targets)]
        elif number == 2:
            targets = (ring.to_ap, ring.to_am, ring.to_a2)
            moves = [(k + 4, mine.at[a], d) for k, d in enumerate(targets)]
        else:
            moves = [(7, mine, ring.partner)]
        return [
            pltpu.make_async_remote_copy(
                src_ref=place,
                dst_ref=place,
                send_sem=gs.at[k],
                recv_sem=gr.at[k],
                device_id={"dp": d},
                device_id_type=MESH,
            )
            for k, place, d in moves
        ]

    def spread_step(number):
        if number == 0:
            every[core, a, b, zh] = vec_out[...]
        else:
            for c in spread(number - 1):
                c.wait()
        if number < 4:
            for c in spread(number):
                c.start()
        else:
            for part in range(8):
                rows = [None] * 8
                for c, first, at, row in ring.slabs(part):
                    rows[row // 16] = every[c, first, at // 32, (at // 16) % 2]
                flipped = jnp.concatenate(rows, axis=0).T
                sum_out[:, part * 128 : (part + 1) * 128] = flipped[8:16]

    def extra(j):
        @pl.when(j == 0)
        def _():
            for c in local[:5]:
                c.wait()
            ga[0] = dot(branch_ref[...], wout[...], NT).astype(bf16)
            ga[1] = dot(branch_ref[...], woth[3], NT).astype(bf16)

        @pl.when((j >= 1) & (j < 9))
        def _():
            pair = j - 1
            half, p = pair // 4, pair % 4
            lanes = pl.ds(pl.multiple_of(p * 128, 128), 128)
            lane = lax.broadcasted_iota(jnp.int32, lse_ref.shape, 1)
            lses = [
                jnp.sum(jnp.where(lane == 2 * pair + side, lse_ref[...], 0.0), axis=1, keepdims=True)
                for side in range(2)
            ]
            one, two, three = attend_back_pair(
                q_v[half, :, lanes],
                k_v[half, :, lanes],
                v_v[half, :, lanes],
                lses,
                ga[half, :, lanes],
                (slopes[2 * pair], slopes[2 * pair + 1]),
            )
            dq[half, :, lanes] = one
            dk[half, :, lanes] = two
            dv[half, :, lanes] = three

        @pl.when(j == 8)
        def _():
            att_copy.start()

        for k in range(3):
            @pl.when(j == 9 + k)
            def _(k=k):
                if k == 0:
                    for c in local[5:]:
                        c.wait()
                one = dot(parts[k][0], wqkv[k], NT)
                two = dot(parts[k][1], woth[k])
                if k == 0:
                    token_ref[...] = one + two
                else:
                    token_ref[...] += one + two

        @pl.when(j == 12)
        def _():
            def rows_of(r, carry):
                rows = pl.ds(pl.multiple_of(r * 64, 64), 64)
                n, root = layer_norm_parts(tokens[rows, :].astype(f32))
                back, ggain, gshift = layer_norm_back(token_ref[rows, :], n, root, gain_ref[...])
                token_ref[rows, :] = grad[rows, :] + back
                small[8:9, :] += ggain[None]
                small[9:10, :] += gshift[None]
                return carry

            lax.fori_loop(0, 8, rows_of, 0)

        for number in range(5):
            @pl.when(j == 15 + number)
            def _(number=number):
                spread_step(number)

    ring.run(make, finish, extra)


def backward(slopes, n2, cot, branch, n1, lse, vec, up_sums, gain, act, gh, att, q, k, v, wout, woth, wqkv, tokens, grad):
    length, width = n1.shape
    vmem = pl.BlockSpec(memory_space=pltpu.VMEM)
    hbm = pl.BlockSpec(memory_space=pl.ANY)
    return pl.pallas_call(
        back_kernel,
        in_specs=[pl.BlockSpec(memory_space=pltpu.SMEM)] + [vmem] * 8 + [hbm] * 11,
        out_specs=[vmem] * 8,
        out_shape=[
            jax.ShapeDtypeStruct((16, 2048), f32),
            jax.ShapeDtypeStruct((16, 2048), f32),
            jax.ShapeDtypeStruct((16, 512), f32),
            jax.ShapeDtypeStruct((16, 1536), f32),
            jax.ShapeDtypeStruct((16, 128), f32),
            jax.ShapeDtypeStruct((16, 128), f32),
            jax.ShapeDtypeStruct((8, 1024), f32),
            jax.ShapeDtypeStruct((length, width), f32),
        ],
        scratch_shapes=[
            pltpu.VMEM((2, length, W), bf16),
            pltpu.VMEM(q.shape, bf16),
            pltpu.VMEM(q.shape, bf16),
            pltpu.VMEM(q.shape, bf16),
            pltpu.VMEM(wout.shape, bf16),
            pltpu.VMEM(woth.shape, bf16),
            pltpu.VMEM(wqkv.shape, bf16),
            pltpu.VMEM(tokens.shape, bf16),
            pltpu.VMEM(grad.shape, f32),
            pltpu.VMEM(q.shape, bf16),
            pltpu.VMEM(q.shape, bf16),
            pltpu.VMEM(q.shape, bf16),
            pltpu.VMEM(q.shape, bf16),
            pltpu.VMEM((128, width), f32),
            pltpu.VMEM((2, 4, 4, 2, 16, 128), f32),
            pltpu.SemaphoreType.DMA((3,)),
            pltpu.SemaphoreType.DMA((8,)),
            pltpu.SemaphoreType.DMA((8,)),
            pltpu.SemaphoreType.DMA((8,)),
            *ring_scratch(14),
        ],
        compiler_params=pltpu.CompilerParams(
            collective_id=0, has_side_effects=True, vmem_limit_bytes=63 * 2**20
        ),
    )(slopes, n2, cot, branch, n1, lse, vec, up_sums, gain, act, gh, att, q, k, v, wout, woth, wqkv, tokens, grad)


def on_device(
    tokens,
    gain_one,
    shift_one,
    qkv_weight,
    qv_bias,
    out_weight,
    out_bias,
    gain_two,
    shift_two,
    up_weight,
    up_bias,
    down_weight,
    down_bias,
    cotangent,
):
    dp, tensor = lax.axis_index("dp"), lax.axis_index("tensor")
    core, x, y = dp % 2, (dp // 2) % 4, (dp // 8) % 4
    ring = jnp.where(core == 0, x, y)
    ring_other = jnp.where(core == 0, y, x)
    piece_id = 4 * core + ring
    far_id = 4 * core + (ring + 2) % 4
    offsets = (0, 3, 1, 2)
    other_ids = [4 * core + (ring + o) % 4 for o in offsets]
    other_ids += [4 * (1 - core) + (ring_other + o) % 4 for o in offsets]

    qkv_t = qkv_weight.transpose(1, 2, 0)
    head_piece = jnp.concatenate(
        [
            lax.dynamic_slice_in_dim(qkv_t, piece_id * DH, DH, 1).reshape(3 * DH, -1),
            lax.dynamic_slice_in_dim(out_weight, piece_id * DH, DH, 0),
        ],
        axis=0,
    )
    piece = jnp.stack(
        [
            head_piece,
            lax.dynamic_slice_in_dim(up_weight, piece_id * 256, 256, 1).T,
            lax.dynamic_slice_in_dim(down_weight, piece_id * 256, 256, 0),
            lax.dynamic_slice_in_dim(down_weight, far_id * 256, 256, 0),
        ]
    ).astype(f32)
    own_bias = qv_bias.astype(f32)
    by_head = own_bias.reshape(2, 8, DH)
    bias_piece = jnp.concatenate(
        [
            jnp.concatenate([by_head[0], by_head[0], by_head[1], by_head[1]], axis=1),
            up_bias.astype(f32).reshape(8, 256),
        ],
        axis=0,
    )
    own_heads = tensor * 8 + jnp.arange(8, dtype=jnp.int32)
    oth_heads = (1 - tensor) * 8 + jnp.stack(other_ids).astype(jnp.int32)
    slopes = jnp.exp2(-8.0 * (jnp.concatenate([own_heads, oth_heads]) + 1).astype(f32) / 16)
    rows = jnp.concatenate(
        [
            jnp.stack([gain_one, shift_one, gain_two, shift_two, out_bias.astype(f32)]),
            jnp.zeros((3, 1024), f32),
        ]
    )
    wqkv = qkv_weight.transpose(1, 0, 2)
    (
        normed_one,
        queries,
        key_rows,
        values,
        attended,
        lse,
        woth,
        _,
        normed_two,
        active_own,
        gh_own,
        grad_up_bias,
        block_out,
        grad_middle,
        grad_branch,
        sums_two,
    ) = forward(
        slopes,
        tokens,
        rows,
        wqkv,
        own_bias,
        bias_piece,
        out_weight,
        piece,
        up_weight,
        up_bias.astype(f32)[None],
        down_weight,
        cotangent,
        gain_two[None],
        down_bias.astype(f32)[None],
    )
    share_down, share_up, share_out, share_qkv, vector, late, summed, token_grad = backward(
        slopes,
        normed_two,
        cotangent,
        grad_branch,
        normed_one,
        lse,
        sums_two,
        grad_up_bias.reshape(2, 1024),
        gain_one[None],
        active_own,
        gh_own,
        attended,
        queries,
        key_rows,
        values,
        out_weight,
        woth,
        wqkv,
        tokens,
        grad_middle,
    )
    return (
        block_out,
        token_grad,
        late[:, 8],
        late[:, 9],
        share_qkv.reshape(16, 3, 512),
        summed[4].reshape(2, 512),
        share_out.T,
        vector[:, 2],
        vector[:, 0],
        vector[:, 1],
        share_up,
        summed[2:4].reshape(2048),
        share_down.T,
        vector[:, 3],
    )


def solution(mesh):
    placed = (
        P("dp", None),
        P(),
        P(),
        P(None, None, "tensor"),
        P(None, "tensor"),
        P("tensor", None),
        P(),
        P(),
        P(),
        P(None, "tensor"),
        P("tensor"),
        P("tensor", None),
        P(),
        P("dp", None),
    )
    return jax.shard_map(
        on_device,
        mesh=mesh,
        in_specs=placed,
        out_specs=(
            P("dp", None),
            P("dp", None),
            P("dp"),
            P("dp"),
            P("dp", None, "tensor"),
            P(None, "tensor"),
            P("tensor", "dp"),
            P("dp"),
            P("dp"),
            P("dp"),
            P("dp", "tensor"),
            P("tensor"),
            P("tensor", "dp"),
            P("dp"),
        ),
        check_vma=False,
    )
```

```python
import functools
import math

import jax
import jax.numpy as jnp
from jax import lax
from jax.experimental import pallas as pl
from jax.experimental.pallas import tpu as pltpu
from jax.sharding import PartitionSpec as P

DH = 64
epsilon = 1e-05
bf16 = jnp.bfloat16
f32 = jnp.float32


def layer_norm_parts(values):
    centre = jnp.mean(values, axis=-1, keepdims=True)
    centered = values - centre
    spread = jnp.mean(centered * centered, axis=-1, keepdims=True)
    r = lax.rsqrt(spread + epsilon)
    return centered * r, r


def layer_norm_back(grad, n, r, gain):
    e = grad * gain
    mean_e = jnp.mean(e, axis=-1, keepdims=True)
    mean_en = jnp.mean(e * n, axis=-1, keepdims=True)
    return (
        r * (e - mean_e - n * mean_en),
        jnp.sum(grad * n, axis=0),
        jnp.sum(grad, axis=0),
    )


GC, GA = 0.7978845608028654, 0.044715


def gelu_both(v):
    square = v * v
    h = 0.5 + 0.5 * jnp.tanh(v * (GC + GC * GA * square))
    value = v * h
    slope = h + (value * (1.0 - h)) * (2.0 * GC + 6.0 * GC * GA * square)
    return value, slope


NT = (((1,), (1,)), ((), ()))
TN = (((0,), (0,)), ((), ()))
NN = (((1,), (0,)), ((), ()))


def dot(a, b, dims=NN):
    return lax.dot_general(a, b, dims, preferred_element_type=f32)


def half_lanes(block, side):
    lane = lax.broadcasted_iota(jnp.int32, block.shape, 1)
    return jnp.where((lane >= 64) == (side == 1), block, jnp.zeros_like(block))


def fill_distance(ref):
    row = lax.broadcasted_iota(jnp.int32, ref.shape, 0)
    col = lax.broadcasted_iota(jnp.int32, ref.shape, 1)
    ref[...] = jnp.where(row >= col, (row - col).astype(f32), 1e30)


def attend_pair(q, k, v, slopes, distance):
    outs, lses = [], []
    scaled = q * 0.125
    for side in range(2):
        out, lse = [], []
        for rows, keys in ((slice(0, 256), 256), (slice(256, 512), 512)):
            s = dot(half_lanes(scaled[rows], side), k[:keys], NT) - slopes[side] * distance[rows, :keys]
            top = jnp.max(s, axis=-1, keepdims=True)
            e = jnp.exp(s - top)
            total = jnp.sum(e, axis=-1, keepdims=True)
            out.append(dot((e * (1.0 / total)).astype(bf16), v[:keys]))
            lse.append(top + jnp.log(total))
        outs.append(jnp.concatenate(out, axis=0))
        lses.append(jnp.concatenate(lse, axis=0))
    lane = lax.broadcasted_iota(jnp.int32, outs[0].shape, 1)
    return jnp.where(lane < 64, outs[0], outs[1]).astype(bf16), lses


def attend_back_pair(q, k, v, lse, g, slopes, distance):
    dqs, dks, dvs = [], [], []
    scaled = q * 0.125
    for side in range(2):
        dq, dk, dv = [], [], []
        for rows, keys in ((slice(0, 256), 256), (slice(256, 512), 512)):
            s = dot(half_lanes(scaled[rows], side), k[:keys], NT) - slopes[side] * distance[rows, :keys]
            a = jnp.exp(s - lse[side][rows])
            w = dot(half_lanes(g[rows], side), v[:keys], NT)
            inner = jnp.sum(a * w, axis=-1, keepdims=True)
            ds = (a * (w - inner)).astype(bf16)
            dv.append(dot(a.astype(bf16), g[rows], TN))
            dq.append(dot(ds, k[:keys]) * 0.125)
            dk.append(dot(ds, q[rows], TN) * 0.125)
        dqs.append(jnp.concatenate(dq, axis=0))
        for parts, total in ((dk, dks), (dv, dvs)):
            total.append(jnp.concatenate([parts[0] + parts[1][:256], parts[1][256:]], axis=0))
    lane = lax.broadcasted_iota(jnp.int32, dqs[0].shape, 1)
    return [jnp.where(lane < 64, p[0], p[1]).astype(bf16) for p in (dqs, dks, dvs)]


def unit_block(n2, cot, up, up_dims, bias, down):
    value, slope = gelu_both(dot(n2, up, up_dims) + bias)
    active = value.astype(bf16)
    gh = (dot(cot, down, NT) * slope).astype(bf16)
    back_dims = NT if up_dims is NN else NN
    return active, gh, dot(active, down), dot(gh, up, back_dims)


MESH = pl.DeviceIdType.MESH


def forward_kernel(
    slopes,
    tokens,
    rows_ref,
    low_rows,
    wqkv,
    wout,
    up_any,
    down_any,
    cot_any,
    n1_out,
    q_out,
    k_out,
    v_out,
    att_out,
    lse_ref,
    woth_out,
    units_any,
    n2_out,
    act_out,
    gh_out,
    gb_ref,
    out_ref,
    grad_ref,
    branch_ref,
    vec_ref,
    n1_ref,
    q_ref,
    k_ref,
    v_ref,
    att_ref,
    woth_ref,
    n2_ref,
    act_ref,
    gh_ref,
    bias_rows,
    bias_piece,
    piece,
    turned,
    distance,
    got,
    got_bias,
    bias_out,
    up,
    down,
    cot,
    feed_ref,
    gn_ref,
    hsend,
    hrecv,
    usend,
    urecv,
    bsend,
    brecv,
    lsem,
    fsem,
    osem,
):
    dp, tensor = lax.axis_index("dp"), lax.axis_index("tensor")
    core, x, y, zh = dp % 2, (dp // 2) % 4, (dp // 8) % 4, dp // 32
    z = zh * 2 + tensor
    ring = jnp.where(core == 0, x, y)

    def device(nx, ny, nz, nc):
        return ((((nz // 2) * 4 + ny) * 4 + nx) * 2 + nc, nz % 2)

    def on_ring(r):
        return device(jnp.where(core == 0, r, x), jnp.where(core == 0, y, r), z, core)

    z_plus, z_minus = device(x, y, (z + 1) % 4, core), device(x, y, (z + 3) % 4, core)
    r_plus, r_minus = on_ring((ring + 1) % 4), on_ring((ring + 3) % 4)
    partner = device(x, y, z, 1 - core)
    barrier = pltpu.get_barrier_semaphore()
    for d in (z_plus, z_minus, r_plus, r_minus, partner):
        pl.semaphore_signal(barrier, inc=1, device_id=d, device_id_type=MESH)
    local = [
        pltpu.make_async_copy(a, b, lsem.at[k])
        for k, (a, b) in enumerate(((up_any, up), (down_any, down), (cot_any, cot)))
    ]
    for c in local:
        c.start()
    pid, fid = 4 * core + ring, 4 * core + (ring + 2) % 4
    for m in range(3):
        turned[...] = wqkv[m, :, pl.ds(pl.multiple_of(pid // 2 * 128, 128), 128)].T
        side = pl.ds(pl.multiple_of(pid % 2 * 64, 64), 64)
        piece[0, m * 64 : m * 64 + 64, :] = turned[side, :].astype(f32)
    piece[0, 192:256, :] = wout[pl.ds(pl.multiple_of(pid * 64, 64), 64), :].astype(f32)
    bias_rows[...] = low_rows[...].astype(f32)
    for p in range(8):
        q_part = bias_rows[4:5, 64 * p : 64 * p + 64]
        v_part = bias_rows[4:5, 512 + 64 * p : 576 + 64 * p]
        bias_piece[p : p + 1, :] = jnp.concatenate([q_part, q_part, v_part, v_part], axis=1)
        bias_piece[8 + p : 9 + p, :] = bias_rows[2 + p // 4 : 3 + p // 4, p % 4 * 256 : p % 4 * 256 + 256]
    pl.semaphore_wait(barrier, 5)

    def place(u, slot, sub):
        at = pl.ds(sub * 64, 64)
        return got.at[slot, at] if u == 0 else units_any.at[u - 1, slot, at]

    def move(u, src, slot, sub, way, target):
        send = hsend.at[slot, sub, way] if u == 0 else usend.at[u - 1, slot, sub, way]
        recv = hrecv.at[slot, sub] if u == 0 else urecv.at[u - 1, slot, sub]
        return pltpu.make_async_remote_copy(
            src_ref=src,
            dst_ref=place(u, slot, sub),
            send_sem=send,
            recv_sem=recv,
            device_id=target,
            device_id_type=MESH,
        )

    started = [[], [], []]

    def begin(u, src, slot, sub, target):
        c = move(u, src, slot, sub, 0, target)
        c.start()
        started[u].append(c)

    def arrived(u, slot, sub):
        move(u, place(u, slot, sub), slot, sub, 0, partner).wait_recv()

    bias_move = pltpu.make_async_remote_copy(
        src_ref=bias_piece, dst_ref=got_bias, send_sem=bsend, recv_sem=brecv, device_id=z_plus, device_id_type=MESH
    )
    outgoing = []

    def leave(k, src, dst):
        c = pltpu.make_async_copy(src, dst, osem.at[k])
        c.start()
        outgoing.append(c)

    def to_z(u, src, slot):
        for sub in (0, 2, 1, 3):
            begin(u, piece.at[src, pl.ds(sub * 64, 64)], slot, sub, z_plus if sub < 2 else z_minus)

    to_z(0, 0, 0)
    bias_move.start()
    fill_distance(distance)

    def own_came(u, subs):
        for sub in subs:
            arrived(u, 0, sub)
            begin(u, place(u, 0, sub), 1, sub, r_plus)
            begin(u, place(u, 0, sub), 2, sub, r_minus)
        for sub in subs:
            begin(u, place(u, 0, sub), 4, sub, partner)

    def next_came(u, low, high):
        arrived(u, 1, low)
        if low < 2 and u < 2:
            begin(u, place(u, 1, low), 3, low, r_plus)
        begin(u, place(u, 1, low), 5, low, partner)
        arrived(u, 2, high)
        if high >= 2 and u < 2:
            begin(u, place(u, 2, high), 3, high, r_minus)
        begin(u, place(u, 2, high), 6, high, partner)

    def far_came(u, subs):
        for sub in subs:
            arrived(u, 3, sub)
            begin(u, place(u, 3, sub), 7, sub, partner)

    def swapped(u, slots):
        for slot in slots:
            for sub in range(4):
                arrived(u, slot, sub)

    pump = [lambda u=u, f=f: f(u) for u in range(3) for f in (
        lambda u: own_came(u, (0, 2)),
        lambda u: own_came(u, (1, 3)),
        lambda u: next_came(u, 0, 2),
        lambda u: next_came(u, 2, 0),
        lambda u: next_came(u, 1, 3),
        lambda u: next_came(u, 3, 1),
        lambda u: far_came(u, (0, 2)),
        lambda u: far_came(u, (1, 3)),
        lambda u: swapped(u, range(4, 8) if u < 2 else (4, 5, 6)),
    )]

    def norm_one(r, carry):
        at = pl.ds(r * 128, 128)
        n, _ = layer_norm_parts(tokens[at, :].astype(f32))
        n1_ref[at, :] = (n * rows_ref[0:1, :] + rows_ref[1:2, :]).astype(bf16)
        return carry

    lax.fori_loop(0, 4, norm_one, 0)
    n1 = n1_ref[...]
    q_ref[0] = (dot(n1, wqkv[0]) + bias_rows[4:5, :512]).astype(bf16)
    k_ref[0] = dot(n1, wqkv[1]).astype(bf16)
    v_ref[0] = (dot(n1, wqkv[2]) + bias_rows[4:5, 512:]).astype(bf16)
    leave(0, n1_ref, n1_out)
    for c in local:
        c.wait()
    piece[1] = up[:, pl.ds(pl.multiple_of(pid * 256, 256), 256)].T.astype(f32)
    piece[2] = down[pl.ds(pl.multiple_of(pid * 256, 256), 256), :].astype(f32)
    piece[3] = down[pl.ds(pl.multiple_of(fid * 256, 256), 256), :].astype(f32)
    to_z(1, 1, 0)
    to_z(2, 2, 0)
    to_z(2, 3, 3)

    lse_ref[...] = jnp.zeros_like(lse_ref)

    def put_lse(head, pair):
        lane = lax.broadcasted_iota(jnp.int32, lse_ref.shape, 1)
        for side in range(2):
            lse_ref[...] = jnp.where(lane == head + side, pair[side], lse_ref[...])

    def own_pair(p, carry):
        lanes = pl.ds(pl.multiple_of(p * 128, 128), 128)
        out, lse = attend_pair(
            q_ref[0, :, lanes], k_ref[0, :, lanes], v_ref[0, :, lanes], (slopes[2 * p], slopes[2 * p + 1]), distance
        )
        att_ref[0, :, lanes] = out
        put_lse(2 * p, lse)
        return carry

    lax.fori_loop(0, 1, own_pair, 0)
    pump[0]()
    lax.fori_loop(1, 4, own_pair, 0)
    pump[1]()
    pump[2]()
    feed_ref[...] = dot(att_ref[0], wout[...])
    for k in range(3, 6):
        pump[k]()
    bias_move.wait()
    ring_other = jnp.where(core == 0, y, x)
    for k, o in enumerate((0, 3, 1, 2)):
        for slot, pid in ((k, 4 * core + (ring + o) % 4), (k + 4, 4 * (1 - core) + (ring_other + o) % 4)):
            bias_out[slot : slot + 1, :] = got_bias[pl.ds(pid, 1), :]
            bias_out[8 + slot : 9 + slot, :] = got_bias[pl.ds(8 + pid, 1), :]

    def other_pair(p, carry):
        lanes = pl.ds(pl.multiple_of(p * 128, 128), 128)
        for m in range(4):
            for side in range(2):
                at = pl.ds(pl.multiple_of(p * 128 + side * 64, 64), 64)
                woth_ref[m, at, :] = got[2 * p + side, m * 64 : m * 64 + 64, :].astype(bf16)
        low, high = bias_out[pl.ds(2 * p, 1), :], bias_out[pl.ds(2 * p + 1, 1), :]
        parts = []
        for m in range(3):
            parts.append(dot(n1_ref[...], woth_ref[m, lanes, :], NT))
        lane = lax.broadcasted_iota(jnp.int32, (1, 128), 1)
        q = (parts[0] + jnp.where(lane < 64, low[:, :128], high[:, :128])).astype(bf16)
        k = parts[1].astype(bf16)
        v = (parts[2] + jnp.where(lane < 64, low[:, 128:], high[:, 128:])).astype(bf16)
        q_ref[1, :, lanes] = q
        k_ref[1, :, lanes] = k
        v_ref[1, :, lanes] = v
        out, lse = attend_pair(q, k, v, (slopes[8 + 2 * p], slopes[9 + 2 * p]), distance)
        att_ref[1, :, lanes] = out
        put_lse(8 + 2 * p, lse)
        return carry

    lax.fori_loop(0, 1, other_pair, 0)
    for k in (9, 6, 7, 8, 10):
        pump[k]()
    lax.fori_loop(1, 4, other_pair, 0)
    pump[11]()
    feed_ref[...] += dot(att_ref[1], woth_ref[3])
    pump[12]()

    def norm_two(r, carry):
        at = pl.ds(r * 128, 128)
        middle = tokens[at, :].astype(f32) + (feed_ref[at, :] + bias_rows[0:1, :])
        grad_ref[at, :] = middle
        n, _ = layer_norm_parts(middle)
        n2_ref[at, :] = (n * rows_ref[2:3, :] + rows_ref[3:4, :]).astype(bf16)
        return carry

    lax.fori_loop(0, 4, norm_two, 0)
    leave(1, q_ref, q_out)
    leave(2, k_ref, k_out)
    leave(3, v_ref, v_out)
    leave(4, att_ref, att_out)
    leave(5, woth_ref, woth_out)
    leave(6, n2_ref, n2_out)
    pump[13]()
    pump[14]()
    feed_ref[...] = jnp.zeros_like(feed_ref)
    gn_ref[...] = jnp.zeros_like(gn_ref)

    def unit_step(i, carry):
        lanes = pl.ds(pl.multiple_of(i * 512, 512), 512)
        within = pl.ds(pl.multiple_of(i % 2 * 512, 512), 512)
        where = (pl.ds(2 + i // 2, 1), within)
        active, gh, feed, gn = unit_block(
            n2_ref[...], cot[...], up[:, lanes], NN, bias_rows[where], down[lanes, :]
        )
        act_ref[:, lanes] = active
        gh_ref[:, lanes] = gh
        gb_ref[pl.ds(i // 2, 1), within] = jnp.sum(gh.astype(f32), axis=0, keepdims=True)
        feed_ref[...] += feed
        gn_ref[...] += gn
        return carry

    def fetch(number, slots):
        return [
            pltpu.make_async_copy(
                units_any.at[k, slot], got.at[4 * number + 2 * k + n], fsem.at[number, 2 * k + n]
            )
            for k in range(2)
            for n, slot in enumerate(slots)
        ]

    def other_step(number, slots):
        for c in fetch(number, slots):
            c.wait()
        up_two, down_two = (
            jnp.concatenate([got[4 * number + 2 * k].astype(bf16), got[4 * number + 2 * k + 1].astype(bf16)], axis=0)
            for k in range(2)
        )
        bias = jnp.concatenate([bias_out[8 + slot : 9 + slot, :] for slot in slots], axis=1)
        _, _, feed, gn = unit_block(n2_ref[...], cot[...], up_two, NT, bias, down_two)
        feed_ref[...] += feed
        gn_ref[...] += gn

    def bring(number, slots):
        for c in fetch(number, slots):
            c.start()

    lax.fori_loop(0, 1, unit_step, 0)
    for k in (18, 15, 16):
        pump[k]()
    lax.fori_loop(1, 2, unit_step, 0)
    for k in (19, 17):
        pump[k]()
    lax.fori_loop(2, 3, unit_step, 0)
    pump[20]()
    pump[21]()
    lax.fori_loop(3, 4, unit_step, 0)
    leave(7, act_ref, act_out)
    leave(8, gh_ref, gh_out)
    for c in started[0]:
        c.wait_send()
    swapped(2, (4,))
    bring(0, (0, 4))
    pump[22]()
    pump[24]()
    pump[25]()
    swapped(2, (7,))
    bring(1, (3, 7))
    other_step(0, (0, 4))
    pump[23]()
    bring(0, (1, 2))
    other_step(1, (3, 7))
    swapped(2, (5, 6))
    bring(1, (5, 6))
    other_step(0, (1, 2))
    other_step(1, (5, 6))
    vec_ref[...] = jnp.zeros_like(vec_ref)

    def rows_of(r, carry):
        at = pl.ds(pl.multiple_of(r * 64, 64), 64)
        middle = grad_ref[at, :]
        cotangent = cot[at, :].astype(f32)
        out_ref[at, :] = (middle + (feed_ref[at, :] + bias_rows[1:2, :])).astype(bf16)
        n, root = layer_norm_parts(middle)
        back, ggain, gshift = layer_norm_back(gn_ref[at, :], n, root, rows_ref[2:3, :])
        whole = cotangent + back
        rounded = whole.astype(bf16)
        grad_ref[at, :] = whole
        branch_ref[at, :] = rounded
        vec_ref[0:1, :] += ggain[None]
        vec_ref[1:2, :] += gshift[None]
        vec_ref[2:3, :] += jnp.sum(rounded.astype(f32), axis=0, keepdims=True)
        vec_ref[3:4, :] += jnp.sum(cotangent, axis=0, keepdims=True)
        return carry

    lax.fori_loop(0, 8, rows_of, 0)
    for c in started[1] + started[2]:
        c.wait_send()
    for c in outgoing:
        c.wait()


def forward(slopes, tokens, rows, low_rows, wqkv, wout, up, down, cot):
    length, width = tokens.shape
    local, units = wout.shape[0], up.shape[1]
    vmem = pl.BlockSpec(memory_space=pltpu.VMEM)
    hbm = pl.BlockSpec(memory_space=pl.ANY)

    def out(shape, kind):
        return jax.ShapeDtypeStruct(shape, kind)

    return pl.pallas_call(
        forward_kernel,
        in_specs=[pl.BlockSpec(memory_space=pltpu.SMEM)] + [vmem] * 5 + [hbm] * 3,
        out_specs=[hbm] * 5 + [vmem] + [hbm] * 5 + [vmem] * 5,
        out_shape=[
            out((length, width), bf16),
            out((2, length, local), bf16),
            out((2, length, local), bf16),
            out((2, length, local), bf16),
            out((2, length, local), bf16),
            out((length, 128), f32),
            out((4, local, width), bf16),
            out((2, 8, 256, width), f32),
            out((length, width), bf16),
            out((length, units), bf16),
            out((length, units), bf16),
            out((2, width), f32),
            out((length, width), bf16),
            out((length, width), f32),
            out((length, width), bf16),
            out((8, width), f32),
        ],
        scratch_shapes=[
            pltpu.VMEM((length, width), bf16),
            *[pltpu.VMEM((2, length, local), bf16)] * 4,
            pltpu.VMEM((4, local, width), bf16),
            pltpu.VMEM((length, width), bf16),
            pltpu.VMEM((length, units), bf16),
            pltpu.VMEM((length, units), bf16),
            pltpu.VMEM((8, width), f32),
            pltpu.VMEM((16, 256), f32),
            pltpu.VMEM((4, 256, width), f32),
            pltpu.VMEM((128, width), bf16),
            pltpu.VMEM((length, length), f32),
            pltpu.VMEM((8, 256, width), f32),
            pltpu.VMEM((16, 256), f32),
            pltpu.VMEM((16, 256), f32),
            pltpu.VMEM((width, units), bf16),
            pltpu.VMEM((units, width), bf16),
            pltpu.VMEM((length, width), bf16),
            pltpu.VMEM((length, width), f32),
            pltpu.VMEM((length, width), f32),
            pltpu.SemaphoreType.DMA((8, 4, 1)),
            pltpu.SemaphoreType.DMA((8, 4)),
            pltpu.SemaphoreType.DMA((2, 8, 4, 1)),
            pltpu.SemaphoreType.DMA((2, 8, 4)),
            pltpu.SemaphoreType.DMA,
            pltpu.SemaphoreType.DMA,
            pltpu.SemaphoreType.DMA((3,)),
            pltpu.SemaphoreType.DMA((2, 4)),
            pltpu.SemaphoreType.DMA((9,)),
        ],
        compiler_params=pltpu.CompilerParams(
            collective_id=1, has_side_effects=True, vmem_limit_bytes=62 * 2**20
        ),
    )(slopes, tokens, rows, low_rows, wqkv, wout, up, down, cot)


W = 512
OFFSETS = (0, 1, 2, 3, 4, 5, 6)
SLOTS = 4


def ring_scratch(nb):
    return [
        pltpu.VMEM((2, 512, 512), bf16),
        pltpu.VMEM((SLOTS, 4, 128, W), f32),
        pltpu.VMEM((2, 4, 128, W), f32),
        pltpu.VMEM((SLOTS, 4, 128, W), f32),
        pltpu.VMEM((nb, 64, W), f32),
        pltpu.VMEM((nb, 64, W), f32),
        pltpu.VMEM((nb, 128, W), f32),
        pltpu.VMEM((nb, 128, W), f32),
        pltpu.VMEM((SLOTS, 4, 32, W), f32),
        pltpu.VMEM((nb, 16, W), f32),
        pltpu.VMEM((nb, 16, W), f32),
        pltpu.VMEM((nb, 32, W), f32),
        pltpu.VMEM((nb, 32, W), f32),
        pltpu.VMEM((SLOTS, 2, 16, W), f32),
        pltpu.VMEM((nb, 16, W), f32),
        pltpu.SemaphoreType.DMA((10, nb)),
        pltpu.SemaphoreType.DMA((10, nb)),
        pltpu.SemaphoreType.REGULAR,
    ]


class Ring:
    def __init__(self, blocks, narrow, scratch):
        self.blocks, self.narrow = blocks, narrow
        (
            self.lt, self.s, self.other, self.crecv, self.p1, self.m1, self.p2, self.m2, self.t,
            self.q1, self.r1, self.q2, self.r2, self.u, self.zrecv, self.ssem, self.rsem, self.credit,
        ) = scratch
        dp = lax.axis_index("dp")
        core = dp % 2
        x, y, zh = (dp // 2) % 4, (dp // 8) % 4, dp // 32
        self.core, self.zh = core, zh
        a = jnp.where(core == 0, x, y)
        b = jnp.where(core == 0, y, x)
        self.a, self.b = a, b

        def device(na, nb):
            nx = jnp.where(core == 0, na, nb)
            ny = jnp.where(core == 0, nb, na)
            return ((zh * 4 + ny) * 4 + nx) * 2 + core

        self.ap, self.am, self.a2 = (a + 1) % 4, (a + 3) % 4, (a + 2) % 4
        self.bp, self.bm, self.b2 = (b + 1) % 4, (b + 3) % 4, (b + 2) % 4
        self.to_ap, self.to_am = device(self.ap, b), device(self.am, b)
        self.to_bp, self.to_bm = device(a, self.bp), device(a, self.bm)
        self.to_a2, self.to_b2 = device(self.a2, b), device(a, self.b2)
        self.partner = dp + 1 - 2 * core
        self.across = dp + 32 - 64 * zh
        barrier = pltpu.get_barrier_semaphore()
        everyone = (
            self.partner, self.to_ap, self.to_am, self.to_bp, self.to_bm, self.to_a2, self.to_b2, self.across,
        )
        for d in everyone:
            pl.semaphore_signal(barrier, inc=1, device_id={"dp": d}, device_id_type=MESH)
        self.barrier = barrier

    def enter(self):
        pl.semaphore_wait(self.barrier, 8)

    def copies(self, stage, i, wide):
        def copy(kind, src, dst, d):
            if not wide:
                lanes = (slice(None),) * (len(src.shape) - 1) + (pl.ds(0, 128),)
                src, dst = src.at[lanes], dst.at[lanes]
            return pltpu.make_async_remote_copy(
                src_ref=src,
                dst_ref=dst,
                send_sem=self.ssem.at[kind, i],
                recv_sem=self.rsem.at[kind, i],
                device_id={"dp": d},
                device_id_type=MESH,
            )

        k = i % SLOTS
        if stage == 0:
            return [copy(0, self.other.at[i % 2], self.crecv.at[k], self.partner)]
        if stage == 1:
            return [
                copy(1, self.s.at[k, self.a2, pl.ds(0, 64)], self.p1.at[i], self.to_ap),
                copy(2, self.s.at[k, self.a2, pl.ds(64, 64)], self.m1.at[i], self.to_am),
            ]
        if stage == 2:
            return [
                copy(3, self.s.at[k, self.ap], self.p2.at[i], self.to_ap),
                copy(4, self.s.at[k, self.am], self.m2.at[i], self.to_am),
            ]
        if stage == 3:
            return [
                copy(5, self.t.at[k, self.b2, pl.ds(0, 16)], self.q1.at[i], self.to_bp),
                copy(6, self.t.at[k, self.b2, pl.ds(16, 16)], self.r1.at[i], self.to_bm),
            ]
        if stage == 4:
            return [
                copy(7, self.t.at[k, self.bp], self.q2.at[i], self.to_bp),
                copy(8, self.t.at[k, self.bm], self.r2.at[i], self.to_bm),
            ]
        return [copy(9, self.u.at[k, 1 - self.zh], self.zrecv.at[i], self.across)]

    def each(self, stage, i, act):
        few = functools.reduce(jnp.logical_or, [i == n for n in self.narrow])
        for wide in (True, False):
            @pl.when(few != wide)
            def _(wide=wide):
                for c in self.copies(stage, i, wide):
                    act(c)

    def start(self, stage, i):
        self.each(stage, i, lambda c: c.start())

    def wait(self, stage, i):
        self.each(stage, i, lambda c: c.wait())

    @staticmethod
    def slabs(part):
        for k in range(8):
            yx, c = k // 2, k % 2
            half, row = part // 4, part % 4
            first, second = (yx, row) if c == 0 else (row, yx)
            yield c, first, (second * 2 + half) * 16, k * 16

    def turn(self, left):
        for part in range(8):
            flipped = left[:, part * 128 : (part + 1) * 128].T
            for c, first, at, row in self.slabs(part):
                self.lt[c, first * 128 + at : first * 128 + at + 16, :] = flipped[row : row + 16, :]

    def make_product(self, i, right):
        own = dot(self.lt[self.core], right)
        away = dot(self.lt[1 - self.core], right)
        for chunk in range(4):
            self.s[i % SLOTS, chunk] = own[chunk * 128 : (chunk + 1) * 128]
            self.other[i % 2, chunk] = away[chunk * 128 : (chunk + 1) * 128]

    def make_small(self, i, small):
        k = i % SLOTS
        for part in range(8):
            flipped = small[:, part * 128 : (part + 1) * 128].T
            for c, first, at, row in self.slabs(part):
                @pl.when(self.core == c)
                def _(first=first, at=at, row=row, flipped=flipped):
                    self.s[k, first, at : at + 16, :128] = flipped[row : row + 16, :]

                @pl.when(self.core != c)
                def _(first=first, at=at, row=row, flipped=flipped):
                    self.other[i % 2, first, at : at + 16, :128] = flipped[row : row + 16, :]

    def sent(self, i):
        @pl.when(i >= SLOTS)
        def _():
            pl.semaphore_wait(self.credit, 1)

        self.start(0, i)

    def join_cores(self, i):
        self.wait(0, i)
        k = i % SLOTS
        for chunk in range(4):
            self.s[k, chunk] = self.s[k, chunk] + self.crecv[k, chunk]

        @pl.when(i + SLOTS < self.blocks)
        def _():
            pl.semaphore_signal(
                self.credit, inc=1, device_id={"dp": self.partner}, device_id_type=MESH
            )

        self.start(1, i)

    def first_ring(self, i):
        self.wait(1, i)
        s, k = self.s, i % SLOTS
        s[k, self.ap, :64] = s[k, self.ap, :64] + self.p1[i]
        s[k, self.am, 64:] = s[k, self.am, 64:] + self.m1[i]
        self.start(2, i)

    def first_done(self, i):
        self.wait(2, i)
        k = i % SLOTS
        for chunk in range(4):
            rows = pl.ds(chunk * 32, 32)
            self.t[k, chunk] = self.s[k, self.a, rows] + self.p2[i, rows] + self.m2[i, rows]
        self.start(3, i)

    def second_ring(self, i):
        self.wait(3, i)
        t, k = self.t, i % SLOTS
        t[k, self.bp, :16] = t[k, self.bp, :16] + self.q1[i]
        t[k, self.bm, 16:] = t[k, self.bm, 16:] + self.r1[i]
        self.start(4, i)

    def second_done(self, i):
        self.wait(4, i)
        k = i % SLOTS
        for chunk in range(2):
            rows = pl.ds(chunk * 16, 16)
            self.u[k, chunk] = self.t[k, self.b, rows] + self.q2[i, rows] + self.r2[i, rows]
        self.start(5, i)

    def share(self, i):
        self.wait(5, i)
        return self.u[i % SLOTS, self.zh] + self.zrecv[i]

    def run(self, make, finish, extra):
        def made(i):
            make(i)
            self.sent(i)

        stages = (
            made, self.join_cores, self.first_ring, self.first_done, self.second_ring, self.second_done,
            lambda i: finish(i, self.share(i)),
        )

        def step(j, carry):
            for stage, offset in zip(stages, OFFSETS):
                i = j - offset

                @pl.when((i >= 0) & (i < self.blocks))
                def _(stage=stage, i=i):
                    stage(i)

            extra(j)
            return carry

        lax.fori_loop(0, self.blocks + OFFSETS[-1], step, 0)


def cols_of(i, first):
    return pl.ds(pl.multiple_of((i - first) * W, W), W)


def at_step(cond):
    def wrap(f):
        pl.when(cond)(f)

    return wrap


def back_kernel(
    slopes, n2_ref, cot_ref, branch_ref, n1_ref, lse_ref, vec_two, up_sums, gain_ref,
    act_any, gh_any, att_any, q_any, k_any, v_any, wout_any, woth_any, wqkv_any, tokens_any, grad_any,
    down_out, up_out, out_out, qkv_out, vec_out, vec_late, sum_out, token_ref,
    distance, rbuf, q_v, k_v, v_v, wout, woth, wqkv, tokens, grad, ga, dq, dk, dv, small, every,
    rsems, lsem, gs, gr, *ring_refs,
):
    early = ((q_any, q_v), (k_any, k_v), (v_any, v_v), (wout_any, wout), (woth_any, woth))
    late = ((wqkv_any, wqkv), (tokens_any, tokens), (grad_any, grad))
    local = [
        pltpu.make_async_copy(src, dst, lsem.at[k]) for k, (src, dst) in enumerate(early + late)
    ]

    def right(kind, n):
        src = (act_any, gh_any)[kind]
        return pltpu.make_async_copy(src.at[:, cols_of(n, 4 * kind)], rbuf.at[n % 2], rsems.at[n % 2])

    right(0, 0).start()
    for c in local:
        c.start()
    att_copy = pltpu.make_async_copy(att_any.at[0], ga.at[0], rsems.at[2])
    ring = Ring(14, (4, 9), ring_refs)
    fill_distance(distance)
    ring.turn(cot_ref)
    ring.enter()
    core, a, b, zh = ring.core, ring.a, ring.b, ring.zh
    parts = (dq, dk, dv)

    def make(i):
        for first, left in ((5, n2_ref), (10, branch_ref), (11, n1_ref)):
            @pl.when(i == first)
            def _(left=left):
                ring.turn(left)

        for kind in range(2):
            first = 5 * kind

            @pl.when((i >= first) & (i < first + 4))
            def _(kind=kind):
                n = i - kind

                @pl.when(n < 3 + 4 * kind)
                def _():
                    right(kind, n + 1).start()

                if kind == 0:
                    @pl.when(n == 3)
                    def _():
                        right(1, n + 1).start()

                right(kind, n).wait()
                ring.make_product(i, rbuf[n % 2])

        @pl.when(i == 4)
        def _():
            small[...] = jnp.zeros_like(small)
            small[0:8, :] = vec_two[...]
            small[10:12, :] = up_sums[...]
            small[12:13, :512] = jnp.sum(dq[0].astype(f32), axis=0, keepdims=True)
            small[12:13, 512:] = jnp.sum(dv[0].astype(f32), axis=0, keepdims=True)

        @pl.when((i == 4) | (i == 9))
        def _():
            ring.make_small(i, small)

        @pl.when(i == 10)
        def _():
            att_copy.wait()
            ring.make_product(i, ga[0])

        for k in range(3):
            @pl.when(i == 11 + k)
            def _(k=k):
                ring.make_product(i, parts[k][0])

    def finish(i, share):
        for first, target in ((0, down_out), (5, up_out)):
            @pl.when((i >= first) & (i < first + 4))
            def _(first=first, target=target):
                target[:, cols_of(i, first)] = share

        @pl.when(i == 4)
        def _():
            vec_out[...] = share[:, :128]

        @pl.when(i == 9)
        def _():
            vec_late[...] = share[:, :128]

        @pl.when(i == 10)
        def _():
            out_out[...] = share

        @pl.when(i >= 11)
        def _():
            qkv_out[i - 11] = share

    def spread(number):
        mine = every.at[core]
        if number == 0:
            moves = [(0, mine.at[a, b, zh], ring.across)]
        elif number == 1:
            targets = (ring.to_bp, ring.to_bm, ring.to_b2)
            moves = [(k + 1, mine.at[a, b], d) for k, d in enumerate(targets)]
        elif number == 2:
            targets = (ring.to_ap, ring.to_am, ring.to_a2)
            moves = [(k + 4, mine.at[a], d) for k, d in enumerate(targets)]
        else:
            moves = [(7, mine, ring.partner)]
        return [
            pltpu.make_async_remote_copy(
                src_ref=place,
                dst_ref=place,
                send_sem=gs.at[k],
                recv_sem=gr.at[k],
                device_id={"dp": d},
                device_id_type=MESH,
            )
            for k, place, d in moves
        ]

    def spread_step(number):
        if number == 0:
            every[core, a, b, zh] = vec_out[...]
        else:
            for c in spread(number - 1):
                c.wait()
        if number < 4:
            for c in spread(number):
                c.start()
        else:
            for part in range(8):
                rows = [None] * 8
                for c, first, at, row in ring.slabs(part):
                    rows[row // 16] = every[c, first, at // 32, (at // 16) % 2]
                flipped = jnp.concatenate(rows, axis=0).T
                sum_out[:, part * 128 : (part + 1) * 128] = flipped[8:16]

    def extra(j):
        @pl.when(j == 0)
        def _():
            for c in local[:5]:
                c.wait()
            ga[0] = dot(branch_ref[...], wout[...], NT).astype(bf16)
            ga[1] = dot(branch_ref[...], woth[3], NT).astype(bf16)

        def one_pair(pair, carry):
            half, p = pair // 4, pair % 4
            lanes = pl.ds(pl.multiple_of(p * 128, 128), 128)
            lane = lax.broadcasted_iota(jnp.int32, lse_ref.shape, 1)
            lses = [
                jnp.sum(jnp.where(lane == 2 * pair + side, lse_ref[...], 0.0), axis=1, keepdims=True)
                for side in range(2)
            ]
            one, two, three = attend_back_pair(
                q_v[half, :, lanes],
                k_v[half, :, lanes],
                v_v[half, :, lanes],
                lses,
                ga[half, :, lanes],
                (slopes[2 * pair], slopes[2 * pair + 1]),
                distance,
            )
            dq[half, :, lanes] = one
            dk[half, :, lanes] = two
            dv[half, :, lanes] = three
            return carry

        @pl.when((j >= 1) & (j < 5))
        def _():
            lax.fori_loop(2 * j - 2, 2 * j, one_pair, 0)

        @pl.when(j == 4)
        def _():
            att_copy.start()

        for k in range(3):
            @pl.when(j == 5 + k)
            def _(k=k):
                if k == 0:
                    for c in local[5:]:
                        c.wait()
                one = dot(parts[k][0], wqkv[k], NT)
                two = dot(parts[k][1], woth[k])
                if k == 0:
                    token_ref[...] = one + two
                else:
                    token_ref[...] += one + two

        @pl.when(j == 8)
        def _():
            def rows_of(r, carry):
                rows = pl.ds(pl.multiple_of(r * 64, 64), 64)
                n, root = layer_norm_parts(tokens[rows, :].astype(f32))
                back, ggain, gshift = layer_norm_back(token_ref[rows, :], n, root, gain_ref[0:1, :])
                token_ref[rows, :] = grad[rows, :] + back
                small[8:9, :] += ggain[None]
                small[9:10, :] += gshift[None]
                return carry

            lax.fori_loop(0, 8, rows_of, 0)

        for number in range(5):
            @pl.when(j == 11 + number)
            def _(number=number):
                spread_step(number)

    ring.run(make, finish, extra)


def backward(slopes, n2, cot, branch, n1, lse, vec, up_sums, gain, act, gh, att, q, k, v, wout, woth, wqkv, tokens, grad):
    length, width = n1.shape
    vmem = pl.BlockSpec(memory_space=pltpu.VMEM)
    hbm = pl.BlockSpec(memory_space=pl.ANY)
    return pl.pallas_call(
        back_kernel,
        in_specs=[pl.BlockSpec(memory_space=pltpu.SMEM)] + [vmem] * 8 + [hbm] * 11,
        out_specs=[vmem] * 8,
        out_shape=[
            jax.ShapeDtypeStruct((16, 2048), f32),
            jax.ShapeDtypeStruct((16, 2048), f32),
            jax.ShapeDtypeStruct((16, 512), f32),
            jax.ShapeDtypeStruct((3, 16, 512), f32),
            jax.ShapeDtypeStruct((16, 128), f32),
            jax.ShapeDtypeStruct((16, 128), f32),
            jax.ShapeDtypeStruct((8, 1024), f32),
            jax.ShapeDtypeStruct((length, width), f32),
        ],
        scratch_shapes=[
            pltpu.VMEM((length, length), f32),
            pltpu.VMEM((2, length, W), bf16),
            pltpu.VMEM(q.shape, bf16),
            pltpu.VMEM(q.shape, bf16),
            pltpu.VMEM(q.shape, bf16),
            pltpu.VMEM(wout.shape, bf16),
            pltpu.VMEM(woth.shape, bf16),
            pltpu.VMEM(wqkv.shape, bf16),
            pltpu.VMEM(tokens.shape, bf16),
            pltpu.VMEM(grad.shape, f32),
            pltpu.VMEM(q.shape, bf16),
            pltpu.VMEM(q.shape, bf16),
            pltpu.VMEM(q.shape, bf16),
            pltpu.VMEM(q.shape, bf16),
            pltpu.VMEM((128, width), f32),
            pltpu.VMEM((2, 4, 4, 2, 16, 128), f32),
            pltpu.SemaphoreType.DMA((3,)),
            pltpu.SemaphoreType.DMA((8,)),
            pltpu.SemaphoreType.DMA((8,)),
            pltpu.SemaphoreType.DMA((8,)),
            *ring_scratch(14),
        ],
        compiler_params=pltpu.CompilerParams(
            collective_id=0, has_side_effects=True, vmem_limit_bytes=63 * 2**20
        ),
    )(slopes, n2, cot, branch, n1, lse, vec, up_sums, gain, act, gh, att, q, k, v, wout, woth, wqkv, tokens, grad)


def on_device(
    tokens,
    gain_one,
    shift_one,
    qkv_weight,
    qv_bias,
    out_weight,
    out_bias,
    gain_two,
    shift_two,
    up_weight,
    up_bias,
    down_weight,
    down_bias,
    cotangent,
):
    dp, tensor = lax.axis_index("dp"), lax.axis_index("tensor")
    core, x, y = dp % 2, (dp // 2) % 4, (dp // 8) % 4
    ring = jnp.where(core == 0, x, y)
    ring_other = jnp.where(core == 0, y, x)
    offsets = (0, 3, 1, 2)
    other_ids = [4 * core + (ring + o) % 4 for o in offsets]
    other_ids += [4 * (1 - core) + (ring_other + o) % 4 for o in offsets]

    own_heads = tensor * 8 + jnp.arange(8, dtype=jnp.int32)
    oth_heads = (1 - tensor) * 8 + jnp.stack(other_ids).astype(jnp.int32)
    slopes = jnp.exp2(-8.0 * (jnp.concatenate([own_heads, oth_heads]) + 1).astype(f32) / 16)
    rows = jnp.concatenate([gain_one, shift_one, gain_two, shift_two]).reshape(4, 1024)
    low_rows = jnp.concatenate(
        [out_bias, down_bias, up_bias, qv_bias[0], qv_bias[1], jnp.zeros((3072,), bf16)]
    ).reshape(8, 1024)
    wqkv = qkv_weight.transpose(1, 0, 2)
    (
        normed_one,
        queries,
        key_rows,
        values,
        attended,
        lse,
        woth,
        _,
        normed_two,
        active_own,
        gh_own,
        grad_up_bias,
        block_out,
        grad_middle,
        grad_branch,
        sums_two,
    ) = forward(
        slopes,
        tokens,
        rows,
        low_rows,
        wqkv,
        out_weight,
        up_weight,
        down_weight,
        cotangent,
    )
    share_down, share_up, share_out, share_qkv, vector, late, summed, token_grad = backward(
        slopes,
        normed_two,
        cotangent,
        grad_branch,
        normed_one,
        lse,
        sums_two,
        grad_up_bias,
        rows,
        active_own,
        gh_own,
        attended,
        queries,
        key_rows,
        values,
        out_weight,
        woth,
        wqkv,
        tokens,
        grad_middle,
    )
    return (
        block_out,
        token_grad,
        late[:, 8],
        late[:, 9],
        share_qkv.transpose(1, 0, 2),
        summed[4].reshape(2, 512),
        share_out.T,
        vector[:, 2],
        vector[:, 0],
        vector[:, 1],
        share_up,
        summed[2:4].reshape(2048),
        share_down.T,
        vector[:, 3],
    )


def solution(mesh):
    placed = (
        P("dp", None),
        P(),
        P(),
        P(None, None, "tensor"),
        P(None, "tensor"),
        P("tensor", None),
        P(),
        P(),
        P(),
        P(None, "tensor"),
        P("tensor"),
        P("tensor", None),
        P(),
        P("dp", None),
    )
    return jax.shard_map(
        on_device,
        mesh=mesh,
        in_specs=placed,
        out_specs=(
            P("dp", None),
            P("dp", None),
            P("dp"),
            P("dp"),
            P("dp", None, "tensor"),
            P(None, "tensor"),
            P("tensor", "dp"),
            P("dp"),
            P("dp"),
            P("dp"),
            P("dp", "tensor"),
            P("tensor"),
            P("tensor", "dp"),
            P("dp"),
        ),
        check_vma=False,
    )
```

```python
import functools
import math

import jax
import jax.numpy as jnp
from jax import lax
from jax.experimental import pallas as pl
from jax.experimental.pallas import tpu as pltpu
from jax.sharding import PartitionSpec as P

DH = 64
epsilon = 1e-05
bf16 = jnp.bfloat16
f32 = jnp.float32


def layer_norm_parts(values):
    centre = jnp.mean(values, axis=-1, keepdims=True)
    centered = values - centre
    spread = jnp.mean(centered * centered, axis=-1, keepdims=True)
    r = lax.rsqrt(spread + epsilon)
    return centered * r, r


def layer_norm_back(grad, n, r, gain):
    e = grad * gain
    mean_e = jnp.mean(e, axis=-1, keepdims=True)
    mean_en = jnp.mean(e * n, axis=-1, keepdims=True)
    return (
        r * (e - mean_e - n * mean_en),
        jnp.sum(grad * n, axis=0),
        jnp.sum(grad, axis=0),
    )


GC, GA = 0.7978845608028654, 0.044715


def gelu_both(v):
    square = v * v
    h = 0.5 + 0.5 * jnp.tanh(v * (GC + GC * GA * square))
    value = v * h
    slope = h + (value * (1.0 - h)) * (2.0 * GC + 6.0 * GC * GA * square)
    return value, slope


NT = (((1,), (1,)), ((), ()))
TN = (((0,), (0,)), ((), ()))
NN = (((1,), (0,)), ((), ()))


def dot(a, b, dims=NN):
    return lax.dot_general(a, b, dims, preferred_element_type=f32)


def half_lanes(block, side):
    lane = lax.broadcasted_iota(jnp.int32, block.shape, 1)
    return jnp.where((lane >= 64) == (side == 1), block, jnp.zeros_like(block))


def fill_distance(ref):
    row = lax.broadcasted_iota(jnp.int32, ref.shape, 0)
    col = lax.broadcasted_iota(jnp.int32, ref.shape, 1)
    ref[...] = jnp.where(row >= col, (row - col).astype(f32), 1e30)


def attend_pair(q, k, v, slopes, distance):
    outs, lses = [], []
    scaled = q * 0.125
    for side in range(2):
        out, lse = [], []
        for rows, keys in ((slice(0, 256), 256), (slice(256, 512), 512)):
            s = dot(half_lanes(scaled[rows], side), k[:keys], NT) - slopes[side] * distance[rows, :keys]
            top = jnp.max(s, axis=-1, keepdims=True)
            e = jnp.exp(s - top)
            total = jnp.sum(e, axis=-1, keepdims=True)
            out.append(dot((e * (1.0 / total)).astype(bf16), v[:keys]))
            lse.append(top + jnp.log(total))
        outs.append(jnp.concatenate(out, axis=0))
        lses.append(jnp.concatenate(lse, axis=0))
    lane = lax.broadcasted_iota(jnp.int32, outs[0].shape, 1)
    return jnp.where(lane < 64, outs[0], outs[1]).astype(bf16), lses


def attend_back_pair(q, k, v, lse, g, slopes, distance):
    dqs, dks, dvs = [], [], []
    scaled = q * 0.125
    for side in range(2):
        dq, dk, dv = [], [], []
        for rows, keys in ((slice(0, 256), 256), (slice(256, 512), 512)):
            s = dot(half_lanes(scaled[rows], side), k[:keys], NT) - slopes[side] * distance[rows, :keys]
            a = jnp.exp(s - lse[side][rows])
            w = dot(half_lanes(g[rows], side), v[:keys], NT)
            inner = jnp.sum(a * w, axis=-1, keepdims=True)
            ds = (a * (w - inner)).astype(bf16)
            dv.append(dot(a.astype(bf16), g[rows], TN))
            dq.append(dot(ds, k[:keys]) * 0.125)
            dk.append(dot(ds, q[rows], TN) * 0.125)
        dqs.append(jnp.concatenate(dq, axis=0))
        for parts, total in ((dk, dks), (dv, dvs)):
            total.append(jnp.concatenate([parts[0] + parts[1][:256], parts[1][256:]], axis=0))
    lane = lax.broadcasted_iota(jnp.int32, dqs[0].shape, 1)
    return [jnp.where(lane < 64, p[0], p[1]).astype(bf16) for p in (dqs, dks, dvs)]


def unit_block(n2, cot, up, up_dims, bias, down):
    value, slope = gelu_both(dot(n2, up, up_dims) + bias)
    active = value.astype(bf16)
    gh = (dot(cot, down, NT) * slope).astype(bf16)
    back_dims = NT if up_dims is NN else NN
    return active, gh, dot(active, down), dot(gh, up, back_dims)


MESH = pl.DeviceIdType.MESH


def forward_kernel(
    slopes,
    tokens,
    rows_ref,
    low_rows,
    wqkv,
    wout,
    up_any,
    down_any,
    cot_any,
    n1_out,
    q_out,
    k_out,
    v_out,
    att_out,
    lse_ref,
    woth_out,
    units_any,
    n2_out,
    act_out,
    gh_out,
    gb_ref,
    out_ref,
    grad_ref,
    branch_ref,
    vec_ref,
    n1_ref,
    q_ref,
    k_ref,
    v_ref,
    att_ref,
    woth_ref,
    n2_ref,
    act_ref,
    gh_ref,
    bias_rows,
    bias_piece,
    piece,
    turned,
    distance,
    got,
    got_bias,
    bias_out,
    up,
    down,
    cot,
    feed_ref,
    gn_ref,
    hsend,
    hrecv,
    usend,
    urecv,
    bsend,
    brecv,
    lsem,
    fsem,
    osem,
):
    dp, tensor = lax.axis_index("dp"), lax.axis_index("tensor")
    core, x, y, zh = dp % 2, (dp // 2) % 4, (dp // 8) % 4, dp // 32
    z = zh * 2 + tensor
    ring = jnp.where(core == 0, x, y)

    def device(nx, ny, nz, nc):
        return ((((nz // 2) * 4 + ny) * 4 + nx) * 2 + nc, nz % 2)

    def on_ring(r):
        return device(jnp.where(core == 0, r, x), jnp.where(core == 0, y, r), z, core)

    z_plus, z_minus = device(x, y, (z + 1) % 4, core), device(x, y, (z + 3) % 4, core)
    r_plus, r_minus = on_ring((ring + 1) % 4), on_ring((ring + 3) % 4)
    partner = device(x, y, z, 1 - core)
    barrier = pltpu.get_barrier_semaphore()
    for d in (z_plus, z_minus, r_plus, r_minus, partner):
        pl.semaphore_signal(barrier, inc=1, device_id=d, device_id_type=MESH)
    local = [
        pltpu.make_async_copy(a, b, lsem.at[k])
        for k, (a, b) in enumerate(((up_any, up), (down_any, down), (cot_any, cot)))
    ]
    for c in local:
        c.start()
    pid, fid = 4 * core + ring, 4 * core + (ring + 2) % 4
    for m in range(3):
        turned[...] = wqkv[m, :, pl.ds(pl.multiple_of(pid // 2 * 128, 128), 128)].T
        side = pl.ds(pl.multiple_of(pid % 2 * 64, 64), 64)
        piece[0, m * 64 : m * 64 + 64, :] = turned[side, :].astype(f32)
    piece[0, 192:256, :] = wout[pl.ds(pl.multiple_of(pid * 64, 64), 64), :].astype(f32)
    bias_rows[...] = low_rows[...].astype(f32)
    for p in range(8):
        q_part = bias_rows[4:5, 64 * p : 64 * p + 64]
        v_part = bias_rows[4:5, 512 + 64 * p : 576 + 64 * p]
        bias_piece[p : p + 1, :] = jnp.concatenate([q_part, q_part, v_part, v_part], axis=1)
        bias_piece[8 + p : 9 + p, :] = bias_rows[2 + p // 4 : 3 + p // 4, p % 4 * 256 : p % 4 * 256 + 256]
    pl.semaphore_wait(barrier, 5)

    def place(u, slot, sub):
        at = pl.ds(sub * 64, 64)
        return got.at[slot, at] if u == 0 else units_any.at[u - 1, slot, at]

    def move(u, src, slot, sub, way, target):
        send = hsend.at[slot, sub, way] if u == 0 else usend.at[u - 1, slot, sub, way]
        recv = hrecv.at[slot, sub] if u == 0 else urecv.at[u - 1, slot, sub]
        return pltpu.make_async_remote_copy(
            src_ref=src,
            dst_ref=place(u, slot, sub),
            send_sem=send,
            recv_sem=recv,
            device_id=target,
            device_id_type=MESH,
        )

    started = [[], [], []]

    def begin(u, src, slot, sub, target):
        c = move(u, src, slot, sub, 0, target)
        c.start()
        started[u].append(c)

    def arrived(u, slot, sub):
        move(u, place(u, slot, sub), slot, sub, 0, partner).wait_recv()

    bias_move = pltpu.make_async_remote_copy(
        src_ref=bias_piece, dst_ref=got_bias, send_sem=bsend, recv_sem=brecv, device_id=z_plus, device_id_type=MESH
    )
    outgoing = []

    def leave(k, src, dst):
        c = pltpu.make_async_copy(src, dst, osem.at[k])
        c.start()
        outgoing.append(c)

    def to_z(u, src, slot):
        for sub in (0, 2, 1, 3):
            begin(u, piece.at[src, pl.ds(sub * 64, 64)], slot, sub, z_plus if sub < 2 else z_minus)

    to_z(0, 0, 0)
    bias_move.start()
    fill_distance(distance)

    def own_came(u, subs):
        for sub in subs:
            arrived(u, 0, sub)
            begin(u, place(u, 0, sub), 1, sub, r_plus)
            begin(u, place(u, 0, sub), 2, sub, r_minus)
        for sub in subs:
            begin(u, place(u, 0, sub), 4, sub, partner)

    def next_came(u, low, high):
        arrived(u, 1, low)
        if low < 2 and u < 2:
            begin(u, place(u, 1, low), 3, low, r_plus)
        begin(u, place(u, 1, low), 5, low, partner)
        arrived(u, 2, high)
        if high >= 2 and u < 2:
            begin(u, place(u, 2, high), 3, high, r_minus)
        begin(u, place(u, 2, high), 6, high, partner)

    def far_came(u, subs):
        for sub in subs:
            arrived(u, 3, sub)
            begin(u, place(u, 3, sub), 7, sub, partner)

    def swapped(u, slots):
        for slot in slots:
            for sub in range(4):
                arrived(u, slot, sub)

    pump = [lambda u=u, f=f: f(u) for u in range(3) for f in (
        lambda u: own_came(u, (0, 2)),
        lambda u: own_came(u, (1, 3)),
        lambda u: next_came(u, 0, 2),
        lambda u: next_came(u, 2, 0),
        lambda u: next_came(u, 1, 3),
        lambda u: next_came(u, 3, 1),
        lambda u: far_came(u, (0, 2)),
        lambda u: far_came(u, (1, 3)),
        lambda u: swapped(u, range(4, 8) if u < 2 else (4, 5, 6)),
    )]

    def norm_one(r, carry):
        at = pl.ds(r * 128, 128)
        n, _ = layer_norm_parts(tokens[at, :].astype(f32))
        n1_ref[at, :] = (n * rows_ref[0:1, :] + rows_ref[1:2, :]).astype(bf16)
        return carry

    lax.fori_loop(0, 4, norm_one, 0)
    n1 = n1_ref[...]
    q_ref[0] = (dot(n1, wqkv[0]) + bias_rows[4:5, :512]).astype(bf16)
    k_ref[0] = dot(n1, wqkv[1]).astype(bf16)
    v_ref[0] = (dot(n1, wqkv[2]) + bias_rows[4:5, 512:]).astype(bf16)
    leave(0, n1_ref, n1_out)
    for c in local:
        c.wait()
    piece[1] = up[:, pl.ds(pl.multiple_of(pid * 256, 256), 256)].T.astype(f32)
    piece[2] = down[pl.ds(pl.multiple_of(pid * 256, 256), 256), :].astype(f32)
    piece[3] = down[pl.ds(pl.multiple_of(fid * 256, 256), 256), :].astype(f32)
    to_z(1, 1, 0)
    to_z(2, 2, 0)
    to_z(2, 3, 3)

    lse_ref[...] = jnp.zeros_like(lse_ref)

    def put_lse(head, pair):
        lane = lax.broadcasted_iota(jnp.int32, lse_ref.shape, 1)
        for side in range(2):
            lse_ref[...] = jnp.where(lane == head + side, pair[side], lse_ref[...])

    def own_pair(p, carry):
        lanes = pl.ds(pl.multiple_of(p * 128, 128), 128)
        out, lse = attend_pair(
            q_ref[0, :, lanes], k_ref[0, :, lanes], v_ref[0, :, lanes], (slopes[2 * p], slopes[2 * p + 1]), distance
        )
        att_ref[0, :, lanes] = out
        put_lse(2 * p, lse)
        return carry

    lax.fori_loop(0, 1, own_pair, 0)
    pump[0]()
    lax.fori_loop(1, 4, own_pair, 0)
    pump[1]()
    pump[2]()
    feed_ref[...] = dot(att_ref[0], wout[...])
    for k in range(3, 6):
        pump[k]()
    bias_move.wait()
    ring_other = jnp.where(core == 0, y, x)
    for k, o in enumerate((0, 3, 1, 2)):
        for slot, pid in ((k, 4 * core + (ring + o) % 4), (k + 4, 4 * (1 - core) + (ring_other + o) % 4)):
            bias_out[slot : slot + 1, :] = got_bias[pl.ds(pid, 1), :]
            bias_out[8 + slot : 9 + slot, :] = got_bias[pl.ds(8 + pid, 1), :]

    def other_pair(p, carry):
        lanes = pl.ds(pl.multiple_of(p * 128, 128), 128)
        for m in range(4):
            for side in range(2):
                at = pl.ds(pl.multiple_of(p * 128 + side * 64, 64), 64)
                woth_ref[m, at, :] = got[2 * p + side, m * 64 : m * 64 + 64, :].astype(bf16)
        low, high = bias_out[pl.ds(2 * p, 1), :], bias_out[pl.ds(2 * p + 1, 1), :]
        parts = []
        for m in range(3):
            parts.append(dot(n1_ref[...], woth_ref[m, lanes, :], NT))
        lane = lax.broadcasted_iota(jnp.int32, (1, 128), 1)
        q = (parts[0] + jnp.where(lane < 64, low[:, :128], high[:, :128])).astype(bf16)
        k = parts[1].astype(bf16)
        v = (parts[2] + jnp.where(lane < 64, low[:, 128:], high[:, 128:])).astype(bf16)
        q_ref[1, :, lanes] = q
        k_ref[1, :, lanes] = k
        v_ref[1, :, lanes] = v
        out, lse = attend_pair(q, k, v, (slopes[8 + 2 * p], slopes[9 + 2 * p]), distance)
        att_ref[1, :, lanes] = out
        put_lse(8 + 2 * p, lse)
        return carry

    lax.fori_loop(0, 1, other_pair, 0)
    for k in (9, 6, 7, 8, 10):
        pump[k]()
    lax.fori_loop(1, 4, other_pair, 0)
    pump[11]()
    feed_ref[...] += dot(att_ref[1], woth_ref[3])
    pump[12]()

    def norm_two(r, carry):
        at = pl.ds(r * 128, 128)
        middle = tokens[at, :].astype(f32) + (feed_ref[at, :] + bias_rows[0:1, :])
        grad_ref[at, :] = middle
        n, _ = layer_norm_parts(middle)
        n2_ref[at, :] = (n * rows_ref[2:3, :] + rows_ref[3:4, :]).astype(bf16)
        return carry

    lax.fori_loop(0, 4, norm_two, 0)
    leave(1, q_ref, q_out)
    leave(2, k_ref, k_out)
    leave(3, v_ref, v_out)
    leave(4, att_ref, att_out)
    leave(5, woth_ref, woth_out)
    leave(6, n2_ref, n2_out)
    pump[13]()
    pump[14]()
    feed_ref[...] = jnp.zeros_like(feed_ref)
    gn_ref[...] = jnp.zeros_like(gn_ref)

    def unit_step(i, carry):
        lanes = pl.ds(pl.multiple_of(i * 512, 512), 512)
        within = pl.ds(pl.multiple_of(i % 2 * 512, 512), 512)
        where = (pl.ds(2 + i // 2, 1), within)
        active, gh, feed, gn = unit_block(
            n2_ref[...], cot[...], up[:, lanes], NN, bias_rows[where], down[lanes, :]
        )
        act_ref[:, lanes] = active
        gh_ref[:, lanes] = gh
        gb_ref[pl.ds(i // 2, 1), within] = jnp.sum(gh.astype(f32), axis=0, keepdims=True)
        feed_ref[...] += feed
        gn_ref[...] += gn
        return carry

    def fetch(number, slots):
        return [
            pltpu.make_async_copy(
                units_any.at[k, slot], got.at[4 * number + 2 * k + n], fsem.at[number, 2 * k + n]
            )
            for k in range(2)
            for n, slot in enumerate(slots)
        ]

    def other_step(number, slots):
        for c in fetch(number, slots):
            c.wait()
        up_two, down_two = (
            jnp.concatenate([got[4 * number + 2 * k].astype(bf16), got[4 * number + 2 * k + 1].astype(bf16)], axis=0)
            for k in range(2)
        )
        bias = jnp.concatenate([bias_out[8 + slot : 9 + slot, :] for slot in slots], axis=1)
        _, _, feed, gn = unit_block(n2_ref[...], cot[...], up_two, NT, bias, down_two)
        feed_ref[...] += feed
        gn_ref[...] += gn

    def bring(number, slots):
        for c in fetch(number, slots):
            c.start()

    lax.fori_loop(0, 1, unit_step, 0)
    for k in (18, 15, 16):
        pump[k]()
    lax.fori_loop(1, 2, unit_step, 0)
    for k in (19, 17):
        pump[k]()
    lax.fori_loop(2, 3, unit_step, 0)
    pump[20]()
    pump[21]()
    lax.fori_loop(3, 4, unit_step, 0)
    leave(7, act_ref, act_out)
    leave(8, gh_ref, gh_out)
    for c in started[0]:
        c.wait_send()
    swapped(2, (4,))
    bring(0, (0, 4))
    pump[22]()
    pump[24]()
    pump[25]()
    swapped(2, (7,))
    bring(1, (3, 7))
    other_step(0, (0, 4))
    pump[23]()
    bring(0, (1, 2))
    other_step(1, (3, 7))
    swapped(2, (5, 6))
    bring(1, (5, 6))
    other_step(0, (1, 2))
    other_step(1, (5, 6))
    vec_ref[...] = jnp.zeros_like(vec_ref)

    def rows_of(r, carry):
        at = pl.ds(pl.multiple_of(r * 64, 64), 64)
        middle = grad_ref[at, :]
        cotangent = cot[at, :].astype(f32)
        out_ref[at, :] = (middle + (feed_ref[at, :] + bias_rows[1:2, :])).astype(bf16)
        n, root = layer_norm_parts(middle)
        back, ggain, gshift = layer_norm_back(gn_ref[at, :], n, root, rows_ref[2:3, :])
        whole = cotangent + back
        rounded = whole.astype(bf16)
        grad_ref[at, :] = whole
        branch_ref[at, :] = rounded
        vec_ref[0:1, :] += ggain[None]
        vec_ref[1:2, :] += gshift[None]
        vec_ref[2:3, :] += jnp.sum(rounded.astype(f32), axis=0, keepdims=True)
        vec_ref[3:4, :] += jnp.sum(cotangent, axis=0, keepdims=True)
        return carry

    lax.fori_loop(0, 8, rows_of, 0)
    for c in started[1] + started[2]:
        c.wait_send()
    for c in outgoing:
        c.wait()


def forward(slopes, tokens, rows, low_rows, wqkv, wout, up, down, cot):
    length, width = tokens.shape
    local, units = wout.shape[0], up.shape[1]
    vmem = pl.BlockSpec(memory_space=pltpu.VMEM)
    hbm = pl.BlockSpec(memory_space=pl.ANY)

    def out(shape, kind):
        return jax.ShapeDtypeStruct(shape, kind)

    return pl.pallas_call(
        forward_kernel,
        in_specs=[pl.BlockSpec(memory_space=pltpu.SMEM)] + [vmem] * 5 + [hbm] * 3,
        out_specs=[hbm] * 5 + [vmem] + [hbm] * 5 + [vmem] * 5,
        out_shape=[
            out((length, width), bf16),
            out((2, length, local), bf16),
            out((2, length, local), bf16),
            out((2, length, local), bf16),
            out((2, length, local), bf16),
            out((length, 128), f32),
            out((4, local, width), bf16),
            out((2, 8, 256, width), f32),
            out((length, width), bf16),
            out((length, units), bf16),
            out((length, units), bf16),
            out((2, width), f32),
            out((length, width), bf16),
            out((length, width), f32),
            out((length, width), bf16),
            out((8, width), f32),
        ],
        scratch_shapes=[
            pltpu.VMEM((length, width), bf16),
            *[pltpu.VMEM((2, length, local), bf16)] * 4,
            pltpu.VMEM((4, local, width), bf16),
            pltpu.VMEM((length, width), bf16),
            pltpu.VMEM((length, units), bf16),
            pltpu.VMEM((length, units), bf16),
            pltpu.VMEM((8, width), f32),
            pltpu.VMEM((16, 256), f32),
            pltpu.VMEM((4, 256, width), f32),
            pltpu.VMEM((128, width), bf16),
            pltpu.VMEM((length, length), f32),
            pltpu.VMEM((8, 256, width), f32),
            pltpu.VMEM((16, 256), f32),
            pltpu.VMEM((16, 256), f32),
            pltpu.VMEM((width, units), bf16),
            pltpu.VMEM((units, width), bf16),
            pltpu.VMEM((length, width), bf16),
            pltpu.VMEM((length, width), f32),
            pltpu.VMEM((length, width), f32),
            pltpu.SemaphoreType.DMA((8, 4, 1)),
            pltpu.SemaphoreType.DMA((8, 4)),
            pltpu.SemaphoreType.DMA((2, 8, 4, 1)),
            pltpu.SemaphoreType.DMA((2, 8, 4)),
            pltpu.SemaphoreType.DMA,
            pltpu.SemaphoreType.DMA,
            pltpu.SemaphoreType.DMA((3,)),
            pltpu.SemaphoreType.DMA((2, 4)),
            pltpu.SemaphoreType.DMA((9,)),
        ],
        compiler_params=pltpu.CompilerParams(
            collective_id=1, has_side_effects=True, vmem_limit_bytes=62 * 2**20
        ),
    )(slopes, tokens, rows, low_rows, wqkv, wout, up, down, cot)


W = 512
OFFSETS = (0, 1, 2, 4, 5, 6, 7)
SLOTS = 5


def ring_scratch(nb):
    return [
        pltpu.VMEM((2, 512, 512), bf16),
        pltpu.VMEM((SLOTS, 4, 128, W), f32),
        pltpu.VMEM((2, 4, 128, W), f32),
        pltpu.VMEM((SLOTS, 4, 128, W), f32),
        pltpu.VMEM((nb, 64, W), f32),
        pltpu.VMEM((nb, 64, W), f32),
        pltpu.VMEM((nb, 128, W), f32),
        pltpu.VMEM((nb, 128, W), f32),
        pltpu.VMEM((SLOTS, 4, 32, W), f32),
        pltpu.VMEM((nb, 16, W), f32),
        pltpu.VMEM((nb, 16, W), f32),
        pltpu.VMEM((nb, 32, W), f32),
        pltpu.VMEM((nb, 32, W), f32),
        pltpu.VMEM((SLOTS, 2, 16, W), f32),
        pltpu.VMEM((nb, 16, W), f32),
        pltpu.SemaphoreType.DMA((10, nb)),
        pltpu.SemaphoreType.DMA((10, nb)),
        pltpu.SemaphoreType.REGULAR,
    ]


class Ring:
    def __init__(self, blocks, narrow, scratch):
        self.blocks, self.narrow = blocks, narrow
        (
            self.lt, self.s, self.other, self.crecv, self.p1, self.m1, self.p2, self.m2, self.t,
            self.q1, self.r1, self.q2, self.r2, self.u, self.zrecv, self.ssem, self.rsem, self.credit,
        ) = scratch
        dp = lax.axis_index("dp")
        core = dp % 2
        x, y, zh = (dp // 2) % 4, (dp // 8) % 4, dp // 32
        self.core, self.zh = core, zh
        a = jnp.where(core == 0, x, y)
        b = jnp.where(core == 0, y, x)
        self.a, self.b = a, b

        def device(na, nb):
            nx = jnp.where(core == 0, na, nb)
            ny = jnp.where(core == 0, nb, na)
            return ((zh * 4 + ny) * 4 + nx) * 2 + core

        self.ap, self.am, self.a2 = (a + 1) % 4, (a + 3) % 4, (a + 2) % 4
        self.bp, self.bm, self.b2 = (b + 1) % 4, (b + 3) % 4, (b + 2) % 4
        self.to_ap, self.to_am = device(self.ap, b), device(self.am, b)
        self.to_bp, self.to_bm = device(a, self.bp), device(a, self.bm)
        self.to_a2, self.to_b2 = device(self.a2, b), device(a, self.b2)
        self.partner = dp + 1 - 2 * core
        self.across = dp + 32 - 64 * zh
        barrier = pltpu.get_barrier_semaphore()
        everyone = (
            self.partner, self.to_ap, self.to_am, self.to_bp, self.to_bm, self.to_a2, self.to_b2, self.across,
        )
        for d in everyone:
            pl.semaphore_signal(barrier, inc=1, device_id={"dp": d}, device_id_type=MESH)
        self.barrier = barrier

    def enter(self):
        pl.semaphore_wait(self.barrier, 8)

    def copies(self, stage, i, wide):
        def copy(kind, src, dst, d):
            if not wide:
                lanes = (slice(None),) * (len(src.shape) - 1) + (pl.ds(0, 128),)
                src, dst = src.at[lanes], dst.at[lanes]
            return pltpu.make_async_remote_copy(
                src_ref=src,
                dst_ref=dst,
                send_sem=self.ssem.at[kind, i],
                recv_sem=self.rsem.at[kind, i],
                device_id={"dp": d},
                device_id_type=MESH,
            )

        k = i % SLOTS
        if stage == 0:
            return [copy(0, self.other.at[i % 2], self.crecv.at[k], self.partner)]
        if stage == 1:
            return [
                copy(1, self.s.at[k, self.a2, pl.ds(0, 64)], self.p1.at[i], self.to_ap),
                copy(2, self.s.at[k, self.a2, pl.ds(64, 64)], self.m1.at[i], self.to_am),
            ]
        if stage == 2:
            return [
                copy(3, self.s.at[k, self.ap], self.p2.at[i], self.to_ap),
                copy(4, self.s.at[k, self.am], self.m2.at[i], self.to_am),
            ]
        if stage == 3:
            return [
                copy(5, self.t.at[k, self.b2, pl.ds(0, 16)], self.q1.at[i], self.to_bp),
                copy(6, self.t.at[k, self.b2, pl.ds(16, 16)], self.r1.at[i], self.to_bm),
            ]
        if stage == 4:
            return [
                copy(7, self.t.at[k, self.bp], self.q2.at[i], self.to_bp),
                copy(8, self.t.at[k, self.bm], self.r2.at[i], self.to_bm),
            ]
        return [copy(9, self.u.at[k, 1 - self.zh], self.zrecv.at[i], self.across)]

    def each(self, stage, i, act):
        few = functools.reduce(jnp.logical_or, [i == n for n in self.narrow])
        for wide in (True, False):
            @pl.when(few != wide)
            def _(wide=wide):
                for c in self.copies(stage, i, wide):
                    act(c)

    def start(self, stage, i):
        self.each(stage, i, lambda c: c.start())

    def wait(self, stage, i):
        self.each(stage, i, lambda c: c.wait())

    @staticmethod
    def slabs(part):
        for k in range(8):
            yx, c = k // 2, k % 2
            half, row = part // 4, part % 4
            first, second = (yx, row) if c == 0 else (row, yx)
            yield c, first, (second * 2 + half) * 16, k * 16

    def turn(self, left):
        for part in range(8):
            flipped = left[:, part * 128 : (part + 1) * 128].T
            for c, first, at, row in self.slabs(part):
                self.lt[c, first * 128 + at : first * 128 + at + 16, :] = flipped[row : row + 16, :]

    def make_product(self, i, right):
        own = dot(self.lt[self.core], right)
        away = dot(self.lt[1 - self.core], right)
        for chunk in range(4):
            self.s[i % SLOTS, chunk] = own[chunk * 128 : (chunk + 1) * 128]
            self.other[i % 2, chunk] = away[chunk * 128 : (chunk + 1) * 128]

    def make_small(self, i, small):
        k = i % SLOTS
        for part in range(8):
            flipped = small[:, part * 128 : (part + 1) * 128].T
            for c, first, at, row in self.slabs(part):
                @pl.when(self.core == c)
                def _(first=first, at=at, row=row, flipped=flipped):
                    self.s[k, first, at : at + 16, :128] = flipped[row : row + 16, :]

                @pl.when(self.core != c)
                def _(first=first, at=at, row=row, flipped=flipped):
                    self.other[i % 2, first, at : at + 16, :128] = flipped[row : row + 16, :]

    def sent(self, i):
        @pl.when(i >= SLOTS)
        def _():
            pl.semaphore_wait(self.credit, 1)

        self.start(0, i)

    def join_cores(self, i):
        self.wait(0, i)
        k = i % SLOTS
        for chunk in range(4):
            self.s[k, chunk] = self.s[k, chunk] + self.crecv[k, chunk]

        @pl.when(i + SLOTS < self.blocks)
        def _():
            pl.semaphore_signal(
                self.credit, inc=1, device_id={"dp": self.partner}, device_id_type=MESH
            )

        self.start(1, i)

    def first_ring(self, i):
        self.wait(1, i)
        s, k = self.s, i % SLOTS
        s[k, self.ap, :64] = s[k, self.ap, :64] + self.p1[i]
        s[k, self.am, 64:] = s[k, self.am, 64:] + self.m1[i]
        self.start(2, i)

    def first_done(self, i):
        self.wait(2, i)
        k = i % SLOTS
        for chunk in range(4):
            rows = pl.ds(chunk * 32, 32)
            self.t[k, chunk] = self.s[k, self.a, rows] + self.p2[i, rows] + self.m2[i, rows]
        self.start(3, i)

    def second_ring(self, i):
        self.wait(3, i)
        t, k = self.t, i % SLOTS
        t[k, self.bp, :16] = t[k, self.bp, :16] + self.q1[i]
        t[k, self.bm, 16:] = t[k, self.bm, 16:] + self.r1[i]
        self.start(4, i)

    def second_done(self, i):
        self.wait(4, i)
        k = i % SLOTS
        for chunk in range(2):
            rows = pl.ds(chunk * 16, 16)
            self.u[k, chunk] = self.t[k, self.b, rows] + self.q2[i, rows] + self.r2[i, rows]
        self.start(5, i)

    def share(self, i):
        self.wait(5, i)
        return self.u[i % SLOTS, self.zh] + self.zrecv[i]

    def run(self, make, finish, extra):
        def made(i):
            make(i)
            self.sent(i)

        stages = (
            made, self.join_cores, self.first_ring, self.first_done, self.second_ring, self.second_done,
            lambda i: finish(i, self.share(i)),
        )

        def step(j, carry):
            for stage, offset in zip(stages, OFFSETS):
                i = j - offset

                @pl.when((i >= 0) & (i < self.blocks))
                def _(stage=stage, i=i):
                    stage(i)

            extra(j)
            return carry

        lax.fori_loop(0, self.blocks + OFFSETS[-1], step, 0)


def cols_of(i, first):
    return pl.ds(pl.multiple_of((i - first) * W, W), W)


def at_step(cond):
    def wrap(f):
        pl.when(cond)(f)

    return wrap


def back_kernel(
    slopes, n2_ref, cot_ref, branch_ref, n1_ref, lse_ref, vec_two, up_sums, gain_ref,
    act_any, gh_any, att_any, q_any, k_any, v_any, wout_any, woth_any, wqkv_any, tokens_any, grad_any,
    down_out, up_out, out_out, qkv_out, vec_out, vec_late, sum_out, token_ref,
    distance, rbuf, q_v, k_v, v_v, wout, woth, wqkv, tokens, grad, ga, dq, dk, dv, small, every,
    rsems, lsem, gs, gr, *ring_refs,
):
    early = ((q_any, q_v), (k_any, k_v), (v_any, v_v), (wout_any, wout), (woth_any, woth))
    late = ((wqkv_any, wqkv), (tokens_any, tokens), (grad_any, grad))
    local = [
        pltpu.make_async_copy(src, dst, lsem.at[k]) for k, (src, dst) in enumerate(early + late)
    ]

    def right(kind, n):
        src = (act_any, gh_any)[kind]
        return pltpu.make_async_copy(src.at[:, cols_of(n, 4 * kind)], rbuf.at[n % 2], rsems.at[n % 2])

    right(0, 0).start()
    for c in local:
        c.start()
    att_copy = pltpu.make_async_copy(att_any.at[0], ga.at[0], rsems.at[2])
    ring = Ring(14, (4, 9), ring_refs)
    fill_distance(distance)
    ring.turn(cot_ref)
    ring.enter()
    core, a, b, zh = ring.core, ring.a, ring.b, ring.zh
    parts = (dq, dk, dv)

    def make(i):
        for first, left in ((5, n2_ref), (10, branch_ref), (11, n1_ref)):
            @pl.when(i == first)
            def _(left=left):
                ring.turn(left)

        for kind in range(2):
            first = 5 * kind

            @pl.when((i >= first) & (i < first + 4))
            def _(kind=kind):
                n = i - kind

                @pl.when(n < 3 + 4 * kind)
                def _():
                    right(kind, n + 1).start()

                if kind == 0:
                    @pl.when(n == 3)
                    def _():
                        right(1, n + 1).start()

                right(kind, n).wait()
                ring.make_product(i, rbuf[n % 2])

        @pl.when(i == 4)
        def _():
            small[...] = jnp.zeros_like(small)
            small[0:8, :] = vec_two[...]
            small[10:12, :] = up_sums[...]
            small[12:13, :512] = jnp.sum(dq[0].astype(f32), axis=0, keepdims=True)
            small[12:13, 512:] = jnp.sum(dv[0].astype(f32), axis=0, keepdims=True)

        @pl.when((i == 4) | (i == 9))
        def _():
            ring.make_small(i, small)

        @pl.when(i == 10)
        def _():
            att_copy.wait()
            ring.make_product(i, ga[0])

        for k in range(3):
            @pl.when(i == 11 + k)
            def _(k=k):
                ring.make_product(i, parts[k][0])

    def finish(i, share):
        for first, target in ((0, down_out), (5, up_out)):
            @pl.when((i >= first) & (i < first + 4))
            def _(first=first, target=target):
                target[:, cols_of(i, first)] = share

        @pl.when(i == 4)
        def _():
            vec_out[...] = share[:, :128]

        @pl.when(i == 9)
        def _():
            vec_late[...] = share[:, :128]

        @pl.when(i == 10)
        def _():
            out_out[...] = share

        @pl.when(i >= 11)
        def _():
            qkv_out[i - 11] = share

    def spread(number):
        mine = every.at[core]
        if number == 0:
            moves = [(0, mine.at[a, b, zh], ring.across)]
        elif number == 1:
            targets = (ring.to_bp, ring.to_bm, ring.to_b2)
            moves = [(k + 1, mine.at[a, b], d) for k, d in enumerate(targets)]
        elif number == 2:
            targets = (ring.to_ap, ring.to_am, ring.to_a2)
            moves = [(k + 4, mine.at[a], d) for k, d in enumerate(targets)]
        else:
            moves = [(7, mine, ring.partner)]
        return [
            pltpu.make_async_remote_copy(
                src_ref=place,
                dst_ref=place,
                send_sem=gs.at[k],
                recv_sem=gr.at[k],
                device_id={"dp": d},
                device_id_type=MESH,
            )
            for k, place, d in moves
        ]

    def spread_step(number):
        if number == 0:
            every[core, a, b, zh] = vec_out[...]
        else:
            for c in spread(number - 1):
                c.wait()
        if number < 4:
            for c in spread(number):
                c.start()
        else:
            for part in range(8):
                rows = [None] * 8
                for c, first, at, row in ring.slabs(part):
                    rows[row // 16] = every[c, first, at // 32, (at // 16) % 2]
                flipped = jnp.concatenate(rows, axis=0).T
                sum_out[:, part * 128 : (part + 1) * 128] = flipped[8:16]

    def extra(j):
        @pl.when(j == 0)
        def _():
            for c in local[:5]:
                c.wait()
            ga[0] = dot(branch_ref[...], wout[...], NT).astype(bf16)
            ga[1] = dot(branch_ref[...], woth[3], NT).astype(bf16)

        def one_pair(pair, carry):
            half, p = pair // 4, pair % 4
            lanes = pl.ds(pl.multiple_of(p * 128, 128), 128)
            lane = lax.broadcasted_iota(jnp.int32, lse_ref.shape, 1)
            lses = [
                jnp.sum(jnp.where(lane == 2 * pair + side, lse_ref[...], 0.0), axis=1, keepdims=True)
                for side in range(2)
            ]
            one, two, three = attend_back_pair(
                q_v[half, :, lanes],
                k_v[half, :, lanes],
                v_v[half, :, lanes],
                lses,
                ga[half, :, lanes],
                (slopes[2 * pair], slopes[2 * pair + 1]),
                distance,
            )
            dq[half, :, lanes] = one
            dk[half, :, lanes] = two
            dv[half, :, lanes] = three
            return carry

        @pl.when((j >= 1) & (j < 5))
        def _():
            lax.fori_loop(2 * j - 2, 2 * j, one_pair, 0)

        @pl.when(j == 4)
        def _():
            att_copy.start()

        for k in range(3):
            @pl.when(j == 5 + k)
            def _(k=k):
                if k == 0:
                    for c in local[5:]:
                        c.wait()
                one = dot(parts[k][0], wqkv[k], NT)
                two = dot(parts[k][1], woth[k])
                if k == 0:
                    token_ref[...] = one + two
                else:
                    token_ref[...] += one + two

        @pl.when(j == 8)
        def _():
            def rows_of(r, carry):
                rows = pl.ds(pl.multiple_of(r * 64, 64), 64)
                n, root = layer_norm_parts(tokens[rows, :].astype(f32))
                back, ggain, gshift = layer_norm_back(token_ref[rows, :], n, root, gain_ref[0:1, :])
                token_ref[rows, :] = grad[rows, :] + back
                small[8:9, :] += ggain[None]
                small[9:10, :] += gshift[None]
                return carry

            lax.fori_loop(0, 8, rows_of, 0)

        for number in range(5):
            @pl.when(j == 12 + number)
            def _(number=number):
                spread_step(number)

    ring.run(make, finish, extra)


def backward(slopes, n2, cot, branch, n1, lse, vec, up_sums, gain, act, gh, att, q, k, v, wout, woth, wqkv, tokens, grad):
    length, width = n1.shape
    vmem = pl.BlockSpec(memory_space=pltpu.VMEM)
    hbm = pl.BlockSpec(memory_space=pl.ANY)
    return pl.pallas_call(
        back_kernel,
        in_specs=[pl.BlockSpec(memory_space=pltpu.SMEM)] + [vmem] * 8 + [hbm] * 11,
        out_specs=[vmem] * 8,
        out_shape=[
            jax.ShapeDtypeStruct((16, 2048), f32),
            jax.ShapeDtypeStruct((16, 2048), f32),
            jax.ShapeDtypeStruct((16, 512), f32),
            jax.ShapeDtypeStruct((3, 16, 512), f32),
            jax.ShapeDtypeStruct((16, 128), f32),
            jax.ShapeDtypeStruct((16, 128), f32),
            jax.ShapeDtypeStruct((8, 1024), f32),
            jax.ShapeDtypeStruct((length, width), f32),
        ],
        scratch_shapes=[
            pltpu.VMEM((length, length), f32),
            pltpu.VMEM((2, length, W), bf16),
            pltpu.VMEM(q.shape, bf16),
            pltpu.VMEM(q.shape, bf16),
            pltpu.VMEM(q.shape, bf16),
            pltpu.VMEM(wout.shape, bf16),
            pltpu.VMEM(woth.shape, bf16),
            pltpu.VMEM(wqkv.shape, bf16),
            pltpu.VMEM(tokens.shape, bf16),
            pltpu.VMEM(grad.shape, f32),
            pltpu.VMEM(q.shape, bf16),
            pltpu.VMEM(q.shape, bf16),
            pltpu.VMEM(q.shape, bf16),
            pltpu.VMEM(q.shape, bf16),
            pltpu.VMEM((128, width), f32),
            pltpu.VMEM((2, 4, 4, 2, 16, 128), f32),
            pltpu.SemaphoreType.DMA((3,)),
            pltpu.SemaphoreType.DMA((8,)),
            pltpu.SemaphoreType.DMA((8,)),
            pltpu.SemaphoreType.DMA((8,)),
            *ring_scratch(14),
        ],
        compiler_params=pltpu.CompilerParams(
            collective_id=0, has_side_effects=True, vmem_limit_bytes=63 * 2**20
        ),
    )(slopes, n2, cot, branch, n1, lse, vec, up_sums, gain, act, gh, att, q, k, v, wout, woth, wqkv, tokens, grad)


def on_device(
    tokens,
    gain_one,
    shift_one,
    qkv_weight,
    qv_bias,
    out_weight,
    out_bias,
    gain_two,
    shift_two,
    up_weight,
    up_bias,
    down_weight,
    down_bias,
    cotangent,
):
    dp, tensor = lax.axis_index("dp"), lax.axis_index("tensor")
    core, x, y = dp % 2, (dp // 2) % 4, (dp // 8) % 4
    ring = jnp.where(core == 0, x, y)
    ring_other = jnp.where(core == 0, y, x)
    offsets = (0, 3, 1, 2)
    other_ids = [4 * core + (ring + o) % 4 for o in offsets]
    other_ids += [4 * (1 - core) + (ring_other + o) % 4 for o in offsets]

    own_heads = tensor * 8 + jnp.arange(8, dtype=jnp.int32)
    oth_heads = (1 - tensor) * 8 + jnp.stack(other_ids).astype(jnp.int32)
    slopes = jnp.exp2(-8.0 * (jnp.concatenate([own_heads, oth_heads]) + 1).astype(f32) / 16)
    rows = jnp.concatenate([gain_one, shift_one, gain_two, shift_two]).reshape(4, 1024)
    low_rows = jnp.concatenate(
        [out_bias, down_bias, up_bias, qv_bias[0], qv_bias[1], jnp.zeros((3072,), bf16)]
    ).reshape(8, 1024)
    wqkv = qkv_weight.transpose(1, 0, 2)
    (
        normed_one,
        queries,
        key_rows,
        values,
        attended,
        lse,
        woth,
        _,
        normed_two,
        active_own,
        gh_own,
        grad_up_bias,
        block_out,
        grad_middle,
        grad_branch,
        sums_two,
    ) = forward(
        slopes,
        tokens,
        rows,
        low_rows,
        wqkv,
        out_weight,
        up_weight,
        down_weight,
        cotangent,
    )
    share_down, share_up, share_out, share_qkv, vector, late, summed, token_grad = backward(
        slopes,
        normed_two,
        cotangent,
        grad_branch,
        normed_one,
        lse,
        sums_two,
        grad_up_bias,
        rows,
        active_own,
        gh_own,
        attended,
        queries,
        key_rows,
        values,
        out_weight,
        woth,
        wqkv,
        tokens,
        grad_middle,
    )
    return (
        block_out,
        token_grad,
        late[:, 8],
        late[:, 9],
        share_qkv.transpose(1, 0, 2),
        summed[4].reshape(2, 512),
        share_out.T,
        vector[:, 2],
        vector[:, 0],
        vector[:, 1],
        share_up,
        summed[2:4].reshape(2048),
        share_down.T,
        vector[:, 3],
    )


def solution(mesh):
    placed = (
        P("dp", None),
        P(),
        P(),
        P(None, None, "tensor"),
        P(None, "tensor"),
        P("tensor", None),
        P(),
        P(),
        P(),
        P(None, "tensor"),
        P("tensor"),
        P("tensor", None),
        P(),
        P("dp", None),
    )
    return jax.shard_map(
        on_device,
        mesh=mesh,
        in_specs=placed,
        out_specs=(
            P("dp", None),
            P("dp", None),
            P("dp"),
            P("dp"),
            P("dp", None, "tensor"),
            P(None, "tensor"),
            P("tensor", "dp"),
            P("dp"),
            P("dp"),
            P("dp"),
            P("dp", "tensor"),
            P("tensor"),
            P("tensor", "dp"),
            P("dp"),
        ),
        check_vma=False,
    )
```

```python
import functools
import math

import jax
import jax.numpy as jnp
from jax import lax
from jax.experimental import pallas as pl
from jax.experimental.pallas import tpu as pltpu
from jax.sharding import PartitionSpec as P

DH = 64
epsilon = 1e-05
bf16 = jnp.bfloat16
f32 = jnp.float32


def layer_norm_parts(values):
    centre = jnp.mean(values, axis=-1, keepdims=True)
    centered = values - centre
    spread = jnp.mean(centered * centered, axis=-1, keepdims=True)
    r = lax.rsqrt(spread + epsilon)
    return centered * r, r


def layer_norm_back(grad, n, r, gain):
    e = grad * gain
    mean_e = jnp.mean(e, axis=-1, keepdims=True)
    mean_en = jnp.mean(e * n, axis=-1, keepdims=True)
    return (
        r * (e - mean_e - n * mean_en),
        jnp.sum(grad * n, axis=0),
        jnp.sum(grad, axis=0),
    )


GC, GA = 0.7978845608028654, 0.044715


def gelu_both(v):
    square = v * v
    h = 0.5 + 0.5 * jnp.tanh(v * (GC + GC * GA * square))
    value = v * h
    slope = h + (value * (1.0 - h)) * (2.0 * GC + 6.0 * GC * GA * square)
    return value, slope


NT = (((1,), (1,)), ((), ()))
TN = (((0,), (0,)), ((), ()))
NN = (((1,), (0,)), ((), ()))


def dot(a, b, dims=NN):
    return lax.dot_general(a, b, dims, preferred_element_type=f32)


def half_lanes(block, side):
    lane = lax.broadcasted_iota(jnp.int32, block.shape, 1)
    return jnp.where((lane >= 64) == (side == 1), block, jnp.zeros_like(block))


def fill_distance(ref):
    row = lax.broadcasted_iota(jnp.int32, ref.shape, 0)
    col = lax.broadcasted_iota(jnp.int32, ref.shape, 1)
    ref[...] = jnp.where(row >= col, (row - col).astype(f32), 1e30)


def attend_pair(q, k, v, slopes, distance):
    outs, lses = [], []
    scaled = q * 0.125
    for side in range(2):
        out, lse = [], []
        for rows, keys in ((slice(0, 256), 256), (slice(256, 512), 512)):
            s = dot(half_lanes(scaled[rows], side), k[:keys], NT) - slopes[side] * distance[rows, :keys]
            top = jnp.max(s, axis=-1, keepdims=True)
            e = jnp.exp(s - top)
            total = jnp.sum(e, axis=-1, keepdims=True)
            out.append(dot((e * (1.0 / total)).astype(bf16), v[:keys]))
            lse.append(top + jnp.log(total))
        outs.append(jnp.concatenate(out, axis=0))
        lses.append(jnp.concatenate(lse, axis=0))
    lane = lax.broadcasted_iota(jnp.int32, outs[0].shape, 1)
    return jnp.where(lane < 64, outs[0], outs[1]).astype(bf16), lses


def attend_back_pair(q, k, v, lse, g, slopes, distance):
    dqs, dks, dvs = [], [], []
    scaled = q * 0.125
    for side in range(2):
        dq, dk, dv = [], [], []
        for rows, keys in ((slice(0, 256), 256), (slice(256, 512), 512)):
            s = dot(half_lanes(scaled[rows], side), k[:keys], NT) - slopes[side] * distance[rows, :keys]
            a = jnp.exp(s - lse[side][rows])
            w = dot(half_lanes(g[rows], side), v[:keys], NT)
            inner = jnp.sum(a * w, axis=-1, keepdims=True)
            ds = (a * (w - inner)).astype(bf16)
            dv.append(dot(a.astype(bf16), g[rows], TN))
            dq.append(dot(ds, k[:keys]) * 0.125)
            dk.append(dot(ds, q[rows], TN) * 0.125)
        dqs.append(jnp.concatenate(dq, axis=0))
        for parts, total in ((dk, dks), (dv, dvs)):
            total.append(jnp.concatenate([parts[0] + parts[1][:256], parts[1][256:]], axis=0))
    lane = lax.broadcasted_iota(jnp.int32, dqs[0].shape, 1)
    return [jnp.where(lane < 64, p[0], p[1]).astype(bf16) for p in (dqs, dks, dvs)]


def unit_block(n2, cot, up, up_dims, bias, down):
    value, slope = gelu_both(dot(n2, up, up_dims) + bias)
    active = value.astype(bf16)
    gh = (dot(cot, down, NT) * slope).astype(bf16)
    back_dims = NT if up_dims is NN else NN
    return active, gh, dot(active, down), dot(gh, up, back_dims)


MESH = pl.DeviceIdType.MESH


def forward_kernel(
    slopes,
    tokens,
    rows_ref,
    low_rows,
    wqkv,
    wout,
    up_any,
    down_any,
    cot_any,
    n1_out,
    q_out,
    k_out,
    v_out,
    att_out,
    lse_ref,
    woth_out,
    units_any,
    n2_out,
    act_out,
    gh_out,
    gb_ref,
    out_ref,
    grad_ref,
    branch_ref,
    vec_ref,
    n1_ref,
    q_ref,
    k_ref,
    v_ref,
    att_ref,
    woth_ref,
    n2_ref,
    act_ref,
    gh_ref,
    bias_rows,
    bias_piece,
    piece,
    turned,
    distance,
    got,
    got_bias,
    bias_out,
    up,
    down,
    cot,
    feed_ref,
    gn_ref,
    hsend,
    hrecv,
    usend,
    urecv,
    bsend,
    brecv,
    lsem,
    fsem,
    osem,
):
    dp, tensor = lax.axis_index("dp"), lax.axis_index("tensor")
    core, x, y, zh = dp % 2, (dp // 2) % 4, (dp // 8) % 4, dp // 32
    z = zh * 2 + tensor
    ring = jnp.where(core == 0, x, y)

    def device(nx, ny, nz, nc):
        return ((((nz // 2) * 4 + ny) * 4 + nx) * 2 + nc, nz % 2)

    def on_ring(r):
        return device(jnp.where(core == 0, r, x), jnp.where(core == 0, y, r), z, core)

    z_plus, z_minus = device(x, y, (z + 1) % 4, core), device(x, y, (z + 3) % 4, core)
    r_plus, r_minus = on_ring((ring + 1) % 4), on_ring((ring + 3) % 4)
    partner = device(x, y, z, 1 - core)
    barrier = pltpu.get_barrier_semaphore()
    for d in (z_plus, z_minus, r_plus, r_minus, partner):
        pl.semaphore_signal(barrier, inc=1, device_id=d, device_id_type=MESH)
    local = [
        pltpu.make_async_copy(a, b, lsem.at[k])
        for k, (a, b) in enumerate(((up_any, up), (down_any, down), (cot_any, cot)))
    ]
    for c in local:
        c.start()
    pid, fid = 4 * core + ring, 4 * core + (ring + 2) % 4
    for m in range(3):
        turned[...] = wqkv[m, :, pl.ds(pl.multiple_of(pid // 2 * 128, 128), 128)].T
        side = pl.ds(pl.multiple_of(pid % 2 * 64, 64), 64)
        piece[0, m * 64 : m * 64 + 64, :] = turned[side, :].astype(f32)
    piece[0, 192:256, :] = wout[pl.ds(pl.multiple_of(pid * 64, 64), 64), :].astype(f32)
    bias_rows[...] = low_rows[...].astype(f32)
    for p in range(8):
        q_part = bias_rows[4:5, 64 * p : 64 * p + 64]
        v_part = bias_rows[4:5, 512 + 64 * p : 576 + 64 * p]
        bias_piece[p : p + 1, :] = jnp.concatenate([q_part, q_part, v_part, v_part], axis=1)
        bias_piece[8 + p : 9 + p, :] = bias_rows[2 + p // 4 : 3 + p // 4, p % 4 * 256 : p % 4 * 256 + 256]
    pl.semaphore_wait(barrier, 5)

    def place(u, slot, sub):
        at = pl.ds(sub * 64, 64)
        return got.at[slot, at] if u == 0 else units_any.at[u - 1, slot, at]

    def move(u, src, slot, sub, way, target):
        send = hsend.at[slot, sub, way] if u == 0 else usend.at[u - 1, slot, sub, way]
        recv = hrecv.at[slot, sub] if u == 0 else urecv.at[u - 1, slot, sub]
        return pltpu.make_async_remote_copy(
            src_ref=src,
            dst_ref=place(u, slot, sub),
            send_sem=send,
            recv_sem=recv,
            device_id=target,
            device_id_type=MESH,
        )

    started = [[], [], []]

    def begin(u, src, slot, sub, target):
        c = move(u, src, slot, sub, 0, target)
        c.start()
        started[u].append(c)

    def arrived(u, slot, sub):
        move(u, place(u, slot, sub), slot, sub, 0, partner).wait_recv()

    bias_move = pltpu.make_async_remote_copy(
        src_ref=bias_piece, dst_ref=got_bias, send_sem=bsend, recv_sem=brecv, device_id=z_plus, device_id_type=MESH
    )
    outgoing = []

    def leave(k, src, dst):
        c = pltpu.make_async_copy(src, dst, osem.at[k])
        c.start()
        outgoing.append(c)

    def to_z(u, src, slot):
        for sub in (0, 2, 1, 3):
            begin(u, piece.at[src, pl.ds(sub * 64, 64)], slot, sub, z_plus if sub < 2 else z_minus)

    to_z(0, 0, 0)
    bias_move.start()
    fill_distance(distance)

    def own_came(u, subs):
        for sub in subs:
            arrived(u, 0, sub)
            begin(u, place(u, 0, sub), 1, sub, r_plus)
            begin(u, place(u, 0, sub), 2, sub, r_minus)
        for sub in subs:
            begin(u, place(u, 0, sub), 4, sub, partner)

    def next_came(u, low, high):
        arrived(u, 1, low)
        if low < 2 and u < 2:
            begin(u, place(u, 1, low), 3, low, r_plus)
        begin(u, place(u, 1, low), 5, low, partner)
        arrived(u, 2, high)
        if high >= 2 and u < 2:
            begin(u, place(u, 2, high), 3, high, r_minus)
        begin(u, place(u, 2, high), 6, high, partner)

    def far_came(u, subs):
        for sub in subs:
            arrived(u, 3, sub)
            begin(u, place(u, 3, sub), 7, sub, partner)

    def swapped(u, slots):
        for slot in slots:
            for sub in range(4):
                arrived(u, slot, sub)

    pump = [lambda u=u, f=f: f(u) for u in range(3) for f in (
        lambda u: own_came(u, (0, 2)),
        lambda u: own_came(u, (1, 3)),
        lambda u: next_came(u, 0, 2),
        lambda u: next_came(u, 2, 0),
        lambda u: next_came(u, 1, 3),
        lambda u: next_came(u, 3, 1),
        lambda u: far_came(u, (0, 2)),
        lambda u: far_came(u, (1, 3)),
        lambda u: swapped(u, range(4, 8) if u < 2 else (4, 5, 6)),
    )]

    def norm_one(r, carry):
        at = pl.ds(r * 128, 128)
        n, _ = layer_norm_parts(tokens[at, :].astype(f32))
        n1_ref[at, :] = (n * rows_ref[0:1, :] + rows_ref[1:2, :]).astype(bf16)
        return carry

    lax.fori_loop(0, 4, norm_one, 0)
    n1 = n1_ref[...]
    q_ref[0] = (dot(n1, wqkv[0]) + bias_rows[4:5, :512]).astype(bf16)
    k_ref[0] = dot(n1, wqkv[1]).astype(bf16)
    v_ref[0] = (dot(n1, wqkv[2]) + bias_rows[4:5, 512:]).astype(bf16)
    leave(0, n1_ref, n1_out)
    for c in local:
        c.wait()
    piece[1] = up[:, pl.ds(pl.multiple_of(pid * 256, 256), 256)].T.astype(f32)
    piece[2] = down[pl.ds(pl.multiple_of(pid * 256, 256), 256), :].astype(f32)
    piece[3] = down[pl.ds(pl.multiple_of(fid * 256, 256), 256), :].astype(f32)
    to_z(1, 1, 0)
    to_z(2, 2, 0)
    to_z(2, 3, 3)

    lse_ref[...] = jnp.zeros_like(lse_ref)

    def put_lse(head, pair):
        lane = lax.broadcasted_iota(jnp.int32, lse_ref.shape, 1)
        for side in range(2):
            lse_ref[...] = jnp.where(lane == head + side, pair[side], lse_ref[...])

    def own_pair(p, carry):
        lanes = pl.ds(pl.multiple_of(p * 128, 128), 128)
        out, lse = attend_pair(
            q_ref[0, :, lanes], k_ref[0, :, lanes], v_ref[0, :, lanes], (slopes[2 * p], slopes[2 * p + 1]), distance
        )
        att_ref[0, :, lanes] = out
        put_lse(2 * p, lse)
        return carry

    lax.fori_loop(0, 1, own_pair, 0)
    pump[0]()
    lax.fori_loop(1, 4, own_pair, 0)
    pump[1]()
    pump[2]()
    feed_ref[...] = dot(att_ref[0], wout[...])
    for k in range(3, 6):
        pump[k]()
    bias_move.wait()
    ring_other = jnp.where(core == 0, y, x)
    for k, o in enumerate((0, 3, 1, 2)):
        for slot, pid in ((k, 4 * core + (ring + o) % 4), (k + 4, 4 * (1 - core) + (ring_other + o) % 4)):
            bias_out[slot : slot + 1, :] = got_bias[pl.ds(pid, 1), :]
            bias_out[8 + slot : 9 + slot, :] = got_bias[pl.ds(8 + pid, 1), :]

    def other_pair(p, carry):
        lanes = pl.ds(pl.multiple_of(p * 128, 128), 128)
        for m in range(4):
            for side in range(2):
                at = pl.ds(pl.multiple_of(p * 128 + side * 64, 64), 64)
                woth_ref[m, at, :] = got[2 * p + side, m * 64 : m * 64 + 64, :].astype(bf16)
        low, high = bias_out[pl.ds(2 * p, 1), :], bias_out[pl.ds(2 * p + 1, 1), :]
        parts = []
        for m in range(3):
            parts.append(dot(n1_ref[...], woth_ref[m, lanes, :], NT))
        lane = lax.broadcasted_iota(jnp.int32, (1, 128), 1)
        q = (parts[0] + jnp.where(lane < 64, low[:, :128], high[:, :128])).astype(bf16)
        k = parts[1].astype(bf16)
        v = (parts[2] + jnp.where(lane < 64, low[:, 128:], high[:, 128:])).astype(bf16)
        q_ref[1, :, lanes] = q
        k_ref[1, :, lanes] = k
        v_ref[1, :, lanes] = v
        out, lse = attend_pair(q, k, v, (slopes[8 + 2 * p], slopes[9 + 2 * p]), distance)
        att_ref[1, :, lanes] = out
        put_lse(8 + 2 * p, lse)
        return carry

    lax.fori_loop(0, 1, other_pair, 0)
    for k in (9, 6, 7, 8, 10):
        pump[k]()
    lax.fori_loop(1, 4, other_pair, 0)
    pump[11]()
    feed_ref[...] += dot(att_ref[1], woth_ref[3])
    pump[12]()

    def norm_two(r, carry):
        at = pl.ds(r * 128, 128)
        middle = tokens[at, :].astype(f32) + (feed_ref[at, :] + bias_rows[0:1, :])
        grad_ref[at, :] = middle
        n, _ = layer_norm_parts(middle)
        n2_ref[at, :] = (n * rows_ref[2:3, :] + rows_ref[3:4, :]).astype(bf16)
        return carry

    lax.fori_loop(0, 4, norm_two, 0)
    leave(1, q_ref, q_out)
    leave(2, k_ref, k_out)
    leave(3, v_ref, v_out)
    leave(4, att_ref, att_out)
    leave(5, woth_ref, woth_out)
    leave(6, n2_ref, n2_out)
    pump[13]()
    pump[14]()
    feed_ref[...] = jnp.zeros_like(feed_ref)
    gn_ref[...] = jnp.zeros_like(gn_ref)

    def unit_step(i, carry):
        lanes = pl.ds(pl.multiple_of(i * 512, 512), 512)
        within = pl.ds(pl.multiple_of(i % 2 * 512, 512), 512)
        where = (pl.ds(2 + i // 2, 1), within)
        active, gh, feed, gn = unit_block(
            n2_ref[...], cot[...], up[:, lanes], NN, bias_rows[where], down[lanes, :]
        )
        act_ref[:, lanes] = active
        gh_ref[:, lanes] = gh
        gb_ref[pl.ds(i // 2, 1), within] = jnp.sum(gh.astype(f32), axis=0, keepdims=True)
        feed_ref[...] += feed
        gn_ref[...] += gn
        return carry

    def fetch(number, slots):
        return [
            pltpu.make_async_copy(
                units_any.at[k, slot], got.at[4 * number + 2 * k + n], fsem.at[number, 2 * k + n]
            )
            for k in range(2)
            for n, slot in enumerate(slots)
        ]

    def other_step(number, slots):
        for c in fetch(number, slots):
            c.wait()
        up_two, down_two = (
            jnp.concatenate([got[4 * number + 2 * k].astype(bf16), got[4 * number + 2 * k + 1].astype(bf16)], axis=0)
            for k in range(2)
        )
        bias = jnp.concatenate([bias_out[8 + slot : 9 + slot, :] for slot in slots], axis=1)
        _, _, feed, gn = unit_block(n2_ref[...], cot[...], up_two, NT, bias, down_two)
        feed_ref[...] += feed
        gn_ref[...] += gn

    def bring(number, slots):
        for c in fetch(number, slots):
            c.start()

    lax.fori_loop(0, 1, unit_step, 0)
    for k in (18, 15, 16):
        pump[k]()
    lax.fori_loop(1, 2, unit_step, 0)
    for k in (19, 17):
        pump[k]()
    lax.fori_loop(2, 3, unit_step, 0)
    pump[20]()
    pump[21]()
    lax.fori_loop(3, 4, unit_step, 0)
    leave(7, act_ref, act_out)
    leave(8, gh_ref, gh_out)
    for c in started[0]:
        c.wait_send()
    swapped(2, (4,))
    bring(0, (0, 4))
    pump[22]()
    pump[24]()
    pump[25]()
    swapped(2, (7,))
    bring(1, (3, 7))
    other_step(0, (0, 4))
    pump[23]()
    bring(0, (1, 2))
    other_step(1, (3, 7))
    swapped(2, (5, 6))
    bring(1, (5, 6))
    other_step(0, (1, 2))
    other_step(1, (5, 6))
    vec_ref[...] = jnp.zeros_like(vec_ref)

    def rows_of(r, carry):
        at = pl.ds(pl.multiple_of(r * 64, 64), 64)
        middle = grad_ref[at, :]
        cotangent = cot[at, :].astype(f32)
        out_ref[at, :] = (middle + (feed_ref[at, :] + bias_rows[1:2, :])).astype(bf16)
        n, root = layer_norm_parts(middle)
        back, ggain, gshift = layer_norm_back(gn_ref[at, :], n, root, rows_ref[2:3, :])
        whole = cotangent + back
        rounded = whole.astype(bf16)
        grad_ref[at, :] = whole
        branch_ref[at, :] = rounded
        vec_ref[0:1, :] += ggain[None]
        vec_ref[1:2, :] += gshift[None]
        vec_ref[2:3, :] += jnp.sum(rounded.astype(f32), axis=0, keepdims=True)
        vec_ref[3:4, :] += jnp.sum(cotangent, axis=0, keepdims=True)
        return carry

    lax.fori_loop(0, 8, rows_of, 0)
    for c in started[1] + started[2]:
        c.wait_send()
    for c in outgoing:
        c.wait()


def forward(slopes, tokens, rows, low_rows, wqkv, wout, up, down, cot):
    length, width = tokens.shape
    local, units = wout.shape[0], up.shape[1]
    vmem = pl.BlockSpec(memory_space=pltpu.VMEM)
    hbm = pl.BlockSpec(memory_space=pl.ANY)

    def out(shape, kind):
        return jax.ShapeDtypeStruct(shape, kind)

    return pl.pallas_call(
        forward_kernel,
        in_specs=[pl.BlockSpec(memory_space=pltpu.SMEM)] + [vmem] * 5 + [hbm] * 3,
        out_specs=[hbm] * 5 + [vmem] + [hbm] * 5 + [vmem] * 5,
        out_shape=[
            out((length, width), bf16),
            out((2, length, local), bf16),
            out((2, length, local), bf16),
            out((2, length, local), bf16),
            out((2, length, local), bf16),
            out((length, 128), f32),
            out((4, local, width), bf16),
            out((2, 8, 256, width), f32),
            out((length, width), bf16),
            out((length, units), bf16),
            out((length, units), bf16),
            out((2, width), f32),
            out((length, width), bf16),
            out((length, width), f32),
            out((length, width), bf16),
            out((8, width), f32),
        ],
        scratch_shapes=[
            pltpu.VMEM((length, width), bf16),
            *[pltpu.VMEM((2, length, local), bf16)] * 4,
            pltpu.VMEM((4, local, width), bf16),
            pltpu.VMEM((length, width), bf16),
            pltpu.VMEM((length, units), bf16),
            pltpu.VMEM((length, units), bf16),
            pltpu.VMEM((8, width), f32),
            pltpu.VMEM((16, 256), f32),
            pltpu.VMEM((4, 256, width), f32),
            pltpu.VMEM((128, width), bf16),
            pltpu.VMEM((length, length), f32),
            pltpu.VMEM((8, 256, width), f32),
            pltpu.VMEM((16, 256), f32),
            pltpu.VMEM((16, 256), f32),
            pltpu.VMEM((width, units), bf16),
            pltpu.VMEM((units, width), bf16),
            pltpu.VMEM((length, width), bf16),
            pltpu.VMEM((length, width), f32),
            pltpu.VMEM((length, width), f32),
            pltpu.SemaphoreType.DMA((8, 4, 1)),
            pltpu.SemaphoreType.DMA((8, 4)),
            pltpu.SemaphoreType.DMA((2, 8, 4, 1)),
            pltpu.SemaphoreType.DMA((2, 8, 4)),
            pltpu.SemaphoreType.DMA,
            pltpu.SemaphoreType.DMA,
            pltpu.SemaphoreType.DMA((3,)),
            pltpu.SemaphoreType.DMA((2, 4)),
            pltpu.SemaphoreType.DMA((9,)),
        ],
        compiler_params=pltpu.CompilerParams(
            collective_id=1, has_side_effects=True, vmem_limit_bytes=62 * 2**20
        ),
    )(slopes, tokens, rows, low_rows, wqkv, wout, up, down, cot)


W = 512
OFFSETS = (0, 1, 3, 5, 6, 7, 8)
SLOTS = 6


def ring_scratch(nb):
    return [
        pltpu.VMEM((2, 512, 512), bf16),
        pltpu.VMEM((SLOTS, 4, 128, W), f32),
        pltpu.VMEM((2, 4, 128, W), f32),
        pltpu.VMEM((SLOTS, 4, 128, W), f32),
        pltpu.VMEM((nb, 64, W), f32),
        pltpu.VMEM((nb, 64, W), f32),
        pltpu.VMEM((nb, 128, W), f32),
        pltpu.VMEM((nb, 128, W), f32),
        pltpu.VMEM((SLOTS, 4, 32, W), f32),
        pltpu.VMEM((nb, 16, W), f32),
        pltpu.VMEM((nb, 16, W), f32),
        pltpu.VMEM((nb, 32, W), f32),
        pltpu.VMEM((nb, 32, W), f32),
        pltpu.VMEM((SLOTS, 2, 16, W), f32),
        pltpu.VMEM((nb, 16, W), f32),
        pltpu.SemaphoreType.DMA((10, nb)),
        pltpu.SemaphoreType.DMA((10, nb)),
        pltpu.SemaphoreType.REGULAR,
    ]


class Ring:
    def __init__(self, blocks, narrow, scratch):
        self.blocks, self.narrow = blocks, narrow
        (
            self.lt, self.s, self.other, self.crecv, self.p1, self.m1, self.p2, self.m2, self.t,
            self.q1, self.r1, self.q2, self.r2, self.u, self.zrecv, self.ssem, self.rsem, self.credit,
        ) = scratch
        dp = lax.axis_index("dp")
        core = dp % 2
        x, y, zh = (dp // 2) % 4, (dp // 8) % 4, dp // 32
        self.core, self.zh = core, zh
        a = jnp.where(core == 0, x, y)
        b = jnp.where(core == 0, y, x)
        self.a, self.b = a, b

        def device(na, nb):
            nx = jnp.where(core == 0, na, nb)
            ny = jnp.where(core == 0, nb, na)
            return ((zh * 4 + ny) * 4 + nx) * 2 + core

        self.ap, self.am, self.a2 = (a + 1) % 4, (a + 3) % 4, (a + 2) % 4
        self.bp, self.bm, self.b2 = (b + 1) % 4, (b + 3) % 4, (b + 2) % 4
        self.to_ap, self.to_am = device(self.ap, b), device(self.am, b)
        self.to_bp, self.to_bm = device(a, self.bp), device(a, self.bm)
        self.to_a2, self.to_b2 = device(self.a2, b), device(a, self.b2)
        self.partner = dp + 1 - 2 * core
        self.across = dp + 32 - 64 * zh
        barrier = pltpu.get_barrier_semaphore()
        everyone = (
            self.partner, self.to_ap, self.to_am, self.to_bp, self.to_bm, self.to_a2, self.to_b2, self.across,
        )
        for d in everyone:
            pl.semaphore_signal(barrier, inc=1, device_id={"dp": d}, device_id_type=MESH)
        self.barrier = barrier

    def enter(self):
        pl.semaphore_wait(self.barrier, 8)

    def copies(self, stage, i, wide):
        def copy(kind, src, dst, d):
            if not wide:
                lanes = (slice(None),) * (len(src.shape) - 1) + (pl.ds(0, 128),)
                src, dst = src.at[lanes], dst.at[lanes]
            return pltpu.make_async_remote_copy(
                src_ref=src,
                dst_ref=dst,
                send_sem=self.ssem.at[kind, i],
                recv_sem=self.rsem.at[kind, i],
                device_id={"dp": d},
                device_id_type=MESH,
            )

        k = i % SLOTS
        if stage == 0:
            return [copy(0, self.other.at[i % 2], self.crecv.at[k], self.partner)]
        if stage == 1:
            return [
                copy(1, self.s.at[k, self.a2, pl.ds(0, 64)], self.p1.at[i], self.to_ap),
                copy(2, self.s.at[k, self.a2, pl.ds(64, 64)], self.m1.at[i], self.to_am),
            ]
        if stage == 2:
            return [
                copy(3, self.s.at[k, self.ap], self.p2.at[i], self.to_ap),
                copy(4, self.s.at[k, self.am], self.m2.at[i], self.to_am),
            ]
        if stage == 3:
            return [
                copy(5, self.t.at[k, self.b2, pl.ds(0, 16)], self.q1.at[i], self.to_bp),
                copy(6, self.t.at[k, self.b2, pl.ds(16, 16)], self.r1.at[i], self.to_bm),
            ]
        if stage == 4:
            return [
                copy(7, self.t.at[k, self.bp], self.q2.at[i], self.to_bp),
                copy(8, self.t.at[k, self.bm], self.r2.at[i], self.to_bm),
            ]
        return [copy(9, self.u.at[k, 1 - self.zh], self.zrecv.at[i], self.across)]

    def each(self, stage, i, act):
        few = functools.reduce(jnp.logical_or, [i == n for n in self.narrow])
        for wide in (True, False):
            @pl.when(few != wide)
            def _(wide=wide):
                for c in self.copies(stage, i, wide):
                    act(c)

    def start(self, stage, i):
        self.each(stage, i, lambda c: c.start())

    def wait(self, stage, i):
        self.each(stage, i, lambda c: c.wait())

    @staticmethod
    def slabs(part):
        for k in range(8):
            yx, c = k // 2, k % 2
            half, row = part // 4, part % 4
            first, second = (yx, row) if c == 0 else (row, yx)
            yield c, first, (second * 2 + half) * 16, k * 16

    def turn(self, left):
        for part in range(8):
            flipped = left[:, part * 128 : (part + 1) * 128].T
            for c, first, at, row in self.slabs(part):
                self.lt[c, first * 128 + at : first * 128 + at + 16, :] = flipped[row : row + 16, :]

    def make_product(self, i, right):
        own = dot(self.lt[self.core], right)
        away = dot(self.lt[1 - self.core], right)
        for chunk in range(4):
            self.s[i % SLOTS, chunk] = own[chunk * 128 : (chunk + 1) * 128]
            self.other[i % 2, chunk] = away[chunk * 128 : (chunk + 1) * 128]

    def make_small(self, i, small):
        k = i % SLOTS
        for part in range(8):
            flipped = small[:, part * 128 : (part + 1) * 128].T
            for c, first, at, row in self.slabs(part):
                @pl.when(self.core == c)
                def _(first=first, at=at, row=row, flipped=flipped):
                    self.s[k, first, at : at + 16, :128] = flipped[row : row + 16, :]

                @pl.when(self.core != c)
                def _(first=first, at=at, row=row, flipped=flipped):
                    self.other[i % 2, first, at : at + 16, :128] = flipped[row : row + 16, :]

    def sent(self, i):
        @pl.when(i >= SLOTS)
        def _():
            pl.semaphore_wait(self.credit, 1)

        self.start(0, i)

    def join_cores(self, i):
        self.wait(0, i)
        k = i % SLOTS
        for chunk in range(4):
            self.s[k, chunk] = self.s[k, chunk] + self.crecv[k, chunk]

        @pl.when(i + SLOTS < self.blocks)
        def _():
            pl.semaphore_signal(
                self.credit, inc=1, device_id={"dp": self.partner}, device_id_type=MESH
            )

        self.start(1, i)

    def first_ring(self, i):
        self.wait(1, i)
        s, k = self.s, i % SLOTS
        s[k, self.ap, :64] = s[k, self.ap, :64] + self.p1[i]
        s[k, self.am, 64:] = s[k, self.am, 64:] + self.m1[i]
        self.start(2, i)

    def first_done(self, i):
        self.wait(2, i)
        k = i % SLOTS
        for chunk in range(4):
            rows = pl.ds(chunk * 32, 32)
            self.t[k, chunk] = self.s[k, self.a, rows] + self.p2[i, rows] + self.m2[i, rows]
        self.start(3, i)

    def second_ring(self, i):
        self.wait(3, i)
        t, k = self.t, i % SLOTS
        t[k, self.bp, :16] = t[k, self.bp, :16] + self.q1[i]
        t[k, self.bm, 16:] = t[k, self.bm, 16:] + self.r1[i]
        self.start(4, i)

    def second_done(self, i):
        self.wait(4, i)
        k = i % SLOTS
        for chunk in range(2):
            rows = pl.ds(chunk * 16, 16)
            self.u[k, chunk] = self.t[k, self.b, rows] + self.q2[i, rows] + self.r2[i, rows]
        self.start(5, i)

    def share(self, i):
        self.wait(5, i)
        return self.u[i % SLOTS, self.zh] + self.zrecv[i]

    def run(self, make, finish, extra):
        def made(i):
            make(i)
            self.sent(i)

        stages = (
            made, self.join_cores, self.first_ring, self.first_done, self.second_ring, self.second_done,
            lambda i: finish(i, self.share(i)),
        )

        def step(j, carry):
            for stage, offset in zip(stages, OFFSETS):
                i = j - offset

                @pl.when((i >= 0) & (i < self.blocks))
                def _(stage=stage, i=i):
                    stage(i)

            extra(j)
            return carry

        lax.fori_loop(0, self.blocks + OFFSETS[-1], step, 0)


def cols_of(i, first):
    return pl.ds(pl.multiple_of((i - first) * W, W), W)


def at_step(cond):
    def wrap(f):
        pl.when(cond)(f)

    return wrap


def back_kernel(
    slopes, n2_ref, cot_ref, branch_ref, n1_ref, lse_ref, vec_two, up_sums, gain_ref,
    act_any, gh_any, att_any, q_any, k_any, v_any, wout_any, woth_any, wqkv_any, tokens_any, grad_any,
    down_out, up_out, out_out, qkv_out, vec_out, vec_late, sum_out, token_ref,
    distance, rbuf, q_v, k_v, v_v, wout, woth, wqkv, tokens, grad, ga, dq, dk, dv, small, every,
    rsems, lsem, gs, gr, *ring_refs,
):
    early = ((q_any, q_v), (k_any, k_v), (v_any, v_v), (wout_any, wout), (woth_any, woth))
    late = ((wqkv_any, wqkv), (tokens_any, tokens), (grad_any, grad))
    local = [
        pltpu.make_async_copy(src, dst, lsem.at[k]) for k, (src, dst) in enumerate(early + late)
    ]

    def right(kind, n):
        src = (act_any, gh_any)[kind]
        return pltpu.make_async_copy(src.at[:, cols_of(n, 4 * kind)], rbuf.at[n % 2], rsems.at[n % 2])

    right(0, 0).start()
    for c in local:
        c.start()
    att_copy = pltpu.make_async_copy(att_any.at[0], ga.at[0], rsems.at[2])
    ring = Ring(14, (4, 9), ring_refs)
    fill_distance(distance)
    ring.turn(cot_ref)
    ring.enter()
    core, a, b, zh = ring.core, ring.a, ring.b, ring.zh
    parts = (dq, dk, dv)

    def make(i):
        for first, left in ((5, n2_ref), (10, branch_ref), (11, n1_ref)):
            @pl.when(i == first)
            def _(left=left):
                ring.turn(left)

        for kind in range(2):
            first = 5 * kind

            @pl.when((i >= first) & (i < first + 4))
            def _(kind=kind):
                n = i - kind

                @pl.when(n < 3 + 4 * kind)
                def _():
                    right(kind, n + 1).start()

                if kind == 0:
                    @pl.when(n == 3)
                    def _():
                        right(1, n + 1).start()

                right(kind, n).wait()
                ring.make_product(i, rbuf[n % 2])

        @pl.when(i == 4)
        def _():
            small[...] = jnp.zeros_like(small)
            small[0:8, :] = vec_two[...]
            small[10:12, :] = up_sums[...]
            small[12:13, :512] = jnp.sum(dq[0].astype(f32), axis=0, keepdims=True)
            small[12:13, 512:] = jnp.sum(dv[0].astype(f32), axis=0, keepdims=True)

        @pl.when((i == 4) | (i == 9))
        def _():
            ring.make_small(i, small)

        @pl.when(i == 10)
        def _():
            att_copy.wait()
            ring.make_product(i, ga[0])

        for k in range(3):
            @pl.when(i == 11 + k)
            def _(k=k):
                ring.make_product(i, parts[k][0])

    def finish(i, share):
        for first, target in ((0, down_out), (5, up_out)):
            @pl.when((i >= first) & (i < first + 4))
            def _(first=first, target=target):
                target[:, cols_of(i, first)] = share

        @pl.when(i == 4)
        def _():
            vec_out[...] = share[:, :128]

        @pl.when(i == 9)
        def _():
            vec_late[...] = share[:, :128]

        @pl.when(i == 10)
        def _():
            out_out[...] = share

        @pl.when(i >= 11)
        def _():
            qkv_out[i - 11] = share

    def spread(number):
        mine = every.at[core]
        if number == 0:
            moves = [(0, mine.at[a, b, zh], ring.across)]
        elif number == 1:
            targets = (ring.to_bp, ring.to_bm, ring.to_b2)
            moves = [(k + 1, mine.at[a, b], d) for k, d in enumerate(targets)]
        elif number == 2:
            targets = (ring.to_ap, ring.to_am, ring.to_a2)
            moves = [(k + 4, mine.at[a], d) for k, d in enumerate(targets)]
        else:
            moves = [(7, mine, ring.partner)]
        return [
            pltpu.make_async_remote_copy(
                src_ref=place,
                dst_ref=place,
                send_sem=gs.at[k],
                recv_sem=gr.at[k],
                device_id={"dp": d},
                device_id_type=MESH,
            )
            for k, place, d in moves
        ]

    def spread_step(number):
        if number == 0:
            every[core, a, b, zh] = vec_out[...]
        else:
            for c in spread(number - 1):
                c.wait()
        if number < 4:
            for c in spread(number):
                c.start()
        else:
            for part in range(8):
                rows = [None] * 8
                for c, first, at, row in ring.slabs(part):
                    rows[row // 16] = every[c, first, at // 32, (at // 16) % 2]
                flipped = jnp.concatenate(rows, axis=0).T
                sum_out[:, part * 128 : (part + 1) * 128] = flipped[8:16]

    def extra(j):
        @pl.when(j == 0)
        def _():
            for c in local[:5]:
                c.wait()
            ga[0] = dot(branch_ref[...], wout[...], NT).astype(bf16)
            ga[1] = dot(branch_ref[...], woth[3], NT).astype(bf16)

        def one_pair(pair, carry):
            half, p = pair // 4, pair % 4
            lanes = pl.ds(pl.multiple_of(p * 128, 128), 128)
            lane = lax.broadcasted_iota(jnp.int32, lse_ref.shape, 1)
            lses = [
                jnp.sum(jnp.where(lane == 2 * pair + side, lse_ref[...], 0.0), axis=1, keepdims=True)
                for side in range(2)
            ]
            one, two, three = attend_back_pair(
                q_v[half, :, lanes],
                k_v[half, :, lanes],
                v_v[half, :, lanes],
                lses,
                ga[half, :, lanes],
                (slopes[2 * pair], slopes[2 * pair + 1]),
                distance,
            )
            dq[half, :, lanes] = one
            dk[half, :, lanes] = two
            dv[half, :, lanes] = three
            return carry

        @pl.when((j >= 1) & (j < 5))
        def _():
            lax.fori_loop(2 * j - 2, 2 * j, one_pair, 0)

        @pl.when(j == 4)
        def _():
            att_copy.start()

        for k in range(3):
            @pl.when(j == 5 + k)
            def _(k=k):
                if k == 0:
                    for c in local[5:]:
                        c.wait()
                one = dot(parts[k][0], wqkv[k], NT)
                two = dot(parts[k][1], woth[k])
                if k == 0:
                    token_ref[...] = one + two
                else:
                    token_ref[...] += one + two

        @pl.when(j == 8)
        def _():
            def rows_of(r, carry):
                rows = pl.ds(pl.multiple_of(r * 64, 64), 64)
                n, root = layer_norm_parts(tokens[rows, :].astype(f32))
                back, ggain, gshift = layer_norm_back(token_ref[rows, :], n, root, gain_ref[0:1, :])
                token_ref[rows, :] = grad[rows, :] + back
                small[8:9, :] += ggain[None]
                small[9:10, :] += gshift[None]
                return carry

            lax.fori_loop(0, 8, rows_of, 0)

        for number in range(5):
            @pl.when(j == 13 + number)
            def _(number=number):
                spread_step(number)

    ring.run(make, finish, extra)


def backward(slopes, n2, cot, branch, n1, lse, vec, up_sums, gain, act, gh, att, q, k, v, wout, woth, wqkv, tokens, grad):
    length, width = n1.shape
    vmem = pl.BlockSpec(memory_space=pltpu.VMEM)
    hbm = pl.BlockSpec(memory_space=pl.ANY)
    return pl.pallas_call(
        back_kernel,
        in_specs=[pl.BlockSpec(memory_space=pltpu.SMEM)] + [vmem] * 8 + [hbm] * 11,
        out_specs=[vmem] * 8,
        out_shape=[
            jax.ShapeDtypeStruct((16, 2048), f32),
            jax.ShapeDtypeStruct((16, 2048), f32),
            jax.ShapeDtypeStruct((16, 512), f32),
            jax.ShapeDtypeStruct((3, 16, 512), f32),
            jax.ShapeDtypeStruct((16, 128), f32),
            jax.ShapeDtypeStruct((16, 128), f32),
            jax.ShapeDtypeStruct((8, 1024), f32),
            jax.ShapeDtypeStruct((length, width), f32),
        ],
        scratch_shapes=[
            pltpu.VMEM((length, length), f32),
            pltpu.VMEM((2, length, W), bf16),
            pltpu.VMEM(q.shape, bf16),
            pltpu.VMEM(q.shape, bf16),
            pltpu.VMEM(q.shape, bf16),
            pltpu.VMEM(wout.shape, bf16),
            pltpu.VMEM(woth.shape, bf16),
            pltpu.VMEM(wqkv.shape, bf16),
            pltpu.VMEM(tokens.shape, bf16),
            pltpu.VMEM(grad.shape, f32),
            pltpu.VMEM(q.shape, bf16),
            pltpu.VMEM(q.shape, bf16),
            pltpu.VMEM(q.shape, bf16),
            pltpu.VMEM(q.shape, bf16),
            pltpu.VMEM((128, width), f32),
            pltpu.VMEM((2, 4, 4, 2, 16, 128), f32),
            pltpu.SemaphoreType.DMA((3,)),
            pltpu.SemaphoreType.DMA((8,)),
            pltpu.SemaphoreType.DMA((8,)),
            pltpu.SemaphoreType.DMA((8,)),
            *ring_scratch(14),
        ],
        compiler_params=pltpu.CompilerParams(
            collective_id=0, has_side_effects=True, vmem_limit_bytes=63 * 2**20
        ),
    )(slopes, n2, cot, branch, n1, lse, vec, up_sums, gain, act, gh, att, q, k, v, wout, woth, wqkv, tokens, grad)


def on_device(
    tokens,
    gain_one,
    shift_one,
    qkv_weight,
    qv_bias,
    out_weight,
    out_bias,
    gain_two,
    shift_two,
    up_weight,
    up_bias,
    down_weight,
    down_bias,
    cotangent,
):
    dp, tensor = lax.axis_index("dp"), lax.axis_index("tensor")
    core, x, y = dp % 2, (dp // 2) % 4, (dp // 8) % 4
    ring = jnp.where(core == 0, x, y)
    ring_other = jnp.where(core == 0, y, x)
    offsets = (0, 3, 1, 2)
    other_ids = [4 * core + (ring + o) % 4 for o in offsets]
    other_ids += [4 * (1 - core) + (ring_other + o) % 4 for o in offsets]

    own_heads = tensor * 8 + jnp.arange(8, dtype=jnp.int32)
    oth_heads = (1 - tensor) * 8 + jnp.stack(other_ids).astype(jnp.int32)
    slopes = jnp.exp2(-8.0 * (jnp.concatenate([own_heads, oth_heads]) + 1).astype(f32) / 16)
    rows = jnp.concatenate([gain_one, shift_one, gain_two, shift_two]).reshape(4, 1024)
    low_rows = jnp.concatenate(
        [out_bias, down_bias, up_bias, qv_bias[0], qv_bias[1], jnp.zeros((3072,), bf16)]
    ).reshape(8, 1024)
    wqkv = qkv_weight.transpose(1, 0, 2)
    (
        normed_one,
        queries,
        key_rows,
        values,
        attended,
        lse,
        woth,
        _,
        normed_two,
        active_own,
        gh_own,
        grad_up_bias,
        block_out,
        grad_middle,
        grad_branch,
        sums_two,
    ) = forward(
        slopes,
        tokens,
        rows,
        low_rows,
        wqkv,
        out_weight,
        up_weight,
        down_weight,
        cotangent,
    )
    share_down, share_up, share_out, share_qkv, vector, late, summed, token_grad = backward(
        slopes,
        normed_two,
        cotangent,
        grad_branch,
        normed_one,
        lse,
        sums_two,
        grad_up_bias,
        rows,
        active_own,
        gh_own,
        attended,
        queries,
        key_rows,
        values,
        out_weight,
        woth,
        wqkv,
        tokens,
        grad_middle,
    )
    return (
        block_out,
        token_grad,
        late[:, 8],
        late[:, 9],
        share_qkv.transpose(1, 0, 2),
        summed[4].reshape(2, 512),
        share_out.T,
        vector[:, 2],
        vector[:, 0],
        vector[:, 1],
        share_up,
        summed[2:4].reshape(2048),
        share_down.T,
        vector[:, 3],
    )


def solution(mesh):
    placed = (
        P("dp", None),
        P(),
        P(),
        P(None, None, "tensor"),
        P(None, "tensor"),
        P("tensor", None),
        P(),
        P(),
        P(),
        P(None, "tensor"),
        P("tensor"),
        P("tensor", None),
        P(),
        P("dp", None),
    )
    return jax.shard_map(
        on_device,
        mesh=mesh,
        in_specs=placed,
        out_specs=(
            P("dp", None),
            P("dp", None),
            P("dp"),
            P("dp"),
            P("dp", None, "tensor"),
            P(None, "tensor"),
            P("tensor", "dp"),
            P("dp"),
            P("dp"),
            P("dp"),
            P("dp", "tensor"),
            P("tensor"),
            P("tensor", "dp"),
            P("dp"),
        ),
        check_vma=False,
    )
```
